32 devices in a mesh: row: 8 (over z, x), col: 4 (over y, core).
Axes of the slice: x: 2, y: 2, z: 4, core: 2. Of those that a mesh axis runs over, the one named last changes fastest.
Arguments:
- qkv: bfloat16 [3, 1408, 16384], P(None, 'col', 'row'), may hold values from -12.1 to 12.1
- residual_in: bfloat16 [1408, 16384], P('col', 'row'), may hold values from -3 to 3
- out_weight: bfloat16 [1408, 1408], replicated, may hold values from -0.625 to 0.625
- merge_weight: bfloat16 [1408, 5632], P('col'), may hold values from -0.078125 to 0.078125
- merge_gain: float32 [1408], replicated, may hold values from 0.1 to 1.9
- image_groups: int32 [32], replicated, may hold values from 1 to 256, 4096 in all
- dest_row: int32 [4096], P('row'), may hold values from 0 to 4095, as said below
Outputs:
- layer_out: bfloat16 [1408, 16384], P('col', 'row')
- image_rows: bfloat16 [1408, 4096], P('col', 'row')
The draws below stay inside these ranges and needn't reach their ends.
Inputs may be any that keep to these rules, and one draw needn't show every extreme that they name: dest_row is a permutation of 0 to 4095. Of the 512 entries held by each index of row, exactly 64 fall in each aligned block of 512 output rows.
All inputs are finite; a program needn't handle non-finite values.
Results may differ from the reference program's by a relative error of at most 0.0064.
Values may be sent and summed in bfloat16 or wider, within the bound.
No kernel may reach another device: no remote copies, remote signals or barrier semaphores. Data moves between devices by JAX's collectives and lax.ppermute only.
A program may use at most 128 MiB of HBM per device.

```python
import math
import jax
import jax.numpy as jnp
import numpy as np
from jax import lax

D = 1408
HEADS = 16
HEAD_DIM = 88
TOK_DEV = 2048
TOKENS = 16384
GROUPS = 4096
IMAGES = 32
MOST_GROUPS = 256
N_ROW = 8


def draw_qkv(key, part):
    key_base = jax.random.fold_in(jax.random.fold_in(key, 11), 0)
    scales = jnp.array([1.2, 1.2, 1.0], jnp.float32)[:, None, None]
    base = jnp.clip(jax.random.normal(key_base, (3, D, TOKENS), jnp.float32), -8.0, 8.0) * scales
    return base.astype(jnp.bfloat16)


def draw_dest_row(key, part):
    group_rows = TOK_DEV // 4
    share_rows = group_rows // N_ROW
    key_source, key_owner = jax.random.split(jax.random.fold_in(key, 23))
    source_perm = jax.vmap(lambda sub_key: jax.random.permutation(sub_key, group_rows))(jax.random.split(key_source, N_ROW)).astype(jnp.int32)
    owner_perm = jax.vmap(lambda sub_key: jax.random.permutation(sub_key, group_rows))(jax.random.split(key_owner, N_ROW)).astype(jnp.int32)
    offsets = (jnp.arange(N_ROW, dtype=jnp.int32) * group_rows)[:, None]
    source_index = (source_perm + offsets).reshape(N_ROW, N_ROW, share_rows)
    target_index = (owner_perm + offsets).reshape(N_ROW, N_ROW, share_rows).transpose(1, 0, 2)
    result = jnp.zeros((N_ROW * group_rows,), jnp.int32)
    return result.at[source_index.reshape(-1)].set(target_index.reshape(-1))


def steps_of(key, extent, cuts, least, largest):
    gain = 1.0
    for axis_at, parts in cuts:
        heights = jax.random.uniform(jax.random.fold_in(jax.random.fold_in(key, 6), axis_at), (parts,), jnp.float32, least / len(cuts), largest / len(cuts))
        gain = gain * jnp.repeat(jnp.exp(heights), extent[axis_at] // parts).reshape((-1,) + (1,) * (len(extent) - 1 - axis_at))
    return gain


def length_profile(count, total, bound, lean):
    weights = [(1 << 20) // math.isqrt(rank ** lean) + 1 for rank in range(2, count + 1)]
    surplus, counts = total - bound - (count - 1), [1] * (count - 1)
    while surplus > 0:
        candidates = [i for i in range(count - 1) if counts[i] < bound]
        whole, left = sum([weights[i] for i in candidates]), surplus
        for i in candidates:
            extra = min(bound - counts[i], max(1, left * weights[i] // whole), surplus)
            counts[i] = counts[i] + extra
            surplus = surplus - extra
    return np.array([bound] + counts)


def uneven_parts(rng, number_of, total, reach, slope):
    if number_of == 2:
        one = jax.random.randint(rng, (), max(1, total - reach), min(reach, total - 1) + 1)
        return jnp.stack([one, total - one])
    lengths = jnp.asarray(length_profile(number_of, total, reach, slope), jnp.int32)
    couples = (number_of - 1) // 2
    giver, taker = lengths[1:1 + 2 * couples:2], lengths[2:2 + 2 * couples:2]
    room = jnp.minimum(giver - 1, reach - taker)
    moved = jax.random.randint(jax.random.fold_in(rng, 1), (couples,), 0, 1 << 20) % (room + 1)
    lengths = lengths.at[1:1 + 2 * couples:2].set(giver - moved).at[2:2 + 2 * couples:2].set(taker + moved)
    return lengths[jax.random.permutation(jax.random.fold_in(rng, 2), number_of)]


def centred(stream_key, extent, width, bound, pieces=(), held_as=jnp.bfloat16):
    entries = width * jax.random.normal(stream_key, extent, jnp.float32)
    if pieces:
        entries = entries * steps_of(stream_key, extent, pieces, -0.22, 0.18)
    return jnp.clip(entries, -bound, bound).astype(held_as)


def setup_inputs(seed: int = 0) -> dict:
    arg_keys = jax.random.split(jax.random.key(seed), 8)
    return {
        "qkv": draw_qkv(jax.random.fold_in(arg_keys[7], 71), 0),
        "residual_in": centred(arg_keys[1], (D, TOKENS), 0.5, 3.0, ((0, 4), (1, 8))),
        "out_weight": centred(arg_keys[2], (D, D), HEAD_DIM ** -0.5, 0.625),
        "merge_weight": centred(arg_keys[3], (D, 4 * D), (4 * D) ** -0.5, 0.078125, ((0, 4),)),
        "merge_gain": jnp.clip(1.0 + 0.18 * jax.random.normal(arg_keys[4], (D,), jnp.float32), 0.1, 1.9),
        "image_groups": uneven_parts(arg_keys[5], IMAGES, GROUPS, MOST_GROUPS, 2).astype(jnp.int32),
        "dest_row": draw_dest_row(jax.random.fold_in(arg_keys[7], 71), 0),
    }


def image_labels(positions, image_ends, all_tokens):
    inside = (positions >= 0) & (positions < all_tokens)
    counted = lax.optimization_barrier(jnp.sum((positions[:, None] >= image_ends[None, :]).astype(jnp.int32), axis=1)).astype(jnp.int32)
    return jnp.where(inside, counted, -1)

def reference(qkv, residual_in, out_weight, merge_weight, merge_gain, image_groups, dest_row):
    reach_rows = TOK_DEV // 2
    block_rows = min(512, TOK_DEV)
    window = block_rows + 2 * reach_rows
    score_scale = 1.0 / math.sqrt(HEAD_DIM)
    token_major = jnp.transpose(qkv, (0, 2, 1))
    image_ends = jnp.cumsum(image_groups).astype(jnp.int32) * 4
    positions = jnp.arange(TOKENS + 2 * reach_rows, dtype=jnp.int32) - reach_rows
    labels = image_labels(positions, image_ends, TOKENS)
    padded = jnp.pad(token_major[1:], ((0, 0), (reach_rows, reach_rows), (0, 0)))

    def attend(block_id):
        first_row = block_id * block_rows
        queries = lax.dynamic_slice_in_dim(token_major[0], first_row, block_rows, 0).astype(jnp.float32).reshape(block_rows, HEADS, HEAD_DIM)
        key_block = lax.dynamic_slice_in_dim(padded[0], first_row, window, 0).astype(jnp.float32).reshape(window, HEADS, HEAD_DIM)
        value_block = lax.dynamic_slice_in_dim(padded[1], first_row, window, 0).astype(jnp.float32).reshape(window, HEADS, HEAD_DIM)
        query_labels = lax.dynamic_slice_in_dim(labels, first_row + reach_rows, block_rows, 0)
        key_labels = lax.dynamic_slice_in_dim(labels, first_row, window, 0)
        scores = jnp.einsum('qhd,khd->hqk', queries, key_block) * score_scale
        same_image = (query_labels[:, None] == key_labels[None, :])[None]
        scores = jnp.where(same_image, scores, -1e+30)
        row_max = lax.optimization_barrier(jnp.max(scores, axis=2, keepdims=True))
        exponent = jnp.exp(scores - row_max)
        totals = lax.optimization_barrier(jnp.sum(exponent, axis=2))
        weights = exponent.astype(jnp.bfloat16).astype(jnp.float32)
        weighted = jnp.einsum('hqk,khd->qhd', weights, value_block)
        weighted = weighted / jnp.transpose(totals)[:, :, None]
        return weighted.astype(jnp.bfloat16).reshape(block_rows, D)
    attended = lax.map(attend, jnp.arange(TOKENS // block_rows, dtype=jnp.int32)).reshape(TOKENS, D)
    projected = jnp.dot(attended, out_weight, preferred_element_type=jnp.float32)
    layer_rows = (jnp.transpose(residual_in).astype(jnp.float32) + projected).astype(jnp.bfloat16)
    values32 = layer_rows.astype(jnp.float32)
    centre = lax.optimization_barrier(jnp.mean(values32, axis=1, keepdims=True))
    spread = lax.optimization_barrier(jnp.mean(jnp.square(values32 - centre), axis=1, keepdims=True))
    normed = ((values32 - centre) * lax.rsqrt(spread + 1e-06) * merge_gain.astype(jnp.float32)).astype(jnp.bfloat16)
    grouped = normed.reshape(GROUPS, 4 * D)
    merged = jnp.dot(grouped, jnp.transpose(merge_weight), preferred_element_type=jnp.float32).astype(jnp.bfloat16)
    image_rows = jnp.zeros((GROUPS, D), jnp.bfloat16).at[dest_row].set(merged)
    return (jnp.transpose(layer_rows), jnp.transpose(image_rows))
```

```python
import functools
import math

import jax
import jax.numpy as jnp
from jax import lax
from jax.experimental import pallas as pl
from jax.experimental.pallas import tpu as pltpu
from jax.sharding import PartitionSpec as P

HEAD_DIM = 88
TILE = 256
FAR = -1e30
BF = jnp.bfloat16
F32 = jnp.float32


def params(mib):
    return pltpu.CompilerParams(vmem_limit_bytes=mib * 1024 * 1024)


def cost(flops, bytes_accessed):
    return pl.CostEstimate(flops=int(flops), bytes_accessed=int(bytes_accessed), transcendentals=0)


def round_up(value, unit):
    return -(-value // unit) * unit


def key_tile(keys, label, images, depth, kt_ref):
    heads = keys.shape[0] // HEAD_DIM
    tail = depth - HEAD_DIM
    at = lax.broadcasted_iota(jnp.int32, (tail, TILE), 0)
    mask = jnp.where((at == label) | (at >= images), 0.0, FAR)
    for head in range(heads):
        whole = jnp.concatenate([keys[head * HEAD_DIM : (head + 1) * HEAD_DIM], mask], axis=0)
        kt_ref[0, head] = jnp.transpose(whole).astype(BF)


def value_tile(values, v_ref):
    heads = values.shape[0] // HEAD_DIM
    ones = jnp.where(lax.broadcasted_iota(jnp.int32, (8, TILE), 0) == 0, 1.0, 0.0)
    for head in range(heads):
        v_ref[0, head] = jnp.concatenate(
            [values[head * HEAD_DIM : (head + 1) * HEAD_DIM], ones], axis=0
        ).astype(BF)


def prepare_own(images, depth, label_ref, qkv_ref, q_ref, kt_ref, v_ref):
    label = label_ref[0]
    queries = qkv_ref[0].astype(F32)
    heads = queries.shape[0] // HEAD_DIM
    at = lax.broadcasted_iota(jnp.int32, (depth - HEAD_DIM, TILE), 0)
    mark = jnp.where(at == label, 1.0, 0.0)
    for head in range(heads):
        q_ref[0, head] = jnp.concatenate(
            [queries[head * HEAD_DIM : (head + 1) * HEAD_DIM], mark], axis=0
        ).astype(BF)
    key_tile(qkv_ref[1].astype(F32), label, images, depth, kt_ref)
    value_tile(qkv_ref[2].astype(F32), v_ref)


def prepare_halo(images, depth, label_l, label_r, left, right, kt_l, v_l, kt_r, v_r):
    key_tile(left[0].astype(F32), label_l[0], images, depth, kt_l)
    value_tile(left[1].astype(F32), v_l)
    key_tile(right[0].astype(F32), label_r[0], images, depth, kt_r)
    value_tile(right[1].astype(F32), v_r)


def reorder_residual(perm_ref, low_ref, high_ref, out_ref):
    both = jnp.concatenate([low_ref[...], high_ref[...]], axis=1)
    out_ref[0] = jnp.dot(both, perm_ref[...], preferred_element_type=F32).astype(BF)


def attend(pieces, base, rate, bounds, perm_ref, q_low, q_high, *refs):
    count = len({piece for piece, _ in pieces.values()})
    kt_refs, v_refs = refs[:count], refs[count : 2 * count]
    out_ref, kt_s, v_s, acc, top, att, kt_sem, v_sem = refs[2 * count :]
    heads = q_low.shape[1]
    first = jnp.minimum(bounds[0, 0], bounds[1, 0])
    last = jnp.maximum(bounds[0, 1], bounds[1, 1])

    def copies(tile):
        piece, at = pieces[tile]
        slot = tile - base
        return (
            pltpu.make_async_copy(kt_refs[piece].at[at], kt_s.at[slot], kt_sem.at[slot]),
            pltpu.make_async_copy(v_refs[piece].at[at], v_s.at[slot], v_sem.at[slot]),
        )

    for tile in sorted(pieces):

        @pl.when((tile >= first) & (tile < last))
        def _():
            for copy in copies(tile):
                copy.start()

    for tile in sorted(pieces):

        @pl.when((tile >= first) & (tile < last))
        def _():
            for copy in copies(tile):
                copy.wait()

    for side, q_ref in enumerate((q_low, q_high)):
        acc[...] = jnp.zeros_like(acc)
        top[...] = jnp.full_like(top, FAR)

        def step(tile, carry):
            slot = tile - base
            scores = [
                jnp.dot(kt_s[slot, head], q_ref[0, head], preferred_element_type=F32)
                for head in range(heads)
            ]
            for head in range(heads):
                before = top[head]
                now = jnp.maximum(before, jnp.max(scores[head], axis=0, keepdims=True))
                top[head] = now
                keep = jnp.exp2((before - now) * rate)
                weights = jnp.exp2((scores[head] - now) * rate).astype(BF)
                acc[head] = acc[head] * keep + jnp.dot(
                    v_s[slot, head], weights, preferred_element_type=F32
                )
            return carry

        lax.fori_loop(bounds[side, 0], bounds[side, 1], step, 0)
        whole = jnp.concatenate(
            [acc[head, :HEAD_DIM] / acc[head, HEAD_DIM : HEAD_DIM + 1] for head in range(heads)], axis=0
        )
        att[:, side * TILE : (side + 1) * TILE] = whole.astype(BF)
    out_ref[...] = jnp.dot(att[...], perm_ref[...], preferred_element_type=F32).astype(BF)


def project(order, col_ref, perm_ref, wt_ref, mw_ref, gain_ref, res_ref, *refs):
    count = len(order)
    att_refs = refs[:count]
    layer_ref, merged_ref, gathered, layer_s, normed = refs[count:]
    width = att_refs[0].shape[0]
    full = wt_ref.shape[0]
    col = col_ref[0]
    for bit, att_ref in zip(order, att_refs):
        row = pl.multiple_of((col ^ bit) * width, 16)
        gathered[pl.ds(row, width), :] = att_ref[...]
    for part in range(len(order)):
        rows = slice(part * width, (part + 1) * width)
        projected = jnp.dot(wt_ref[rows, :], gathered[...], preferred_element_type=F32)
        layer_s[rows, :] = (res_ref[part, 0].astype(F32) + projected).astype(BF)
    own = layer_s[pl.ds(pl.multiple_of(col * width, 16), width), :]
    layer_ref[...] = lax.dot_general(
        own, perm_ref[...], (((1,), (1,)), ((), ())), preferred_element_type=F32
    ).astype(BF)
    values = layer_s[...].astype(F32)
    centre = jnp.mean(values, axis=0, keepdims=True)
    spread = jnp.mean(jnp.square(values - centre), axis=0, keepdims=True)
    normed[...] = ((values - centre) * lax.rsqrt(spread + 1e-06) * gain_ref[...]).astype(BF)
    groups = normed.shape[1] // 4
    total = jnp.zeros((width, groups), F32)
    for j in range(4):
        total += jnp.dot(
            mw_ref[:, j * full : (j + 1) * full],
            normed[:, j * groups : (j + 1) * groups],
            preferred_element_type=F32,
        )
    merged_ref[...] = total.astype(BF)


def outgoing(slot_ref, place_ref, *refs):
    out_ref = refs[-1]
    total = None
    slots = out_ref.shape[0]
    for stage, merged_ref in enumerate(refs[:-1]):
        groups = merged_ref.shape[1]
        row = lax.broadcasted_iota(jnp.int32, (slots, groups), 0)
        pick = jnp.where(row == slot_ref[stage], 1.0, 0.0).astype(BF)
        rows = jnp.concatenate([merged_ref[...], place_ref[stage]], axis=0)
        term = lax.dot_general(pick, rows, (((1,), (1,)), ((), ())), preferred_element_type=F32)
        total = term if total is None else total + term
    out_ref[...] = total.astype(BF)


def incoming(width, base, in_ref, out_ref):
    place = in_ref[:, width : width + 2].astype(F32)
    target = (place[:, 0:1] * base + place[:, 1:2]).astype(jnp.int32)
    slots = in_ref.shape[0]
    lane = lax.broadcasted_iota(jnp.int32, (slots, slots), 1)
    pick = jnp.where(lane == target, 1.0, 0.0).astype(BF)
    out_ref[...] = lax.dot_general(
        in_ref[:, :width], pick, (((0,), (0,)), ((), ())), preferred_element_type=F32
    ).astype(BF)


def body(qkv, residual_in, out_weight, merge_weight, merge_gain, image_groups, dest_row):
    width = qkv.shape[1]
    tokens = qkv.shape[2]
    heads = width // HEAD_DIM
    full = out_weight.shape[0]
    images = image_groups.shape[0]
    reach = tokens // 2
    own_tiles = tokens // TILE
    far_tiles = reach // TILE
    stages = own_tiles // 2
    depth = round_up(HEAD_DIM + images, 128)
    rate = math.log2(math.e) / math.sqrt(HEAD_DIM)
    rows, cols = lax.axis_size("row"), lax.axis_size("col")
    row_id, col_id = lax.axis_index("row"), lax.axis_index("col")
    forward = [(i, i + 1) for i in range(rows - 1)]
    backward = [(i + 1, i) for i in range(rows - 1)]

    lefts, rights = [], []
    for stage in range(far_tiles):
        tail = lax.slice_in_dim(qkv[1:], tokens - (stage + 1) * TILE, tokens - stage * TILE, axis=2)
        head = lax.slice_in_dim(qkv[1:], stage * TILE, (stage + 1) * TILE, axis=2)
        lefts.append(lax.ppermute(tail, "row", forward))
        rights.append(lax.ppermute(head, "row", backward))

    image_ends = jnp.cumsum(image_groups) * 4
    window_tiles = own_tiles + 2 * far_tiles
    positions = row_id * tokens - reach + jnp.arange(window_tiles * TILE, dtype=jnp.int32)
    labels = jnp.sum((positions[:, None] >= image_ends[None, :]).astype(jnp.int32), axis=1)
    labels = jnp.where(positions >= 0, labels, -1).reshape(window_tiles, 1, TILE)
    starts = row_id * tokens + jnp.arange(own_tiles, dtype=jnp.int32) * TILE
    ends = starts + TILE - 1
    low = jnp.max(jnp.where(image_ends[None, :] <= starts[:, None], image_ends[None, :], 0), axis=1)
    high = jnp.min(
        jnp.where(image_ends[None, :] > ends[:, None], image_ends[None, :], rows * tokens), axis=1
    )
    window_start = row_id * tokens - reach
    low = (low - window_start) // TILE
    high = (high - window_start + TILE - 1) // TILE
    tile_at = jnp.arange(own_tiles, dtype=jnp.int32)
    low = jnp.maximum(low, tile_at)
    high = jnp.minimum(high, tile_at + 2 * far_tiles + 1)

    at = jnp.arange(2 * TILE, dtype=jnp.int32)
    perm = (((at % 4) * (TILE // 2) + at // 4)[:, None] == at[None, :]).astype(BF)

    residual = pl.pallas_call(
        reorder_residual,
        grid=(stages,),
        in_specs=[
            pl.BlockSpec((2 * TILE, 2 * TILE), lambda i: (0, 0)),
            pl.BlockSpec((width, TILE), lambda i: (0, stages - 1 - i)),
            pl.BlockSpec((width, TILE), lambda i: (0, stages + i)),
        ],
        out_specs=pl.BlockSpec((1, width, 2 * TILE), lambda i: (i, 0, 0)),
        out_shape=jax.ShapeDtypeStruct((stages, width, 2 * TILE), BF),
        compiler_params=params(32),
        cost_estimate=cost(2 * width * tokens * 2 * TILE, 4 * width * tokens),
        name="reorder_residual",
    )(perm, residual_in, residual_in)
    residual = lax.all_gather(residual, "col", axis=0)

    kt_shape, v_shape = (heads, TILE, depth), (heads, HEAD_DIM + 8, TILE)
    label_spec = lambda tile: pl.BlockSpec((1, 1, TILE), lambda i: (tile, 0, 0))
    q_tiles, kt_own, v_own = pl.pallas_call(
        functools.partial(prepare_own, images, depth),
        grid=(own_tiles,),
        in_specs=[
            pl.BlockSpec((1, 1, TILE), lambda i: (i + far_tiles, 0, 0)),
            pl.BlockSpec((3, width, TILE), lambda i: (0, 0, i)),
        ],
        out_specs=[
            pl.BlockSpec((1, heads, depth, TILE), lambda i: (i, 0, 0, 0)),
            pl.BlockSpec((1,) + kt_shape, lambda i: (i, 0, 0, 0)),
            pl.BlockSpec((1,) + v_shape, lambda i: (i, 0, 0, 0)),
        ],
        out_shape=[
            jax.ShapeDtypeStruct((own_tiles, heads, depth, TILE), BF),
            jax.ShapeDtypeStruct((own_tiles,) + kt_shape, BF),
            jax.ShapeDtypeStruct((own_tiles,) + v_shape, BF),
        ],
        compiler_params=params(32),
        cost_estimate=cost(2e9, 16 * width * tokens),
        name="prepare_own",
    )(labels, qkv)

    out_weight_t = jnp.transpose(out_weight)
    gain = merge_gain[:, None]
    bits = []
    span = cols // 2
    while span:
        bits.append(span)
        span //= 2
    order = [0]
    for bit in bits:
        order = order + [bit ^ other for other in order]
    col_value = col_id.astype(jnp.int32).reshape(1)

    halo = []
    layers, merged = [], []
    any_spec = pl.BlockSpec(memory_space=pl.ANY)
    smem_spec = pl.BlockSpec(memory_space=pltpu.SMEM)
    vmem_spec = pl.BlockSpec(memory_space=pltpu.VMEM)
    for stage in range(stages):
        left_tile, right_tile = far_tiles - 1 - stage, far_tiles + own_tiles + stage
        chunk_spec = pl.BlockSpec((2, width, TILE), lambda i: (0, 0, 0))
        new = pl.pallas_call(
            functools.partial(prepare_halo, images, depth),
            grid=(1,),
            in_specs=[label_spec(left_tile), label_spec(right_tile), chunk_spec, chunk_spec],
            out_specs=[
                pl.BlockSpec((1,) + kt_shape, lambda i: (0, 0, 0, 0)),
                pl.BlockSpec((1,) + v_shape, lambda i: (0, 0, 0, 0)),
            ]
            * 2,
            out_shape=[
                jax.ShapeDtypeStruct((1,) + kt_shape, BF),
                jax.ShapeDtypeStruct((1,) + v_shape, BF),
            ]
            * 2,
            compiler_params=params(32),
            cost_estimate=cost(5e8, 16 * width * TILE),
            name="prepare_halo",
        )(labels, labels, lefts[stage], rights[stage])
        halo.append(new)

        pieces = {far_tiles + t: (0, t) for t in range(own_tiles)}
        kts, vs = [kt_own], [v_own]
        for before in range(stage + 1):
            for tile, at_piece in (
                (far_tiles - 1 - before, 0),
                (far_tiles + own_tiles + before, 2),
            ):
                pieces[tile] = (len(kts), 0)
                kts.append(halo[before][at_piece])
                vs.append(halo[before][at_piece + 1])
        tiles = len(pieces)
        low_tile, high_tile = stages - 1 - stage, stages + stage
        bounds = jnp.stack(
            [
                jnp.stack([low[low_tile], high[low_tile]]),
                jnp.stack([low[high_tile], high[high_tile]]),
            ]
        )
        q_spec = lambda tile: pl.BlockSpec((1, heads, depth, TILE), lambda i: (tile, 0, 0, 0))
        attended = pl.pallas_call(
            functools.partial(attend, pieces, min(pieces), rate),
            grid=(1,),
            in_specs=[smem_spec, vmem_spec, q_spec(low_tile), q_spec(high_tile)]
            + [any_spec] * (2 * len(kts)),
            out_specs=vmem_spec,
            out_shape=jax.ShapeDtypeStruct((width, 2 * TILE), BF),
            scratch_shapes=[
                pltpu.VMEM((tiles,) + kt_shape, BF),
                pltpu.VMEM((tiles,) + v_shape, BF),
                pltpu.VMEM((heads, HEAD_DIM + 8, TILE), F32),
                pltpu.VMEM((heads, 1, TILE), F32),
                pltpu.VMEM((width, 2 * TILE), BF),
                pltpu.SemaphoreType.DMA((tiles,)),
                pltpu.SemaphoreType.DMA((tiles,)),
            ],
            compiler_params=params(48),
            cost_estimate=cost(4e9, 4e6),
            name="attend",
        )(bounds, perm, q_tiles, q_tiles, *kts, *vs)

        gathered = [attended]
        for bit in bits:
            pairs = [(i, i ^ bit) for i in range(cols)]
            gathered = gathered + [lax.ppermute(piece, "col", pairs) for piece in gathered]

        layer, part = pl.pallas_call(
            functools.partial(project, order),
            grid=(1,),
            in_specs=[
                smem_spec,
                vmem_spec,
                vmem_spec,
                vmem_spec,
                vmem_spec,
                pl.BlockSpec((cols, 1, width, 2 * TILE), functools.partial(lambda s, i: (0, s, 0, 0), stage)),
            ]
            + [vmem_spec] * cols,
            out_specs=[vmem_spec, vmem_spec],
            out_shape=[
                jax.ShapeDtypeStruct((width, 2 * TILE), BF),
                jax.ShapeDtypeStruct((width, TILE // 2), BF),
            ],
            scratch_shapes=[
                pltpu.VMEM((full, 2 * TILE), BF),
                pltpu.VMEM((full, 2 * TILE), BF),
                pltpu.VMEM((full, 2 * TILE), BF),
            ],
            compiler_params=params(48),
            cost_estimate=cost(2 * full * full * 2 * TILE + 2 * width * full * 2 * TILE, 10e6),
            name="project",
        )(col_value, perm, out_weight_t, merge_weight, gain, residual, *gathered)
        layers.append(layer)
        merged.append(part)

    layer_out = jnp.concatenate(
        [layers[s][:, :TILE] for s in reversed(range(stages))]
        + [layers[s][:, TILE:] for s in range(stages)],
        axis=1,
    )

    groups = tokens // 4
    share = groups // rows
    piece_groups = TILE // 4
    owner = dest_row // groups
    place = dest_row % groups
    index = jnp.arange(groups, dtype=jnp.int32)
    rank = jnp.sum(
        ((owner[:, None] == owner[None, :]) & (index[None, :] < index[:, None])).astype(jnp.int32),
        axis=1,
    )
    base = 32
    info = jnp.stack([owner * share + rank, place // base, place % base])
    info = info.reshape(3, own_tiles, piece_groups)
    info = jnp.stack(
        [
            jnp.concatenate([info[:, stages - 1 - s], info[:, stages + s]], axis=1)
            for s in range(stages)
        ],
        axis=1,
    )
    slots = info[0][:, None, :]
    wide = round_up(width + 2, 128)
    places = jnp.concatenate(
        [
            jnp.stack([info[1], info[2]], axis=1).astype(BF),
            jnp.zeros((stages, wide - width - 2, 2 * piece_groups), BF),
        ],
        axis=1,
    )
    sent = pl.pallas_call(
        outgoing,
        out_shape=jax.ShapeDtypeStruct((groups, wide), BF),
        compiler_params=params(32),
        cost_estimate=cost(2 * groups * groups * wide, 2e6),
        name="outgoing",
    )(slots, places, *merged)
    received = lax.all_to_all(
        sent.reshape(rows, share, wide), "row", split_axis=0, concat_axis=0, tiled=True
    ).reshape(groups, wide)
    image_rows = pl.pallas_call(
        functools.partial(incoming, width, base),
        out_shape=jax.ShapeDtypeStruct((width, groups), BF),
        compiler_params=params(32),
        cost_estimate=cost(2 * groups * groups * wide, 2e6),
        name="incoming",
    )(received)
    return (layer_out, image_rows)


def solution(mesh):
    return jax.shard_map(
        body,
        mesh=mesh,
        in_specs=(P(None, "col", "row"), P("col", "row"), P(), P("col", None), P(), P(), P("row")),
        out_specs=(P("col", "row"), P("col", "row")),
        check_vma=False,
    )
```

```python
import functools
import math

import jax
import jax.numpy as jnp
from jax import lax
from jax.experimental import pallas as pl
from jax.experimental.pallas import tpu as pltpu
from jax.sharding import PartitionSpec as P

HEAD_DIM = 88
TILE = 256
FAR = -1e30
BF = jnp.bfloat16
F32 = jnp.float32


def params(mib):
    return pltpu.CompilerParams(vmem_limit_bytes=mib * 1024 * 1024)


def cost(flops, bytes_accessed):
    return pl.CostEstimate(flops=int(flops), bytes_accessed=int(bytes_accessed), transcendentals=0)


def round_up(value, unit):
    return -(-value // unit) * unit


def key_tile(keys, label, images, depth, kt_ref):
    heads = keys.shape[0] // HEAD_DIM
    tail = depth - HEAD_DIM
    at = lax.broadcasted_iota(jnp.int32, (tail, TILE), 0)
    mask = jnp.where((at == label) | (at >= images), 0.0, FAR)
    for head in range(heads):
        whole = jnp.concatenate([keys[head * HEAD_DIM : (head + 1) * HEAD_DIM], mask], axis=0)
        kt_ref[0, head] = jnp.transpose(whole).astype(BF)


def value_tile(values, v_ref):
    heads = values.shape[0] // HEAD_DIM
    ones = jnp.where(lax.broadcasted_iota(jnp.int32, (8, TILE), 0) == 0, 1.0, 0.0)
    for head in range(heads):
        v_ref[0, head] = jnp.concatenate(
            [values[head * HEAD_DIM : (head + 1) * HEAD_DIM], ones], axis=0
        ).astype(BF)


def prepare_own(images, depth, label_ref, qkv_ref, q_ref, kt_ref, v_ref):
    label = label_ref[0]
    queries = qkv_ref[0].astype(F32)
    heads = queries.shape[0] // HEAD_DIM
    at = lax.broadcasted_iota(jnp.int32, (depth - HEAD_DIM, TILE), 0)
    mark = jnp.where(at == label, 1.0, 0.0)
    for head in range(heads):
        q_ref[0, head] = jnp.concatenate(
            [queries[head * HEAD_DIM : (head + 1) * HEAD_DIM], mark], axis=0
        ).astype(BF)
    key_tile(qkv_ref[1].astype(F32), label, images, depth, kt_ref)
    value_tile(qkv_ref[2].astype(F32), v_ref)


def prepare_halo(images, depth, label_l, label_r, left, right, kt_l, v_l, kt_r, v_r):
    key_tile(left[0].astype(F32), label_l[0], images, depth, kt_l)
    value_tile(left[1].astype(F32), v_l)
    key_tile(right[0].astype(F32), label_r[0], images, depth, kt_r)
    value_tile(right[1].astype(F32), v_r)


def reorder_residual(perm_ref, low_ref, high_ref, out_ref):
    both = jnp.concatenate([low_ref[...], high_ref[...]], axis=1)
    out_ref[0] = jnp.dot(both, perm_ref[...], preferred_element_type=F32).astype(BF)


def attend(pieces, base, rate, sides, bounds, perm_ref, q_low, q_high, *refs):
    count = len({piece for piece, _ in pieces.values()})
    kt_refs, v_refs = refs[:count], refs[count : 2 * count]
    out_ref, kt_s, v_s, scores_s, acc, top, att, kt_sem, v_sem = refs[-9:]
    heads = q_low.shape[1]
    low_side, high_side = sides
    first = jnp.minimum(bounds[0, low_side], bounds[0, high_side])
    last = jnp.maximum(bounds[1, low_side], bounds[1, high_side])

    def copies(tile):
        piece, at = pieces[tile]
        slot = tile - base
        return (
            pltpu.make_async_copy(kt_refs[piece].at[at], kt_s.at[slot], kt_sem.at[slot]),
            pltpu.make_async_copy(v_refs[piece].at[at], v_s.at[slot], v_sem.at[slot]),
        )

    for which in range(2):
        for tile in sorted(pieces):

            @pl.when((tile >= first) & (tile < last))
            def _():
                copies(tile)[which].start()

    def wait(which):
        for tile in sorted(pieces):

            @pl.when((tile >= first) & (tile < last))
            def _():
                copies(tile)[which].wait()

    wait(0)
    for side, q_ref in enumerate((q_low, q_high)):
        begin, end = bounds[0, sides[side]], bounds[1, sides[side]]
        acc[...] = jnp.zeros_like(acc)
        top[...] = jnp.full_like(top, FAR)

        def score(tile, carry):
            for head in range(heads):
                scores = jnp.dot(kt_s[tile - base, head], q_ref[0, head], preferred_element_type=F32)
                scores_s[tile - begin, head] = scores
                highest = jnp.max(scores.reshape(TILE // 8, 8, TILE), axis=0)
                top[head] = jnp.maximum(top[head], highest)
            return carry

        lax.fori_loop(begin, end, score, 0)
        if side == 0:
            wait(1)
        tops = [jnp.max(top[head], axis=0, keepdims=True) for head in range(heads)]
        for head in range(heads):
            top[head, 0:1] = tops[head]

        def weigh(tile, carry):
            for head in range(heads):
                scores = scores_s[tile - begin, head]
                weights = jnp.exp2((scores - top[head, 0:1]) * rate).astype(BF)
                acc[head] += jnp.dot(v_s[tile - base, head], weights, preferred_element_type=F32)
            return carry

        lax.fori_loop(begin, end, weigh, 0)
        whole = jnp.concatenate(
            [acc[head, :HEAD_DIM] / acc[head, HEAD_DIM : HEAD_DIM + 1] for head in range(heads)], axis=0
        )
        att[:, side * TILE : (side + 1) * TILE] = whole.astype(BF)
    out_ref[...] = jnp.dot(att[...], perm_ref[...], preferred_element_type=F32).astype(BF)


def project(order, col_ref, perm_ref, gain_ref, res_ref, wt_ref, mw_ref, *refs):
    count = len(order)
    att_refs = refs[:count]
    layer_ref, merged_ref, gathered, layer_s, wt_s, mw_s, att_sem, wt_sem, mw_sem = refs[count:]
    width = att_refs[0].shape[0]
    full = wt_ref.shape[0]
    col = col_ref[0]
    att_copies, wt_copies = [], []
    for part, (bit, att_ref) in enumerate(zip(order, att_refs)):
        row = pl.multiple_of((col ^ bit) * width, 16)
        att_copies.append(
            pltpu.make_async_copy(att_ref, gathered.at[pl.ds(row, width), :], att_sem.at[part])
        )
        rows = pl.ds(part * width, width)
        wt_copies.append(
            pltpu.make_async_copy(wt_ref.at[rows, :], wt_s.at[rows, :], wt_sem.at[part])
        )
    mw_copy = pltpu.make_async_copy(mw_ref, mw_s, mw_sem.at[0])
    for copy in att_copies + wt_copies + [mw_copy]:
        copy.start()
    for copy in att_copies:
        copy.wait()
    total = None
    for part in range(count):
        rows = slice(part * width, (part + 1) * width)
        wt_copies[part].wait()
        projected = jnp.dot(wt_s[rows, :], gathered[...], preferred_element_type=F32)
        layer = (res_ref[part, 0].astype(F32) + projected).astype(BF)
        layer_s[rows, :] = layer
        term = jnp.sum(layer.astype(F32).reshape(width // 8, 8, -1), axis=0)
        total = term if total is None else total + term
    own = layer_s[pl.ds(pl.multiple_of(col * width, 16), width), :]
    layer_ref[...] = lax.dot_general(
        own, perm_ref[...], (((1,), (1,)), ((), ())), preferred_element_type=F32
    ).astype(BF)
    centre = jnp.sum(total, axis=0, keepdims=True) / full
    groups = layer_s.shape[1] // 4
    mw_copy.wait()
    merged = jnp.zeros((width, groups), F32)
    for j in range(4):
        lanes = slice(j * groups, (j + 1) * groups)
        values = layer_s[:, lanes].astype(F32) - centre[:, lanes]
        spread = jnp.sum(jnp.square(values), axis=0, keepdims=True) / full
        normed = (values * lax.rsqrt(spread + 1e-06) * gain_ref[...]).astype(BF)
        merged += jnp.dot(
            mw_s[:, j * full : (j + 1) * full], normed, preferred_element_type=F32
        )
    merged_ref[...] = merged.astype(BF)


def outgoing(slot_ref, place_ref, *refs):
    out_ref = refs[-1]
    total = None
    slots = out_ref.shape[0]
    for stage, merged_ref in enumerate(refs[:-1]):
        groups = merged_ref.shape[1]
        row = lax.broadcasted_iota(jnp.int32, (slots, groups), 0)
        pick = jnp.where(row == slot_ref[stage], 1.0, 0.0).astype(BF)
        rows = jnp.concatenate([merged_ref[...], place_ref[stage]], axis=0)
        term = lax.dot_general(pick, rows, (((1,), (1,)), ((), ())), preferred_element_type=F32)
        total = term if total is None else total + term
    out_ref[...] = total.astype(BF)


def incoming(width, base, in_ref, out_ref):
    place = in_ref[:, width : width + 2].astype(F32)
    target = (place[:, 0:1] * base + place[:, 1:2]).astype(jnp.int32)
    slots = in_ref.shape[0]
    lane = lax.broadcasted_iota(jnp.int32, (slots, slots), 1)
    pick = jnp.where(lane == target, 1.0, 0.0).astype(BF)
    out_ref[...] = lax.dot_general(
        in_ref[:, :width], pick, (((0,), (0,)), ((), ())), preferred_element_type=F32
    ).astype(BF)


def body(qkv, residual_in, out_weight, merge_weight, merge_gain, image_groups, dest_row):
    width = qkv.shape[1]
    tokens = qkv.shape[2]
    heads = width // HEAD_DIM
    full = out_weight.shape[0]
    images = image_groups.shape[0]
    reach = tokens // 2
    own_tiles = tokens // TILE
    far_tiles = reach // TILE
    stages = own_tiles // 2
    depth = round_up(HEAD_DIM + images, 128)
    rate = math.log2(math.e) / math.sqrt(HEAD_DIM)
    rows, cols = lax.axis_size("row"), lax.axis_size("col")
    row_id, col_id = lax.axis_index("row"), lax.axis_index("col")
    forward = [(i, (i + 1) % rows) for i in range(rows)]
    backward = [((i + 1) % rows, i) for i in range(rows)]

    lefts, rights = [], []

    def send_chunk(stage, after):
        tail = lax.slice(qkv, (1, 0, tokens - (stage + 1) * TILE), (3, width, tokens - stage * TILE))
        head = lax.slice(qkv, (1, 0, stage * TILE), (3, width, (stage + 1) * TILE))
        if after is not None:
            tail, head, _ = lax.optimization_barrier((tail, head, after))
        lefts.append(lax.ppermute(tail, "row", forward))
        rights.append(lax.ppermute(head, "row", backward))
        return tail, head

    first_chunk = send_chunk(0, None)

    image_ends = jnp.cumsum(image_groups) * 4
    window_tiles = own_tiles + 2 * far_tiles
    positions = row_id * tokens - reach + jnp.arange(window_tiles * TILE, dtype=jnp.int32)
    labels = jnp.sum((positions[:, None] >= image_ends[None, :]).astype(jnp.int32), axis=1)
    labels = jnp.where(positions >= 0, labels, -1).reshape(window_tiles, 1, TILE)
    starts = row_id * tokens + jnp.arange(own_tiles, dtype=jnp.int32) * TILE
    ends = starts + TILE - 1
    low = jnp.max(jnp.where(image_ends[None, :] <= starts[:, None], image_ends[None, :], 0), axis=1)
    high = jnp.min(
        jnp.where(image_ends[None, :] > ends[:, None], image_ends[None, :], rows * tokens), axis=1
    )
    window_start = row_id * tokens - reach
    low = (low - window_start) // TILE
    high = (high - window_start + TILE - 1) // TILE
    tile_at = jnp.arange(own_tiles, dtype=jnp.int32)
    low = jnp.maximum(low, tile_at)
    high = jnp.minimum(high, tile_at + 2 * far_tiles + 1)

    at = jnp.arange(2 * TILE, dtype=jnp.int32)
    perm = (((at % 4) * (TILE // 2) + at // 4)[:, None] == at[None, :]).astype(BF)

    residual_in, _ = lax.optimization_barrier((residual_in, first_chunk))
    residual = pl.pallas_call(
        reorder_residual,
        grid=(stages,),
        in_specs=[
            pl.BlockSpec((2 * TILE, 2 * TILE), lambda i: (0, 0)),
            pl.BlockSpec((width, TILE), lambda i: (0, stages - 1 - i)),
            pl.BlockSpec((width, TILE), lambda i: (0, stages + i)),
        ],
        out_specs=pl.BlockSpec((1, width, 2 * TILE), lambda i: (i, 0, 0)),
        out_shape=jax.ShapeDtypeStruct((stages, width, 2 * TILE), BF),
        compiler_params=params(32),
        cost_estimate=cost(2 * width * tokens * 2 * TILE, 4 * width * tokens),
        name="reorder_residual",
    )(perm, residual_in, residual_in)
    residual = lax.all_gather(residual, "col", axis=0)

    kt_shape, v_shape = (heads, TILE, depth), (heads, HEAD_DIM + 8, TILE)
    label_spec = lambda tile: pl.BlockSpec((1, 1, TILE), lambda i: (tile, 0, 0))
    q_tiles, kt_own, v_own = pl.pallas_call(
        functools.partial(prepare_own, images, depth),
        grid=(own_tiles,),
        in_specs=[
            pl.BlockSpec((1, 1, TILE), lambda i: (i + far_tiles, 0, 0)),
            pl.BlockSpec((3, width, TILE), lambda i: (0, 0, i)),
        ],
        out_specs=[
            pl.BlockSpec((1, heads, depth, TILE), lambda i: (i, 0, 0, 0)),
            pl.BlockSpec((1,) + kt_shape, lambda i: (i, 0, 0, 0)),
            pl.BlockSpec((1,) + v_shape, lambda i: (i, 0, 0, 0)),
        ],
        out_shape=[
            jax.ShapeDtypeStruct((own_tiles, heads, depth, TILE), BF),
            jax.ShapeDtypeStruct((own_tiles,) + kt_shape, BF),
            jax.ShapeDtypeStruct((own_tiles,) + v_shape, BF),
        ],
        compiler_params=params(32),
        cost_estimate=cost(2e9, 16 * width * tokens),
        name="prepare_own",
    )(labels, qkv)

    send_chunk(1, q_tiles)
    out_weight_t = jnp.transpose(out_weight)
    key_bounds = jnp.stack([low, high])
    gain = merge_gain[:, None]
    bits = []
    span = cols // 2
    while span:
        bits.append(span)
        span //= 2
    order = [0]
    for bit in bits:
        order = order + [bit ^ other for other in order]
    col_value = col_id.astype(jnp.int32).reshape(1)

    halo = []
    layers, merged = [], []
    any_spec = pl.BlockSpec(memory_space=pl.ANY)
    smem_spec = pl.BlockSpec(memory_space=pltpu.SMEM)
    vmem_spec = pl.BlockSpec(memory_space=pltpu.VMEM)
    for stage in range(stages):
        if 2 <= stage + 1 < stages:
            send_chunk(stage + 1, (lefts[stage - 1], rights[stage - 1]))
        left_tile, right_tile = far_tiles - 1 - stage, far_tiles + own_tiles + stage
        chunk_spec = pl.BlockSpec((2, width, TILE), lambda i: (0, 0, 0))
        new = pl.pallas_call(
            functools.partial(prepare_halo, images, depth),
            grid=(1,),
            in_specs=[label_spec(left_tile), label_spec(right_tile), chunk_spec, chunk_spec],
            out_specs=[
                pl.BlockSpec((1,) + kt_shape, lambda i: (0, 0, 0, 0)),
                pl.BlockSpec((1,) + v_shape, lambda i: (0, 0, 0, 0)),
            ]
            * 2,
            out_shape=[
                jax.ShapeDtypeStruct((1,) + kt_shape, BF),
                jax.ShapeDtypeStruct((1,) + v_shape, BF),
            ]
            * 2,
            compiler_params=params(32),
            cost_estimate=cost(5e8, 16 * width * TILE),
            name="prepare_halo",
        )(labels, labels, lefts[stage], rights[stage])
        halo.append(new)

        pieces = {far_tiles + t: (0, t) for t in range(own_tiles)}
        kts, vs = [kt_own], [v_own]
        for before in range(stage + 1):
            for tile, at_piece in (
                (far_tiles - 1 - before, 0),
                (far_tiles + own_tiles + before, 2),
            ):
                pieces[tile] = (len(kts), 0)
                kts.append(halo[before][at_piece])
                vs.append(halo[before][at_piece + 1])
        tiles = len(pieces)
        low_tile, high_tile = stages - 1 - stage, stages + stage
        after = [out_weight_t] if stage < 2 else [merged[stage - 2]]
        q_spec = lambda tile: pl.BlockSpec((1, heads, depth, TILE), lambda i: (tile, 0, 0, 0))
        attended = pl.pallas_call(
            functools.partial(attend, pieces, min(pieces), rate, (low_tile, high_tile)),
            grid=(1,),
            in_specs=[smem_spec, vmem_spec, q_spec(low_tile), q_spec(high_tile)]
            + [any_spec] * (2 * len(kts) + len(after)),
            out_specs=vmem_spec,
            out_shape=jax.ShapeDtypeStruct((width, 2 * TILE), BF),
            scratch_shapes=[
                pltpu.VMEM((tiles,) + kt_shape, BF),
                pltpu.VMEM((tiles,) + v_shape, BF),
                pltpu.VMEM((2 * far_tiles + 1, heads, TILE, TILE), F32),
                pltpu.VMEM((heads, HEAD_DIM + 8, TILE), F32),
                pltpu.VMEM((heads, 8, TILE), F32),
                pltpu.VMEM((width, 2 * TILE), BF),
                pltpu.SemaphoreType.DMA((tiles,)),
                pltpu.SemaphoreType.DMA((tiles,)),
            ],
            compiler_params=params(48),
            cost_estimate=cost(5e9, 4e6),
            name="attend",
        )(key_bounds, perm, q_tiles, q_tiles, *kts, *vs, *after)

        gathered = [attended]
        for bit in bits:
            pairs = [(i, i ^ bit) for i in range(cols)]
            gathered = gathered + [lax.ppermute(piece, "col", pairs) for piece in gathered]

        layer, part = pl.pallas_call(
            functools.partial(project, order),
            grid=(1,),
            in_specs=[
                smem_spec,
                vmem_spec,
                vmem_spec,
                pl.BlockSpec((cols, 1, width, 2 * TILE), functools.partial(lambda s, i: (0, s, 0, 0), stage)),
                any_spec,
                any_spec,
            ]
            + [any_spec] * cols,
            out_specs=[vmem_spec, vmem_spec],
            out_shape=[
                jax.ShapeDtypeStruct((width, 2 * TILE), BF),
                jax.ShapeDtypeStruct((width, TILE // 2), BF),
            ],
            scratch_shapes=[
                pltpu.VMEM((full, 2 * TILE), BF),
                pltpu.VMEM((full, 2 * TILE), BF),
                pltpu.VMEM((full, full), BF),
                pltpu.VMEM((width, 4 * full), BF),
                pltpu.SemaphoreType.DMA((cols,)),
                pltpu.SemaphoreType.DMA((cols,)),
                pltpu.SemaphoreType.DMA((1,)),
            ],
            compiler_params=params(48),
            cost_estimate=cost(2 * full * full * 2 * TILE + 2 * width * full * 2 * TILE, 10e6),
            name="project",
        )(col_value, perm, gain, residual, out_weight_t, merge_weight, *gathered)
        layers.append(layer)
        merged.append(part)

    layer_out = jnp.concatenate(
        [layers[s][:, :TILE] for s in reversed(range(stages))]
        + [layers[s][:, TILE:] for s in range(stages)],
        axis=1,
    )

    groups = tokens // 4
    share = groups // rows
    piece_groups = TILE // 4
    owner = dest_row // groups
    place = dest_row % groups
    index = jnp.arange(groups, dtype=jnp.int32)
    rank = jnp.sum(
        ((owner[:, None] == owner[None, :]) & (index[None, :] < index[:, None])).astype(jnp.int32),
        axis=1,
    )
    base = 32
    info = jnp.stack([owner * share + rank, place // base, place % base])
    info = info.reshape(3, own_tiles, piece_groups)
    info = jnp.stack(
        [
            jnp.concatenate([info[:, stages - 1 - s], info[:, stages + s]], axis=1)
            for s in range(stages)
        ],
        axis=1,
    )
    slots = info[0][:, None, :]
    wide = round_up(width + 2, 128)
    places = jnp.concatenate(
        [
            jnp.stack([info[1], info[2]], axis=1).astype(BF),
            jnp.zeros((stages, wide - width - 2, 2 * piece_groups), BF),
        ],
        axis=1,
    )
    sent = pl.pallas_call(
        outgoing,
        out_shape=jax.ShapeDtypeStruct((groups, wide), BF),
        compiler_params=params(32),
        cost_estimate=cost(2 * groups * groups * wide, 2e6),
        name="outgoing",
    )(slots, places, *merged)
    received = lax.all_to_all(
        sent.reshape(rows, share, wide), "row", split_axis=0, concat_axis=0, tiled=True
    ).reshape(groups, wide)
    image_rows = pl.pallas_call(
        functools.partial(incoming, width, base),
        out_shape=jax.ShapeDtypeStruct((width, groups), BF),
        compiler_params=params(32),
        cost_estimate=cost(2 * groups * groups * wide, 2e6),
        name="incoming",
    )(received)
    return (layer_out, image_rows)


def solution(mesh):
    return jax.shard_map(
        body,
        mesh=mesh,
        in_specs=(P(None, "col", "row"), P("col", "row"), P(), P("col", None), P(), P(), P("row")),
        out_specs=(P("col", "row"), P("col", "row")),
        check_vma=False,
    )
```

```python
import functools
import math

import jax
import jax.numpy as jnp
from jax import lax
from jax.experimental import pallas as pl
from jax.experimental.pallas import tpu as pltpu
from jax.sharding import PartitionSpec as P

HEAD_DIM = 88
TILE = 256
FAR = -1e30
BF = jnp.bfloat16
F32 = jnp.float32


def params(mib):
    return pltpu.CompilerParams(vmem_limit_bytes=mib * 1024 * 1024)


def cost(flops, bytes_accessed):
    return pl.CostEstimate(flops=int(flops), bytes_accessed=int(bytes_accessed), transcendentals=0)


def round_up(value, unit):
    return -(-value // unit) * unit


def key_tile(keys, label, images, depth, kt_ref):
    heads = keys.shape[0] // HEAD_DIM
    tail = depth - HEAD_DIM
    at = lax.broadcasted_iota(jnp.int32, (tail, TILE), 0)
    mask = jnp.where((at == label) | (at >= images), 0.0, FAR)
    for head in range(heads):
        whole = jnp.concatenate([keys[head * HEAD_DIM : (head + 1) * HEAD_DIM], mask], axis=0)
        kt_ref[0, head] = jnp.transpose(whole).astype(BF)


def value_tile(values, v_ref):
    heads = values.shape[0] // HEAD_DIM
    ones = jnp.where(lax.broadcasted_iota(jnp.int32, (8, TILE), 0) == 0, 1.0, 0.0)
    for head in range(heads):
        v_ref[0, head] = jnp.concatenate(
            [values[head * HEAD_DIM : (head + 1) * HEAD_DIM], ones], axis=0
        ).astype(BF)


def prepare_own(images, depth, label_ref, qkv_ref, q_ref, kt_ref, v_ref):
    label = label_ref[0]
    queries = qkv_ref[0].astype(F32)
    heads = queries.shape[0] // HEAD_DIM
    at = lax.broadcasted_iota(jnp.int32, (depth - HEAD_DIM, TILE), 0)
    mark = jnp.where(at == label, 1.0, 0.0)
    for head in range(heads):
        q_ref[0, head] = jnp.concatenate(
            [queries[head * HEAD_DIM : (head + 1) * HEAD_DIM], mark], axis=0
        ).astype(BF)
    key_tile(qkv_ref[1].astype(F32), label, images, depth, kt_ref)
    value_tile(qkv_ref[2].astype(F32), v_ref)


def prepare_halo(images, depth, label_l, label_r, left, right, kt_l, v_l, kt_r, v_r):
    key_tile(left[0].astype(F32), label_l[0], images, depth, kt_l)
    value_tile(left[1].astype(F32), v_l)
    key_tile(right[0].astype(F32), label_r[0], images, depth, kt_r)
    value_tile(right[1].astype(F32), v_r)


def reorder_residual(perm_ref, low_ref, high_ref, out_ref):
    both = jnp.concatenate([low_ref[...], high_ref[...]], axis=1)
    out_ref[0] = jnp.dot(both, perm_ref[...], preferred_element_type=F32).astype(BF)


def attend(pieces, base, rate, sides, bounds, perm_ref, q_low, q_high, *refs):
    count = len({piece for piece, _ in pieces.values()})
    kt_refs, v_refs = refs[:count], refs[count : 2 * count]
    out_ref, kt_s, v_s, scores_s, acc, top, att, kt_sem, v_sem = refs[-9:]
    heads = q_low.shape[1]
    low_side, high_side = sides
    first = jnp.minimum(bounds[0, low_side], bounds[0, high_side])
    last = jnp.maximum(bounds[1, low_side], bounds[1, high_side])

    def copies(tile):
        piece, at = pieces[tile]
        slot = tile - base
        return (
            pltpu.make_async_copy(kt_refs[piece].at[at], kt_s.at[slot], kt_sem.at[slot]),
            pltpu.make_async_copy(v_refs[piece].at[at], v_s.at[slot], v_sem.at[slot]),
        )

    for which in range(2):
        for tile in sorted(pieces):

            @pl.when((tile >= first) & (tile < last))
            def _():
                copies(tile)[which].start()

    def wait(which):
        for tile in sorted(pieces):

            @pl.when((tile >= first) & (tile < last))
            def _():
                copies(tile)[which].wait()

    wait(0)
    for side, q_ref in enumerate((q_low, q_high)):
        begin, end = bounds[0, sides[side]], bounds[1, sides[side]]
        acc[...] = jnp.zeros_like(acc)
        top[...] = jnp.full_like(top, FAR)

        def sweep(step):
            pairs = (end - begin) // 2

            def pair(index, carry):
                step(begin + 2 * index, 2)
                return carry

            def single(index, carry):
                step(end - 1, 1)
                return carry

            lax.fori_loop(0, pairs, pair, 0)
            lax.fori_loop(0, end - begin - 2 * pairs, single, 0)

        def score(tile, span):
            for head in range(heads):
                keys = kt_s[pl.ds(tile - base, span), head].reshape(span * TILE, -1)
                scores = jnp.dot(keys, q_ref[0, head], preferred_element_type=F32)
                scores_s[pl.ds(tile - begin, span), head] = scores.reshape(span, TILE, TILE)
                highest = jnp.max(scores.reshape(span * TILE // 8, 8, TILE), axis=0)
                top[head] = jnp.maximum(top[head], highest)

        sweep(score)
        if side == 0:
            wait(1)
        tops = [jnp.max(top[head], axis=0, keepdims=True) for head in range(heads)]
        for head in range(heads):
            top[head, 0:1] = tops[head]

        def weigh(tile, span):
            for head in range(heads):
                scores = scores_s[pl.ds(tile - begin, span), head].reshape(span * TILE, TILE)
                weights = jnp.exp2((scores - top[head, 0:1]) * rate).astype(BF)
                values = [v_s[tile - base + at, head] for at in range(span)]
                values = values[0] if span == 1 else jnp.concatenate(values, axis=1)
                acc[head] += jnp.dot(values, weights, preferred_element_type=F32)

        sweep(weigh)
        whole = jnp.concatenate(
            [acc[head, :HEAD_DIM] / acc[head, HEAD_DIM : HEAD_DIM + 1] for head in range(heads)], axis=0
        )
        att[:, side * TILE : (side + 1) * TILE] = whole.astype(BF)
    out_ref[...] = jnp.dot(att[...], perm_ref[...], preferred_element_type=F32).astype(BF)


def project(order, last, col_ref, perm_ref, gain_ref, res_ref, wt_ref, mw_ref, *refs):
    count = len(order)
    att_refs, refs = refs[:count], refs[count:]
    if last:
        before_ref, refs = refs[0], refs[1:]
    layer_ref, out_ref, gathered, layer_s, wt_s, mw_s, att_sem, wt_sem, mw_sem = refs
    width = att_refs[0].shape[0]
    full = wt_ref.shape[0]
    col = col_ref[0]
    att_copies, wt_copies = [], []
    for part, (bit, att_ref) in enumerate(zip(order, att_refs)):
        row = pl.multiple_of((col ^ bit) * width, 16)
        att_copies.append(
            pltpu.make_async_copy(att_ref, gathered.at[pl.ds(row, width), :], att_sem.at[part])
        )
        rows = pl.ds(part * width, width)
        wt_copies.append(
            pltpu.make_async_copy(wt_ref.at[rows, :], wt_s.at[rows, :], wt_sem.at[part])
        )
    mw_copy = pltpu.make_async_copy(mw_ref, mw_s, mw_sem.at[0])
    for copy in att_copies + wt_copies + [mw_copy] * last:
        copy.start()
    for copy in att_copies:
        copy.wait()
    total = None
    for part in range(count):
        rows = slice(part * width, (part + 1) * width)
        wt_copies[part].wait()
        projected = jnp.dot(wt_s[rows, :], gathered[...], preferred_element_type=F32)
        layer = (res_ref[part, 0].astype(F32) + projected).astype(BF)
        layer_s[rows, :] = layer
        term = jnp.sum(layer.astype(F32).reshape(width // 8, 8, -1), axis=0)
        total = term if total is None else total + term
    own = layer_s[pl.ds(pl.multiple_of(col * width, 16), width), :]
    layer_ref[...] = lax.dot_general(
        own, perm_ref[...], (((1,), (1,)), ((), ())), preferred_element_type=F32
    ).astype(BF)
    centre = jnp.sum(total, axis=0, keepdims=True) / full
    groups = layer_s.shape[1] // 4
    if last:
        mw_copy.wait()
    merged = jnp.zeros((width, 2 * groups), F32)
    for j in range(4):
        lanes = slice(j * groups, (j + 1) * groups)
        values = layer_s[:, lanes].astype(F32) - centre[:, lanes]
        spread = jnp.sum(jnp.square(values), axis=0, keepdims=True) / full
        normed = (values * lax.rsqrt(spread + 1e-06) * gain_ref[...]).astype(BF)
        if last:
            both = jnp.concatenate([before_ref[:, lanes], normed], axis=1)
            merged += jnp.dot(
                mw_s[:, j * full : (j + 1) * full], both, preferred_element_type=F32
            )
        else:
            out_ref[:, lanes] = normed
    if last:
        out_ref[...] = merged.astype(BF)


def outgoing(pieces, slot_ref, place_ref, *refs):
    merged_refs, out_refs = refs[:-pieces], refs[-pieces:]
    total = None
    share, wide = out_refs[0].shape
    for part, merged_ref in enumerate(merged_refs):
        groups = merged_ref.shape[1]
        row = lax.broadcasted_iota(jnp.int32, (share * pieces, groups), 0)
        pick = jnp.where(row == slot_ref[part], 1.0, 0.0).astype(BF)
        rows = jnp.concatenate([merged_ref[...], place_ref[part]], axis=0)
        term = lax.dot_general(pick, rows, (((1,), (1,)), ((), ())), preferred_element_type=F32)
        total = term if total is None else total + term
    for piece, out_ref in enumerate(out_refs):
        out_ref[...] = total[piece * share : (piece + 1) * share].astype(BF)


def incoming(width, base, *refs):
    in_refs, out_ref = refs[:-1], refs[-1]
    rows = jnp.concatenate([in_ref[...] for in_ref in in_refs], axis=0)
    place = rows[:, width : width + 2].astype(F32)
    target = (place[:, 0:1] * base + place[:, 1:2]).astype(jnp.int32)
    slots = rows.shape[0]
    lane = lax.broadcasted_iota(jnp.int32, (slots, slots), 1)
    pick = jnp.where(lane == target, 1.0, 0.0).astype(BF)
    out_ref[...] = lax.dot_general(
        rows[:, :width], pick, (((0,), (0,)), ((), ())), preferred_element_type=F32
    ).astype(BF)


def body(qkv, residual_in, out_weight, merge_weight, merge_gain, image_groups, dest_row):
    width = qkv.shape[1]
    tokens = qkv.shape[2]
    heads = width // HEAD_DIM
    full = out_weight.shape[0]
    images = image_groups.shape[0]
    reach = tokens // 2
    own_tiles = tokens // TILE
    far_tiles = reach // TILE
    stages = own_tiles // 2
    depth = round_up(HEAD_DIM + images, 128)
    rate = math.log2(math.e) / math.sqrt(HEAD_DIM)
    rows, cols = lax.axis_size("row"), lax.axis_size("col")
    row_id, col_id = lax.axis_index("row"), lax.axis_index("col")
    forward = [(i, (i + 1) % rows) for i in range(rows)]
    backward = [((i + 1) % rows, i) for i in range(rows)]

    lefts, rights = [], []

    def send_chunk(stage, after):
        source = qkv
        if after is not None:
            source, _ = lax.optimization_barrier((qkv, after))
        tail = lax.slice(source, (1, 0, tokens - (stage + 1) * TILE), (3, width, tokens - stage * TILE))
        head = lax.slice(source, (1, 0, stage * TILE), (3, width, (stage + 1) * TILE))
        lefts.append(lax.ppermute(tail, "row", forward))
        rights.append(lax.ppermute(head, "row", backward))
        return tail, head

    first_chunk = send_chunk(0, None)

    image_ends = jnp.cumsum(image_groups) * 4
    window_tiles = own_tiles + 2 * far_tiles
    positions = row_id * tokens - reach + jnp.arange(window_tiles * TILE, dtype=jnp.int32)
    labels = jnp.sum((positions[:, None] >= image_ends[None, :]).astype(jnp.int32), axis=1)
    labels = jnp.where(positions >= 0, labels, -1).reshape(window_tiles, 1, TILE)
    starts = row_id * tokens + jnp.arange(own_tiles, dtype=jnp.int32) * TILE
    ends = starts + TILE - 1
    low = jnp.max(jnp.where(image_ends[None, :] <= starts[:, None], image_ends[None, :], 0), axis=1)
    high = jnp.min(
        jnp.where(image_ends[None, :] > ends[:, None], image_ends[None, :], rows * tokens), axis=1
    )
    window_start = row_id * tokens - reach
    low = (low - window_start) // TILE
    high = (high - window_start + TILE - 1) // TILE
    tile_at = jnp.arange(own_tiles, dtype=jnp.int32)
    low = jnp.maximum(low, tile_at)
    high = jnp.minimum(high, tile_at + 2 * far_tiles + 1)

    at = jnp.arange(2 * TILE, dtype=jnp.int32)
    perm = (((at % 4) * (TILE // 2) + at // 4)[:, None] == at[None, :]).astype(BF)

    qkv_after, _ = lax.optimization_barrier((qkv, first_chunk))
    kt_shape, v_shape = (heads, TILE, depth), (heads, HEAD_DIM + 8, TILE)
    label_spec = lambda tile: pl.BlockSpec((1, 1, TILE), lambda i: (tile, 0, 0))
    q_tiles, kt_own, v_own = pl.pallas_call(
        functools.partial(prepare_own, images, depth),
        grid=(own_tiles,),
        in_specs=[
            pl.BlockSpec((1, 1, TILE), lambda i: (i + far_tiles, 0, 0)),
            pl.BlockSpec((3, width, TILE), lambda i: (0, 0, i)),
        ],
        out_specs=[
            pl.BlockSpec((1, heads, depth, TILE), lambda i: (i, 0, 0, 0)),
            pl.BlockSpec((1,) + kt_shape, lambda i: (i, 0, 0, 0)),
            pl.BlockSpec((1,) + v_shape, lambda i: (i, 0, 0, 0)),
        ],
        out_shape=[
            jax.ShapeDtypeStruct((own_tiles, heads, depth, TILE), BF),
            jax.ShapeDtypeStruct((own_tiles,) + kt_shape, BF),
            jax.ShapeDtypeStruct((own_tiles,) + v_shape, BF),
        ],
        compiler_params=params(63),
        cost_estimate=cost(1e8, 1e5),
        name="prepare_own",
    )(labels, qkv_after)

    send_chunk(1, q_tiles)
    residual_in, _ = lax.optimization_barrier((residual_in, first_chunk))
    residual = pl.pallas_call(
        reorder_residual,
        grid=(stages,),
        in_specs=[
            pl.BlockSpec((2 * TILE, 2 * TILE), lambda i: (0, 0)),
            pl.BlockSpec((width, TILE), lambda i: (0, stages - 1 - i)),
            pl.BlockSpec((width, TILE), lambda i: (0, stages + i)),
        ],
        out_specs=pl.BlockSpec((1, width, 2 * TILE), lambda i: (i, 0, 0)),
        out_shape=jax.ShapeDtypeStruct((stages, width, 2 * TILE), BF),
        compiler_params=params(63),
        cost_estimate=cost(1e8, 1e5),
        name="reorder_residual",
    )(perm, residual_in, residual_in)
    residual = lax.all_gather(residual, "col", axis=0)
    out_weight_t = jnp.transpose(out_weight)
    key_bounds = jnp.stack([low, high])
    gain = merge_gain[:, None]
    bits = []
    span = cols // 2
    while span:
        bits.append(span)
        span //= 2
    order = [0]
    for bit in bits:
        order = order + [bit ^ other for other in order]
    col_value = col_id.astype(jnp.int32).reshape(1)

    halo = []
    layers, parts, gathers = [], [], []
    any_spec = pl.BlockSpec(memory_space=pl.ANY)
    smem_spec = pl.BlockSpec(memory_space=pltpu.SMEM)
    vmem_spec = pl.BlockSpec(memory_space=pltpu.VMEM)
    def spread_pieces(stage, some_bits, after):
        pieces = gathers[stage]
        for bit in some_bits:
            pairs = [(i, i ^ bit) for i in range(cols)]
            sources = pieces
            if after is not None:
                sources, _ = lax.optimization_barrier((pieces, after))
            pieces = pieces + [lax.ppermute(piece, "col", pairs) for piece in sources]
        gathers[stage] = pieces

    def run_project(stage):
        last = stage % 2
        before = [parts[stage - 1]] if last else []
        layer, part = pl.pallas_call(
            functools.partial(project, order, last),
            grid=(1,),
            in_specs=[
                smem_spec,
                vmem_spec,
                vmem_spec,
                pl.BlockSpec((cols, 1, width, 2 * TILE), functools.partial(lambda s, i: (0, s, 0, 0), stage)),
                any_spec,
                any_spec,
            ]
            + [any_spec] * cols
            + [vmem_spec] * last,
            out_specs=[vmem_spec, vmem_spec],
            out_shape=[
                jax.ShapeDtypeStruct((width, 2 * TILE), BF),
                jax.ShapeDtypeStruct((width, TILE) if last else (full, 2 * TILE), BF),
            ],
            scratch_shapes=[
                pltpu.VMEM((full, 2 * TILE), BF),
                pltpu.VMEM((full, 2 * TILE), BF),
                pltpu.VMEM((full, full), BF),
                pltpu.VMEM((width, 4 * full), BF),
                pltpu.SemaphoreType.DMA((cols,)),
                pltpu.SemaphoreType.DMA((cols,)),
                pltpu.SemaphoreType.DMA((1,)),
            ],
            compiler_params=params(63),
            cost_estimate=cost(1e8, 1e5),
            name="project",
        )(col_value, perm, gain, residual, out_weight_t, merge_weight, *gathers[stage], *before)
        layers.append(layer)
        parts.append(part)

    for stage in range(stages):
        if 2 <= stage + 1 < stages:
            send_chunk(stage + 1, (lefts[stage - 1], rights[stage - 1]))
        left_tile, right_tile = far_tiles - 1 - stage, far_tiles + own_tiles + stage
        chunk_spec = pl.BlockSpec((2, width, TILE), lambda i: (0, 0, 0))
        new = pl.pallas_call(
            functools.partial(prepare_halo, images, depth),
            grid=(1,),
            in_specs=[label_spec(left_tile), label_spec(right_tile), chunk_spec, chunk_spec],
            out_specs=[
                pl.BlockSpec((1,) + kt_shape, lambda i: (0, 0, 0, 0)),
                pl.BlockSpec((1,) + v_shape, lambda i: (0, 0, 0, 0)),
            ]
            * 2,
            out_shape=[
                jax.ShapeDtypeStruct((1,) + kt_shape, BF),
                jax.ShapeDtypeStruct((1,) + v_shape, BF),
            ]
            * 2,
            compiler_params=params(63),
            cost_estimate=cost(1e8, 1e5),
            name="prepare_halo",
        )(labels, labels, lefts[stage], rights[stage])
        halo.append(new)

        pieces = {far_tiles + t: (0, t) for t in range(own_tiles)}
        kts, vs = [kt_own], [v_own]
        for before in range(stage + 1):
            for tile, at_piece in (
                (far_tiles - 1 - before, 0),
                (far_tiles + own_tiles + before, 2),
            ):
                pieces[tile] = (len(kts), 0)
                kts.append(halo[before][at_piece])
                vs.append(halo[before][at_piece + 1])
        tiles = len(pieces)
        low_tile, high_tile = stages - 1 - stage, stages + stage
        after = [out_weight_t] if stage < 2 else [layers[stage - 2]]
        q_spec = lambda tile: pl.BlockSpec((1, heads, depth, TILE), lambda i: (tile, 0, 0, 0))
        attended = pl.pallas_call(
            functools.partial(attend, pieces, min(pieces), rate, (low_tile, high_tile)),
            grid=(1,),
            in_specs=[smem_spec, vmem_spec, q_spec(low_tile), q_spec(high_tile)]
            + [any_spec] * (2 * len(kts) + len(after)),
            out_specs=vmem_spec,
            out_shape=jax.ShapeDtypeStruct((width, 2 * TILE), BF),
            scratch_shapes=[
                pltpu.VMEM((tiles,) + kt_shape, BF),
                pltpu.VMEM((tiles,) + v_shape, BF),
                pltpu.VMEM((2 * far_tiles + 1, heads, TILE, TILE), F32),
                pltpu.VMEM((heads, HEAD_DIM + 8, TILE), F32),
                pltpu.VMEM((heads, 8, TILE), F32),
                pltpu.VMEM((width, 2 * TILE), BF),
                pltpu.SemaphoreType.DMA((tiles,)),
                pltpu.SemaphoreType.DMA((tiles,)),
            ],
            compiler_params=params(63),
            cost_estimate=cost(1e8, 1e5),
            name="attend",
        )(key_bounds, perm, q_tiles, q_tiles, *kts, *vs, *after)

        gathers.append([attended])
        spread_pieces(stage, bits[:1], None)
        if stage == 1:
            spread_pieces(0, bits[1:], attended)
        if stage >= 1:
            run_project(stage - 1)
            spread_pieces(stage, bits[1:], layers[stage - 1])
    run_project(stages - 1)

    layer_out = jnp.concatenate(
        [layers[s][:, :TILE] for s in reversed(range(stages))]
        + [layers[s][:, TILE:] for s in range(stages)],
        axis=1,
    )

    groups = tokens // 4
    share = groups // rows
    piece_groups = TILE // 4
    owner = dest_row // groups
    place = dest_row % groups
    index = jnp.arange(groups, dtype=jnp.int32)
    rank = jnp.sum(
        ((owner[:, None] == owner[None, :]) & (index[None, :] < index[:, None])).astype(jnp.int32),
        axis=1,
    )
    base = 32
    away = (owner - row_id) % rows
    info = jnp.stack([away * share + rank, place // base, place % base])
    info = info.reshape(3, own_tiles, piece_groups)
    halves = stages // 2
    info = jnp.stack(
        [
            jnp.concatenate(
                [info[:, t] for s in (2 * h, 2 * h + 1) for t in (stages - 1 - s, stages + s)], axis=1
            )
            for h in range(halves)
        ],
        axis=1,
    )
    slots = info[0][:, None, :]
    wide = round_up(width + 2, 128)
    places = jnp.concatenate(
        [
            jnp.stack([info[1], info[2]], axis=1).astype(BF),
            jnp.zeros((halves, wide - width - 2, 4 * piece_groups), BF),
        ],
        axis=1,
    )
    sent = pl.pallas_call(
        functools.partial(outgoing, rows),
        out_shape=[jax.ShapeDtypeStruct((share, wide), BF)] * rows,
        compiler_params=params(63),
        cost_estimate=cost(1e8, 1e5),
        name="outgoing",
    )(slots, places, *parts[1::2])
    received = [sent[0]] + [
        lax.ppermute(sent[step], "row", [(i, (i + step) % rows) for i in range(rows)])
        for step in range(1, rows)
    ]
    image_rows = pl.pallas_call(
        functools.partial(incoming, width, base),
        out_shape=jax.ShapeDtypeStruct((width, groups), BF),
        compiler_params=params(63),
        cost_estimate=cost(1e8, 1e5),
        name="incoming",
    )(*received)
    return (layer_out, image_rows)


def solution(mesh):
    return jax.shard_map(
        body,
        mesh=mesh,
        in_specs=(P(None, "col", "row"), P("col", "row"), P(), P("col", None), P(), P(), P("row")),
        out_specs=(P("col", "row"), P("col", "row")),
        check_vma=False,
    )
```

```python
import functools
import math

import jax
import jax.numpy as jnp
from jax import lax
from jax.experimental import pallas as pl
from jax.experimental.pallas import tpu as pltpu
from jax.sharding import PartitionSpec as P

HEAD_DIM = 88
TILE = 256
FAR = -1e30
BF = jnp.bfloat16
F32 = jnp.float32


def params(mib):
    return pltpu.CompilerParams(vmem_limit_bytes=mib * 1024 * 1024)


def cost(flops, bytes_accessed):
    return pl.CostEstimate(flops=int(flops), bytes_accessed=int(bytes_accessed), transcendentals=0)


def round_up(value, unit):
    return -(-value // unit) * unit


def key_tile(keys, label, images, depth, kt_ref):
    heads = keys.shape[0] // HEAD_DIM
    tail = depth - HEAD_DIM
    at = lax.broadcasted_iota(jnp.int32, (tail, TILE), 0)
    mask = jnp.where((at == label) | (at >= images), 0.0, FAR)
    for head in range(heads):
        whole = jnp.concatenate([keys[head * HEAD_DIM : (head + 1) * HEAD_DIM], mask], axis=0)
        kt_ref[0, head] = jnp.transpose(whole).astype(BF)


def value_tile(values, v_ref):
    heads = values.shape[0] // HEAD_DIM
    ones = jnp.where(lax.broadcasted_iota(jnp.int32, (8, TILE), 0) == 0, 1.0, 0.0)
    for head in range(heads):
        v_ref[0, head] = jnp.concatenate(
            [values[head * HEAD_DIM : (head + 1) * HEAD_DIM], ones], axis=0
        ).astype(BF)


def prepare_own(images, depth, label_ref, qkv_ref, q_ref, kt_ref, v_ref):
    label = label_ref[0]
    queries = qkv_ref[0].astype(F32)
    heads = queries.shape[0] // HEAD_DIM
    at = lax.broadcasted_iota(jnp.int32, (depth - HEAD_DIM, TILE), 0)
    mark = jnp.where(at == label, 1.0, 0.0)
    for head in range(heads):
        q_ref[0, head] = jnp.concatenate(
            [queries[head * HEAD_DIM : (head + 1) * HEAD_DIM], mark], axis=0
        ).astype(BF)
    key_tile(qkv_ref[1].astype(F32), label, images, depth, kt_ref)
    value_tile(qkv_ref[2].astype(F32), v_ref)


def prepare_halo(images, depth, label_l, label_r, left, right, kt_l, v_l, kt_r, v_r):
    key_tile(left[0].astype(F32), label_l[0], images, depth, kt_l)
    value_tile(left[1].astype(F32), v_l)
    key_tile(right[0].astype(F32), label_r[0], images, depth, kt_r)
    value_tile(right[1].astype(F32), v_r)


def reorder_residual(perm_ref, low_ref, high_ref, out_ref):
    both = jnp.concatenate([low_ref[...], high_ref[...]], axis=1)
    out_ref[0] = jnp.dot(both, perm_ref[...], preferred_element_type=F32).astype(BF)


def attend(own, halves, base, rate, q_tiles, bounds, perm_ref, *refs):
    count = 1 + len(halves)
    q_refs, refs = refs[: len(q_tiles)], refs[len(q_tiles) :]
    kt_refs, v_refs = refs[:count], refs[count : 2 * count]
    out_ref, kt_s, v_s, scores_s, acc, top, att, kt_sem, v_sem = refs[-9:]
    heads = q_refs[0].shape[1]

    def copies(from_refs, to_ref, sem):
        slots = pl.ds(own[0] - base, len(own))
        made = [pltpu.make_async_copy(from_refs[0], to_ref.at[slots], sem.at[0])]
        for tile, operand in halves.items():
            made.append(
                pltpu.make_async_copy(from_refs[operand], to_ref.at[pl.ds(tile - base, 1)], sem.at[operand])
            )
        return made

    kt_copies = copies(kt_refs, kt_s, kt_sem)
    v_copies = copies(v_refs, v_s, v_sem)
    for copy in kt_copies + v_copies:
        copy.start()
    for copy in kt_copies:
        copy.wait()
    for side, q_ref in enumerate(q_refs):
        begin, end = bounds[0, q_tiles[side]], bounds[1, q_tiles[side]]
        acc[...] = jnp.zeros_like(acc)
        top[...] = jnp.full_like(top, FAR)

        def sweep(step):
            pairs = (end - begin) // 2

            def pair(index, carry):
                step(begin + 2 * index, 2)
                return carry

            def single(index, carry):
                step(end - 1, 1)
                return carry

            lax.fori_loop(0, pairs, pair, 0)
            lax.fori_loop(0, end - begin - 2 * pairs, single, 0)

        def score(tile, span):
            for head in range(heads):
                keys = kt_s[pl.ds(tile - base, span), head].reshape(span * TILE, -1)
                scores = jnp.dot(keys, q_ref[0, head], preferred_element_type=F32)
                scores_s[pl.ds(tile - begin, span), head] = scores.reshape(span, TILE, TILE)
                highest = jnp.max(scores.reshape(span * TILE // 8, 8, TILE), axis=0)
                top[head] = jnp.maximum(top[head], highest)

        sweep(score)
        if side == 0:
            for copy in v_copies:
                copy.wait()
        tops = [jnp.max(top[head], axis=0, keepdims=True) for head in range(heads)]
        for head in range(heads):
            top[head, 0:1] = tops[head]

        def weigh(tile, span):
            for head in range(heads):
                scores = scores_s[pl.ds(tile - begin, span), head].reshape(span * TILE, TILE)
                weights = jnp.exp2((scores - top[head, 0:1]) * rate).astype(BF)
                values = [v_s[tile - base + at, head] for at in range(span)]
                values = values[0] if span == 1 else jnp.concatenate(values, axis=1)
                acc[head] += jnp.dot(values, weights, preferred_element_type=F32)

        sweep(weigh)
        whole = jnp.concatenate(
            [acc[head, :HEAD_DIM] / acc[head, HEAD_DIM : HEAD_DIM + 1] for head in range(heads)], axis=0
        )
        att[:, side * TILE : (side + 1) * TILE] = whole.astype(BF)
        if side % 2:
            lanes = slice((side - 1) * TILE, (side + 1) * TILE)
            out_ref[:, lanes] = jnp.dot(
                att[:, lanes], perm_ref[...], preferred_element_type=F32
            ).astype(BF)


def project(order, last, paired, col_ref, perm_ref, gain_ref, res_ref, wt_ref, mw_ref, *refs):
    count = len(order)
    att_refs, refs = refs[:count], refs[count:]
    if paired:
        before_ref, refs = refs[0], refs[1:]
    layer_ref, out_ref, gathered, layer_s, wt_s, mw_s, att_sem, wt_sem, mw_sem = refs
    width = att_refs[0].shape[0]
    full = wt_ref.shape[0]
    block = 2 * TILE
    blocks = layer_s.shape[1] // block
    groups = block // 4
    col = col_ref[0]
    att_copies, wt_copies = [], []
    for part, (bit, att_ref) in enumerate(zip(order, att_refs)):
        row = pl.multiple_of((col ^ bit) * width, 16)
        att_copies.append(
            pltpu.make_async_copy(att_ref, gathered.at[pl.ds(row, width), :], att_sem.at[part])
        )
        rows = pl.ds(part * width, width)
        wt_copies.append(
            pltpu.make_async_copy(wt_ref.at[rows, :], wt_s.at[rows, :], wt_sem.at[part])
        )
    mw_copy = pltpu.make_async_copy(mw_ref, mw_s, mw_sem.at[0])
    for copy in att_copies + wt_copies + [mw_copy] * last:
        copy.start()
    for copy in att_copies:
        copy.wait()
    for part in range(count):
        rows = slice(part * width, (part + 1) * width)
        wt_copies[part].wait()
        for at in range(blocks):
            lanes = slice(at * block, (at + 1) * block)
            projected = jnp.dot(wt_s[rows, :], gathered[:, lanes], preferred_element_type=F32)
            layer_s[rows, lanes] = (res_ref[part, at].astype(F32) + projected).astype(BF)
    own = pl.ds(pl.multiple_of(col * width, 16), width)
    for at in range(blocks):
        lanes = slice(at * block, (at + 1) * block)
        layer_ref[:, lanes] = lax.dot_general(
            layer_s[own, lanes], perm_ref[...], (((1,), (1,)), ((), ())), preferred_element_type=F32
        ).astype(BF)
    if last:
        mw_copy.wait()
    merged = None
    for j in range(4):
        columns = []
        for at in range(blocks):
            lanes = slice(at * block + j * groups, at * block + (j + 1) * groups)
            values = layer_s[:, lanes].astype(F32)
            values = values - jnp.sum(values, axis=0, keepdims=True) / full
            spread = jnp.sum(jnp.square(values), axis=0, keepdims=True) / full
            normed = (values * lax.rsqrt(spread + 1e-06) * gain_ref[...]).astype(BF)
            if last:
                columns.append(normed)
            else:
                out_ref[:, lanes] = normed
        if last:
            if paired:
                columns = [before_ref[:, j * groups : (j + 1) * groups]] + columns
            both = jnp.concatenate(columns, axis=1)
            term = jnp.dot(mw_s[:, j * full : (j + 1) * full], both, preferred_element_type=F32)
            merged = term if merged is None else merged + term
    if last:
        out_ref[...] = merged.astype(BF)


def outgoing(pieces, slot_ref, place_ref, *refs):
    merged_refs, out_refs = refs[:-pieces], refs[-pieces:]
    total = None
    share, wide = out_refs[0].shape
    for part, merged_ref in enumerate(merged_refs):
        groups = merged_ref.shape[1]
        row = lax.broadcasted_iota(jnp.int32, (share * pieces, groups), 0)
        pick = jnp.where(row == slot_ref[part], 1.0, 0.0).astype(BF)
        rows = jnp.concatenate([merged_ref[...], place_ref[part]], axis=0)
        term = lax.dot_general(pick, rows, (((1,), (1,)), ((), ())), preferred_element_type=F32)
        total = term if total is None else total + term
    for piece, out_ref in enumerate(out_refs):
        out_ref[...] = total[piece * share : (piece + 1) * share].astype(BF)


def incoming(width, base, *refs):
    in_refs, out_ref = refs[:-1], refs[-1]
    rows = jnp.concatenate([in_ref[...] for in_ref in in_refs], axis=0)
    place = rows[:, width : width + 2].astype(F32)
    target = (place[:, 0:1] * base + place[:, 1:2]).astype(jnp.int32)
    slots = rows.shape[0]
    lane = lax.broadcasted_iota(jnp.int32, (slots, slots), 1)
    pick = jnp.where(lane == target, 1.0, 0.0).astype(BF)
    out_ref[...] = lax.dot_general(
        rows[:, :width], pick, (((0,), (0,)), ((), ())), preferred_element_type=F32
    ).astype(BF)


def body(qkv, residual_in, out_weight, merge_weight, merge_gain, image_groups, dest_row):
    width = qkv.shape[1]
    tokens = qkv.shape[2]
    heads = width // HEAD_DIM
    full = out_weight.shape[0]
    images = image_groups.shape[0]
    reach = tokens // 2
    own_tiles = tokens // TILE
    far_tiles = reach // TILE
    half = own_tiles // 2
    plan = [half // 2] + [1] * (half - half // 2)
    begins = [sum(plan[:s]) for s in range(len(plan))]
    stages = len(plan)
    depth = round_up(HEAD_DIM + images, 128)
    rate = math.log2(math.e) / math.sqrt(HEAD_DIM)
    rows, cols = lax.axis_size("row"), lax.axis_size("col")
    row_id, col_id = lax.axis_index("row"), lax.axis_index("col")
    forward = [(i, (i + 1) % rows) for i in range(rows)]
    backward = [((i + 1) % rows, i) for i in range(rows)]

    lefts, rights = [], []

    def send_chunk(stage, after):
        source = qkv
        if after is not None:
            source, _ = lax.optimization_barrier((qkv, after))
        near, far = begins[stage] * TILE, (begins[stage] + plan[stage]) * TILE
        tail = lax.slice(source, (1, 0, tokens - far), (3, width, tokens - near))
        head = lax.slice(source, (1, 0, near), (3, width, far))
        lefts.append(lax.ppermute(tail, "row", forward))
        rights.append(lax.ppermute(head, "row", backward))
        return tail, head

    first_chunk = send_chunk(0, None)

    image_ends = jnp.cumsum(image_groups) * 4
    window_tiles = own_tiles + 2 * far_tiles
    positions = row_id * tokens - reach + jnp.arange(window_tiles * TILE, dtype=jnp.int32)
    labels = jnp.sum((positions[:, None] >= image_ends[None, :]).astype(jnp.int32), axis=1)
    labels = jnp.where(positions >= 0, labels, -1).reshape(window_tiles, 1, TILE)
    starts = row_id * tokens + jnp.arange(own_tiles, dtype=jnp.int32) * TILE
    ends = starts + TILE - 1
    low = jnp.max(jnp.where(image_ends[None, :] <= starts[:, None], image_ends[None, :], 0), axis=1)
    high = jnp.min(
        jnp.where(image_ends[None, :] > ends[:, None], image_ends[None, :], rows * tokens), axis=1
    )
    window_start = row_id * tokens - reach
    low = (low - window_start) // TILE
    high = (high - window_start + TILE - 1) // TILE
    tile_at = jnp.arange(own_tiles, dtype=jnp.int32)
    low = jnp.maximum(low, tile_at)
    high = jnp.minimum(high, tile_at + 2 * far_tiles + 1)

    inner = plan[0]

    def pair_tile(block, which):
        near = half - inner + 2 * block + which
        mirrored = half + block if which else half - 1 - block
        if isinstance(block, int):
            return near if block < inner else mirrored
        return jnp.where(block < inner, near, mirrored)

    at = jnp.arange(2 * TILE, dtype=jnp.int32)
    perm = (((at % 4) * (TILE // 2) + at // 4)[:, None] == at[None, :]).astype(BF)

    qkv_after, _ = lax.optimization_barrier((qkv, first_chunk))
    kt_shape, v_shape = (heads, TILE, depth), (heads, HEAD_DIM + 8, TILE)
    label_spec = lambda tile: pl.BlockSpec((1, 1, TILE), lambda i: (tile, 0, 0))
    q_tiles, kt_own, v_own = pl.pallas_call(
        functools.partial(prepare_own, images, depth),
        grid=(own_tiles,),
        in_specs=[
            pl.BlockSpec((1, 1, TILE), lambda i: (i + far_tiles, 0, 0)),
            pl.BlockSpec((3, width, TILE), lambda i: (0, 0, i)),
        ],
        out_specs=[
            pl.BlockSpec((1, heads, depth, TILE), lambda i: (i, 0, 0, 0)),
            pl.BlockSpec((1,) + kt_shape, lambda i: (i, 0, 0, 0)),
            pl.BlockSpec((1,) + v_shape, lambda i: (i, 0, 0, 0)),
        ],
        out_shape=[
            jax.ShapeDtypeStruct((own_tiles, heads, depth, TILE), BF),
            jax.ShapeDtypeStruct((own_tiles,) + kt_shape, BF),
            jax.ShapeDtypeStruct((own_tiles,) + v_shape, BF),
        ],
        compiler_params=params(16),
        cost_estimate=cost(2e9, 1e5),
        name="prepare_own",
    )(labels, qkv_after)

    send_chunk(1, q_tiles)
    residual_in, _ = lax.optimization_barrier((residual_in, first_chunk))
    blocks = own_tiles // 2
    residual = pl.pallas_call(
        reorder_residual,
        grid=(blocks,),
        in_specs=[
            pl.BlockSpec((2 * TILE, 2 * TILE), lambda i: (0, 0)),
            pl.BlockSpec((width, TILE), lambda i: (0, pair_tile(i, 0))),
            pl.BlockSpec((width, TILE), lambda i: (0, pair_tile(i, 1))),
        ],
        out_specs=pl.BlockSpec((1, width, 2 * TILE), lambda i: (i, 0, 0)),
        out_shape=jax.ShapeDtypeStruct((blocks, width, 2 * TILE), BF),
        compiler_params=params(16),
        cost_estimate=cost(2e9, 1e5),
        name="reorder_residual",
    )(perm, residual_in, residual_in)
    residual = lax.all_gather(residual, "col", axis=0)
    out_weight_t = jnp.transpose(out_weight)
    key_bounds = jnp.stack([low, high])
    gain = merge_gain[:, None]
    bits = []
    span = cols // 2
    while span:
        bits.append(span)
        span //= 2
    order = [0]
    for bit in bits:
        order = order + [bit ^ other for other in order]
    col_value = col_id.astype(jnp.int32).reshape(1)

    halo = {}
    layers, parts, gathers = [], [], []
    any_spec = pl.BlockSpec(memory_space=pl.ANY)
    smem_spec = pl.BlockSpec(memory_space=pltpu.SMEM)
    vmem_spec = pl.BlockSpec(memory_space=pltpu.VMEM)
    def spread_pieces(stage, some_bits, after):
        pieces = gathers[stage]
        for bit in some_bits:
            pairs = [(i, i ^ bit) for i in range(cols)]
            sources = pieces
            if after is not None:
                sources, _ = lax.optimization_barrier((pieces, after))
            pieces = pieces + [lax.ppermute(piece, "col", pairs) for piece in sources]
        gathers[stage] = pieces

    def run_project(stage):
        size = plan[stage]
        paired = stage == stages - 1 and stages - 1 > 1
        last = stage == 0 or stage == stages - 1
        before = [parts[stage - 1]] if paired else []
        columns = 2 * size * TILE
        layer, part = pl.pallas_call(
            functools.partial(project, order, last, paired),
            grid=(1,),
            in_specs=[
                smem_spec,
                vmem_spec,
                vmem_spec,
                pl.BlockSpec(
                    (cols, size, width, 2 * TILE),
                    functools.partial(lambda s, i: (0, s, 0, 0), begins[stage] // size),
                ),
                any_spec,
                any_spec,
            ]
            + [any_spec] * cols
            + [vmem_spec] * paired,
            out_specs=[vmem_spec, vmem_spec],
            out_shape=[
                jax.ShapeDtypeStruct((width, columns), BF),
                jax.ShapeDtypeStruct(
                    (width, (size + paired) * TILE // 2) if last else (full, columns), BF
                ),
            ],
            scratch_shapes=[
                pltpu.VMEM((full, columns), BF),
                pltpu.VMEM((full, columns), BF),
                pltpu.VMEM((full, full), BF),
                pltpu.VMEM((width, 4 * full), BF),
                pltpu.SemaphoreType.DMA((cols,)),
                pltpu.SemaphoreType.DMA((cols,)),
                pltpu.SemaphoreType.DMA((1,)),
            ],
            compiler_params=params(32),
            cost_estimate=cost((4 + 4 * size) * 1e9, 1e5),
            name="project",
        )(col_value, perm, gain, residual, out_weight_t, merge_weight, *gathers[stage], *before)
        layers.append(layer)
        parts.append(part)

    for stage in range(stages):
        if 2 <= stage + 1 < stages:
            send_chunk(stage + 1, (lefts[stage - 1], rights[stage - 1]))
        size, near = plan[stage], begins[stage]
        left, right = lefts[stage], rights[stage]
        if stage:
            left, right, _ = lax.optimization_barrier((left, right, gathers[stage - 1][0]))
        for at in range(size):
            left_tile, right_tile = far_tiles - 1 - near - at, far_tiles + own_tiles + near + at
            left_at, right_at = size - 1 - at, at
            new = pl.pallas_call(
                functools.partial(prepare_halo, images, depth),
                grid=(1,),
                in_specs=[
                    label_spec(left_tile),
                    label_spec(right_tile),
                    pl.BlockSpec((2, width, TILE), functools.partial(lambda t, i: (0, 0, t), left_at)),
                    pl.BlockSpec((2, width, TILE), functools.partial(lambda t, i: (0, 0, t), right_at)),
                ],
                out_specs=[
                    pl.BlockSpec((1,) + kt_shape, lambda i: (0, 0, 0, 0)),
                    pl.BlockSpec((1,) + v_shape, lambda i: (0, 0, 0, 0)),
                ]
                * 2,
                out_shape=[
                    jax.ShapeDtypeStruct((1,) + kt_shape, BF),
                    jax.ShapeDtypeStruct((1,) + v_shape, BF),
                ]
                * 2,
                compiler_params=params(16),
                cost_estimate=cost(5e8, 1e5),
                name="prepare_halo",
            )(labels, labels, left, right)
            halo[left_tile] = new[:2]
            halo[right_tile] = new[2:]

        operands = sorted(halo)
        own = list(range(far_tiles, far_tiles + own_tiles))
        base_tile = operands[0]
        tiles = own_tiles + len(operands)
        kts = [kt_own] + [halo[tile][0] for tile in operands]
        vs = [v_own] + [halo[tile][1] for tile in operands]
        queries = [pair_tile(block, which) for block in range(near, near + size) for which in range(2)]
        q_spec = lambda tile: pl.BlockSpec((1, heads, depth, TILE), lambda i: (tile, 0, 0, 0))
        after = [out_weight_t] if stage < 2 else [layers[stage - 2]]
        attended = pl.pallas_call(
            functools.partial(
                attend,
                own,
                {tile: 1 + at for at, tile in enumerate(operands)},
                base_tile,
                rate,
                queries,
            ),
            grid=(1,),
            in_specs=[smem_spec, vmem_spec]
            + [q_spec(tile) for tile in queries]
            + [any_spec] * (2 * len(kts) + len(after)),
            out_specs=vmem_spec,
            out_shape=jax.ShapeDtypeStruct((width, 2 * size * TILE), BF),
            scratch_shapes=[
                pltpu.VMEM((tiles,) + kt_shape, BF),
                pltpu.VMEM((tiles,) + v_shape, BF),
                pltpu.VMEM((2 * far_tiles + 1, heads, TILE, TILE), F32),
                pltpu.VMEM((heads, HEAD_DIM + 8, TILE), F32),
                pltpu.VMEM((heads, 8, TILE), F32),
                pltpu.VMEM((width, 2 * size * TILE), BF),
                pltpu.SemaphoreType.DMA((len(kts),)),
                pltpu.SemaphoreType.DMA((len(kts),)),
            ],
            compiler_params=params(32),
            cost_estimate=cost((5 + 4 * size) * 1e9, 1e5),
            name="attend",
        )(key_bounds, perm, *([q_tiles] * len(queries)), *kts, *vs, *after)

        gathers.append([attended])
        spread_pieces(stage, bits[:1], None)
        if stage == 1:
            spread_pieces(0, bits[1:], attended)
        if stage >= 1:
            run_project(stage - 1)
            spread_pieces(stage, bits[1:], layers[stage - 1])
    run_project(stages - 1)

    tiles_out = [None] * own_tiles
    for stage in range(stages):
        for block in range(plan[stage]):
            for which in range(2):
                lane = (2 * block + which) * TILE
                tile = pair_tile(begins[stage] + block, which)
                tiles_out[tile] = layers[stage][:, lane : lane + TILE]
    layer_out = jnp.concatenate(tiles_out, axis=1)

    groups = tokens // 4
    share = groups // rows
    piece_groups = TILE // 4
    owner = dest_row // groups
    place = dest_row % groups
    index = jnp.arange(groups, dtype=jnp.int32)
    rank = jnp.sum(
        ((owner[:, None] == owner[None, :]) & (index[None, :] < index[:, None])).astype(jnp.int32),
        axis=1,
    )
    base = 32
    away = (owner - row_id) % rows
    info = jnp.stack([away * share + rank, place // base, place % base])
    info = info.reshape(3, own_tiles, piece_groups)
    halves = 2
    info = jnp.stack(
        [
            jnp.concatenate(
                [
                    info[:, pair_tile(block, which)]
                    for block in range(h * blocks // 2, (h + 1) * blocks // 2)
                    for which in range(2)
                ],
                axis=1,
            )
            for h in range(halves)
        ],
        axis=1,
    )
    slots = info[0][:, None, :]
    wide = round_up(width + 2, 128)
    places = jnp.concatenate(
        [
            jnp.stack([info[1], info[2]], axis=1).astype(BF),
            jnp.zeros((halves, wide - width - 2, 4 * piece_groups), BF),
        ],
        axis=1,
    )
    sent = pl.pallas_call(
        functools.partial(outgoing, rows),
        out_shape=[jax.ShapeDtypeStruct((share, wide), BF)] * rows,
        compiler_params=params(16),
        cost_estimate=cost(1e9, 1e5),
        name="outgoing",
    )(slots, places, parts[0], parts[-1])
    received = [sent[0]] + [
        lax.ppermute(sent[step], "row", [(i, (i + step) % rows) for i in range(rows)])
        for step in range(1, rows)
    ]
    image_rows = pl.pallas_call(
        functools.partial(incoming, width, base),
        out_shape=jax.ShapeDtypeStruct((width, groups), BF),
        compiler_params=params(16),
        cost_estimate=cost(1e9, 1e5),
        name="incoming",
    )(*received)
    return (layer_out, image_rows)


def solution(mesh):
    return jax.shard_map(
        body,
        mesh=mesh,
        in_specs=(P(None, "col", "row"), P("col", "row"), P(), P("col", None), P(), P(), P("row")),
        out_specs=(P("col", "row"), P("col", "row")),
        check_vma=False,
    )
```

```python
import functools
import math

import jax
import jax.numpy as jnp
from jax import lax
from jax.experimental import pallas as pl
from jax.experimental.pallas import tpu as pltpu
from jax.sharding import PartitionSpec as P

HEAD_DIM = 88
TILE = 256
FAR = -1e30
BF = jnp.bfloat16
F32 = jnp.float32


def params(mib):
    return pltpu.CompilerParams(vmem_limit_bytes=mib * 1024 * 1024)


def cost(flops, bytes_accessed):
    return pl.CostEstimate(flops=int(flops), bytes_accessed=int(bytes_accessed), transcendentals=0)


def round_up(value, unit):
    return -(-value // unit) * unit


def key_tile(keys, label, images, depth, kt_ref):
    heads = keys.shape[0] // HEAD_DIM
    tail = depth - HEAD_DIM
    at = lax.broadcasted_iota(jnp.int32, (tail, TILE), 0)
    mask = jnp.where((at == label) | (at >= images), 0.0, FAR)
    for head in range(heads):
        whole = jnp.concatenate([keys[head * HEAD_DIM : (head + 1) * HEAD_DIM], mask], axis=0)
        kt_ref[0, head] = jnp.transpose(whole).astype(BF)


def value_tile(values, v_ref):
    heads = values.shape[0] // HEAD_DIM
    ones = jnp.where(lax.broadcasted_iota(jnp.int32, (8, TILE), 0) == 0, 1.0, 0.0)
    for head in range(heads):
        v_ref[0, head] = jnp.concatenate(
            [values[head * HEAD_DIM : (head + 1) * HEAD_DIM], ones], axis=0
        ).astype(BF)


def prepare_own(images, depth, label_ref, qkv_ref, q_ref, kt_ref, v_ref):
    label = label_ref[0]
    queries = qkv_ref[0].astype(F32)
    heads = queries.shape[0] // HEAD_DIM
    at = lax.broadcasted_iota(jnp.int32, (depth - HEAD_DIM, TILE), 0)
    mark = jnp.where(at == label, 1.0, 0.0)
    for head in range(heads):
        q_ref[0, head] = jnp.concatenate(
            [queries[head * HEAD_DIM : (head + 1) * HEAD_DIM], mark], axis=0
        ).astype(BF)
    key_tile(qkv_ref[1].astype(F32), label, images, depth, kt_ref)
    value_tile(qkv_ref[2].astype(F32), v_ref)


def reorder_residual(perm_ref, low_ref, high_ref, out_ref):
    both = jnp.concatenate([low_ref[...], high_ref[...]], axis=1)
    out_ref[0] = jnp.dot(both, perm_ref[...], preferred_element_type=F32).astype(BF)


def attend(own, halos, images, base, rate, q_tiles, bounds, label_ref, perm_ref, *refs):
    count = len(halos)
    q_refs, refs = refs[: len(q_tiles)], refs[len(q_tiles) :]
    kt_ref, v_ref, chunk_refs = refs[0], refs[1], refs[2 : 2 + count]
    refs = refs[-(9 + count) :]
    out_ref, kt_s, v_s, scores_s, acc, top, att = refs[:7]
    raw_s, sems, own_sems = refs[7 : 7 + count], refs[-2], refs[-1]
    heads = q_refs[0].shape[1]
    depth = kt_s.shape[3]
    slots = pl.ds(own[0] - base, len(own))
    chunk_copies = [
        pltpu.make_async_copy(chunk_ref, raw, sems.at[at])
        for at, (chunk_ref, raw) in enumerate(zip(chunk_refs, raw_s))
    ]
    kt_copy = pltpu.make_async_copy(kt_ref, kt_s.at[slots], own_sems.at[0])
    v_copy = pltpu.make_async_copy(v_ref, v_s.at[slots], own_sems.at[1])
    for copy in chunk_copies + [kt_copy, v_copy]:
        copy.start()
    for tiles, copy, raw in zip(halos, chunk_copies, raw_s):
        copy.wait()
        for at, tile in enumerate(tiles):
            lanes = slice(at * TILE, (at + 1) * TILE)
            slot = pl.ds(tile - base, 1)
            key_tile(raw[0, :, lanes].astype(F32), label_ref[tile], images, depth, kt_s.at[slot])
            value_tile(raw[1, :, lanes].astype(F32), v_s.at[slot])
    kt_copy.wait()
    for side, q_ref in enumerate(q_refs):
        begin, end = bounds[0, q_tiles[side]], bounds[1, q_tiles[side]]
        acc[...] = jnp.zeros_like(acc)
        top[...] = jnp.full_like(top, FAR)

        def sweep(step):
            pairs = (end - begin) // 2

            def pair(index, carry):
                step(begin + 2 * index, 2)
                return carry

            def single(index, carry):
                step(end - 1, 1)
                return carry

            lax.fori_loop(0, pairs, pair, 0)
            lax.fori_loop(0, end - begin - 2 * pairs, single, 0)

        def score(tile, span):
            for head in range(heads):
                keys = kt_s[pl.ds(tile - base, span), head].reshape(span * TILE, -1)
                scores = jnp.dot(keys, q_ref[0, head], preferred_element_type=F32)
                scores_s[pl.ds(tile - begin, span), head] = scores.reshape(span, TILE, TILE)
                highest = jnp.max(scores.reshape(span * TILE // 8, 8, TILE), axis=0)
                top[head] = jnp.maximum(top[head], highest)

        sweep(score)
        if side == 0:
            v_copy.wait()
        tops = [jnp.max(top[head], axis=0, keepdims=True) for head in range(heads)]
        for head in range(heads):
            top[head, 0:1] = tops[head]

        def weigh(tile, span):
            for head in range(heads):
                scores = scores_s[pl.ds(tile - begin, span), head].reshape(span * TILE, TILE)
                weights = jnp.exp2((scores - top[head, 0:1]) * rate).astype(BF)
                values = [v_s[tile - base + at, head] for at in range(span)]
                values = values[0] if span == 1 else jnp.concatenate(values, axis=1)
                acc[head] += jnp.dot(values, weights, preferred_element_type=F32)

        sweep(weigh)
        whole = jnp.concatenate(
            [acc[head, :HEAD_DIM] / acc[head, HEAD_DIM : HEAD_DIM + 1] for head in range(heads)], axis=0
        )
        att[:, side * TILE : (side + 1) * TILE] = whole.astype(BF)
        if side % 2:
            lanes = slice((side - 1) * TILE, (side + 1) * TILE)
            out_ref[:, lanes] = jnp.dot(
                att[:, lanes], perm_ref[...], preferred_element_type=F32
            ).astype(BF)


def project(order, last, paired, col_ref, perm_ref, gain_ref, res_ref, wt_ref, mw_ref, *refs):
    count = len(order)
    att_refs, refs = refs[:count], refs[count:]
    if paired:
        before_ref = refs[0]
    refs = refs[-9:]
    layer_ref, out_ref, gathered, layer_s, wt_s, mw_s, att_sem, wt_sem, mw_sem = refs
    width = att_refs[0].shape[0]
    full = wt_ref.shape[0]
    block = 2 * TILE
    blocks = layer_s.shape[1] // block
    groups = block // 4
    col = col_ref[0]
    att_copies, wt_copies = [], []
    for part, (bit, att_ref) in enumerate(zip(order, att_refs)):
        row = pl.multiple_of((col ^ bit) * width, 16)
        att_copies.append(
            pltpu.make_async_copy(att_ref, gathered.at[pl.ds(row, width), :], att_sem.at[part])
        )
        rows = pl.ds(part * width, width)
        wt_copies.append(
            pltpu.make_async_copy(wt_ref.at[rows, :], wt_s.at[rows, :], wt_sem.at[part])
        )
    mw_copy = pltpu.make_async_copy(mw_ref, mw_s, mw_sem.at[0])
    for copy in att_copies + wt_copies + [mw_copy] * last:
        copy.start()
    for copy in att_copies:
        copy.wait()
    for part in range(count):
        rows = slice(part * width, (part + 1) * width)
        wt_copies[part].wait()
        for at in range(blocks):
            lanes = slice(at * block, (at + 1) * block)
            projected = jnp.dot(wt_s[rows, :], gathered[:, lanes], preferred_element_type=F32)
            layer_s[rows, lanes] = (res_ref[part, at].astype(F32) + projected).astype(BF)
    own = pl.ds(pl.multiple_of(col * width, 16), width)
    for at in range(blocks):
        lanes = slice(at * block, (at + 1) * block)
        layer_ref[:, lanes] = lax.dot_general(
            layer_s[own, lanes], perm_ref[...], (((1,), (1,)), ((), ())), preferred_element_type=F32
        ).astype(BF)
    if last:
        mw_copy.wait()
    merged = None
    for j in range(4):
        columns = []
        for at in range(blocks):
            lanes = slice(at * block + j * groups, at * block + (j + 1) * groups)
            values = layer_s[:, lanes].astype(F32)
            values = values - jnp.sum(values, axis=0, keepdims=True) / full
            spread = jnp.sum(jnp.square(values), axis=0, keepdims=True) / full
            normed = (values * lax.rsqrt(spread + 1e-06) * gain_ref[...]).astype(BF)
            if last:
                columns.append(normed)
            else:
                out_ref[:, lanes] = normed
        if last:
            if paired:
                columns = [before_ref[:, j * groups : (j + 1) * groups]] + columns
            both = jnp.concatenate(columns, axis=1)
            term = jnp.dot(mw_s[:, j * full : (j + 1) * full], both, preferred_element_type=F32)
            merged = term if merged is None else merged + term
    if last:
        out_ref[...] = merged.astype(BF)


def outgoing(pieces, slot_ref, place_ref, *refs):
    merged_refs, out_refs = refs[:-pieces], refs[-pieces:]
    total = None
    share, wide = out_refs[0].shape
    for part, merged_ref in enumerate(merged_refs):
        groups = merged_ref.shape[1]
        row = lax.broadcasted_iota(jnp.int32, (share * pieces, groups), 0)
        pick = jnp.where(row == slot_ref[part], 1.0, 0.0).astype(BF)
        rows = jnp.concatenate([merged_ref[...], place_ref[part]], axis=0)
        term = lax.dot_general(pick, rows, (((1,), (1,)), ((), ())), preferred_element_type=F32)
        total = term if total is None else total + term
    for piece, out_ref in enumerate(out_refs):
        out_ref[...] = total[piece * share : (piece + 1) * share].astype(BF)


def incoming(width, base, *refs):
    in_refs, out_ref = refs[:-1], refs[-1]
    rows = jnp.concatenate([in_ref[...] for in_ref in in_refs], axis=0)
    place = rows[:, width : width + 2].astype(F32)
    target = (place[:, 0:1] * base + place[:, 1:2]).astype(jnp.int32)
    slots = rows.shape[0]
    lane = lax.broadcasted_iota(jnp.int32, (slots, slots), 1)
    pick = jnp.where(lane == target, 1.0, 0.0).astype(BF)
    out_ref[...] = lax.dot_general(
        rows[:, :width], pick, (((0,), (0,)), ((), ())), preferred_element_type=F32
    ).astype(BF)


def body(qkv, residual_in, out_weight, merge_weight, merge_gain, image_groups, dest_row):
    width = qkv.shape[1]
    tokens = qkv.shape[2]
    heads = width // HEAD_DIM
    full = out_weight.shape[0]
    images = image_groups.shape[0]
    reach = tokens // 2
    own_tiles = tokens // TILE
    far_tiles = reach // TILE
    half = own_tiles // 2
    plan = [half // 2] + [1] * (half - half // 2)
    begins = [sum(plan[:s]) for s in range(len(plan))]
    stages = len(plan)
    depth = round_up(HEAD_DIM + images, 128)
    rate = math.log2(math.e) / math.sqrt(HEAD_DIM)
    rows, cols = lax.axis_size("row"), lax.axis_size("col")
    row_id, col_id = lax.axis_index("row"), lax.axis_index("col")
    forward = [(i, (i + 1) % rows) for i in range(rows)]
    backward = [((i + 1) % rows, i) for i in range(rows)]

    lefts, rights = [], []

    def send_chunk(stage, after):
        source = qkv
        if after is not None:
            source, _ = lax.optimization_barrier((qkv, after))
        near, far = begins[stage] * TILE, (begins[stage] + plan[stage]) * TILE
        tail = lax.slice(source, (1, 0, tokens - far), (3, width, tokens - near))
        head = lax.slice(source, (1, 0, near), (3, width, far))
        lefts.append(lax.ppermute(tail, "row", forward))
        rights.append(lax.ppermute(head, "row", backward))
        return tail, head

    first_chunk = send_chunk(0, None)

    image_ends = jnp.cumsum(image_groups) * 4
    window_tiles = own_tiles + 2 * far_tiles
    positions = row_id * tokens - reach + jnp.arange(window_tiles * TILE, dtype=jnp.int32)
    labels = jnp.sum((positions[:, None] >= image_ends[None, :]).astype(jnp.int32), axis=1)
    labels = jnp.where(positions >= 0, labels, -1).reshape(window_tiles, 1, TILE)
    starts = row_id * tokens + jnp.arange(own_tiles, dtype=jnp.int32) * TILE
    ends = starts + TILE - 1
    low = jnp.max(jnp.where(image_ends[None, :] <= starts[:, None], image_ends[None, :], 0), axis=1)
    high = jnp.min(
        jnp.where(image_ends[None, :] > ends[:, None], image_ends[None, :], rows * tokens), axis=1
    )
    window_start = row_id * tokens - reach
    low = (low - window_start) // TILE
    high = (high - window_start + TILE - 1) // TILE
    tile_at = jnp.arange(own_tiles, dtype=jnp.int32)
    low = jnp.maximum(low, tile_at)
    high = jnp.minimum(high, tile_at + 2 * far_tiles + 1)

    inner = plan[0]

    def pair_tile(block, which):
        near = half - inner + 2 * block + which
        mirrored = half + block if which else half - 1 - block
        if isinstance(block, int):
            return near if block < inner else mirrored
        return jnp.where(block < inner, near, mirrored)

    at = jnp.arange(2 * TILE, dtype=jnp.int32)
    perm = (((at % 4) * (TILE // 2) + at // 4)[:, None] == at[None, :]).astype(BF)

    qkv_after, _ = lax.optimization_barrier((qkv, first_chunk))
    kt_shape, v_shape = (heads, TILE, depth), (heads, HEAD_DIM + 8, TILE)
    q_tiles, kt_own, v_own = pl.pallas_call(
        functools.partial(prepare_own, images, depth),
        grid=(own_tiles,),
        in_specs=[
            pl.BlockSpec((1, 1, TILE), lambda i: (i + far_tiles, 0, 0)),
            pl.BlockSpec((3, width, TILE), lambda i: (0, 0, i)),
        ],
        out_specs=[
            pl.BlockSpec((1, heads, depth, TILE), lambda i: (i, 0, 0, 0)),
            pl.BlockSpec((1,) + kt_shape, lambda i: (i, 0, 0, 0)),
            pl.BlockSpec((1,) + v_shape, lambda i: (i, 0, 0, 0)),
        ],
        out_shape=[
            jax.ShapeDtypeStruct((own_tiles, heads, depth, TILE), BF),
            jax.ShapeDtypeStruct((own_tiles,) + kt_shape, BF),
            jax.ShapeDtypeStruct((own_tiles,) + v_shape, BF),
        ],
        compiler_params=params(16),
        cost_estimate=cost(2e9, 1e5),
        name="prepare_own",
    )(labels, qkv_after)

    residual_in, _ = lax.optimization_barrier((residual_in, first_chunk))
    blocks = own_tiles // 2
    residual = pl.pallas_call(
        reorder_residual,
        grid=(blocks,),
        in_specs=[
            pl.BlockSpec((2 * TILE, 2 * TILE), lambda i: (0, 0)),
            pl.BlockSpec((width, TILE), lambda i: (0, pair_tile(i, 0))),
            pl.BlockSpec((width, TILE), lambda i: (0, pair_tile(i, 1))),
        ],
        out_specs=pl.BlockSpec((1, width, 2 * TILE), lambda i: (i, 0, 0)),
        out_shape=jax.ShapeDtypeStruct((blocks, width, 2 * TILE), BF),
        compiler_params=params(16),
        cost_estimate=cost(2e9, 1e5),
        name="reorder_residual",
    )(perm, residual_in, residual_in)
    residual = lax.all_gather(residual, "col", axis=0)
    out_weight_t = jnp.transpose(out_weight)
    key_bounds = jnp.stack([low, high])
    gain = merge_gain[:, None]
    bits = []
    span = cols // 2
    while span:
        bits.append(span)
        span //= 2
    order = [0]
    for bit in bits:
        order = order + [bit ^ other for other in order]
    col_value = col_id.astype(jnp.int32).reshape(1)

    layers, parts, gathers = [], [], []
    any_spec = pl.BlockSpec(memory_space=pl.ANY)
    smem_spec = pl.BlockSpec(memory_space=pltpu.SMEM)
    vmem_spec = pl.BlockSpec(memory_space=pltpu.VMEM)
    def spread_pieces(stage, some_bits, after):
        pieces = gathers[stage]
        for bit in some_bits:
            pairs = [(i, i ^ bit) for i in range(cols)]
            sources = pieces
            if after is not None:
                sources, _ = lax.optimization_barrier((pieces, after))
            pieces = pieces + [lax.ppermute(piece, "col", pairs) for piece in sources]
        gathers[stage] = pieces

    def run_project(stage):
        size = plan[stage]
        paired = stage == stages - 1 and stages - 1 > 1
        last = stage == 0 or stage == stages - 1
        before = [parts[stage - 1]] if paired else []
        columns = 2 * size * TILE
        after = [gathers[-1][0]] if stage == 0 else [layers[stage - 1]]
        layer, part = pl.pallas_call(
            functools.partial(project, order, last, paired),
            grid=(1,),
            in_specs=[
                smem_spec,
                vmem_spec,
                vmem_spec,
                pl.BlockSpec(
                    (cols, size, width, 2 * TILE),
                    functools.partial(lambda s, i: (0, s, 0, 0), begins[stage] // size),
                ),
                any_spec,
                any_spec,
            ]
            + [any_spec] * cols
            + [vmem_spec] * paired
            + [any_spec] * len(after),
            out_specs=[vmem_spec, vmem_spec],
            out_shape=[
                jax.ShapeDtypeStruct((width, columns), BF),
                jax.ShapeDtypeStruct(
                    (width, (size + paired) * TILE // 2) if last else (full, columns), BF
                ),
            ],
            scratch_shapes=[
                pltpu.VMEM((full, columns), BF),
                pltpu.VMEM((full, columns), BF),
                pltpu.VMEM((full, full), BF),
                pltpu.VMEM((width, 4 * full), BF),
                pltpu.SemaphoreType.DMA((cols,)),
                pltpu.SemaphoreType.DMA((cols,)),
                pltpu.SemaphoreType.DMA((1,)),
            ],
            compiler_params=params(62),
            cost_estimate=cost((4 + 4 * size) * 1e9, 1e5),
            name="project",
        )(col_value, perm, gain, residual, out_weight_t, merge_weight, *gathers[stage], *before, *after)
        layers.append(layer)
        parts.append(part)

    for stage in range(stages):
        if stage + 1 < stages:
            send_chunk(stage + 1, (lefts[stage], rights[stage]))
        size, near = plan[stage], begins[stage]
        own = list(range(far_tiles, far_tiles + own_tiles))
        base_tile = far_tiles - near - size
        tiles = own_tiles + 2 * (near + size)
        halos, chunks = [], []
        for before in range(stage + 1):
            inner_edge, outer_edge = begins[before], begins[before] + plan[before]
            halos.append(list(range(far_tiles - outer_edge, far_tiles - inner_edge)))
            halos.append([far_tiles + own_tiles + at for at in range(inner_edge, outer_edge)])
            chunks += [lefts[before], rights[before]]
        queries = [pair_tile(block, which) for block in range(near, near + size) for which in range(2)]
        q_spec = lambda tile: pl.BlockSpec((1, heads, depth, TILE), lambda i: (tile, 0, 0, 0))
        after = [out_weight_t] if stage == 0 else [gathers[stage - 1][0]]
        attended = pl.pallas_call(
            functools.partial(attend, own, halos, images, base_tile, rate, queries),
            grid=(1,),
            in_specs=[smem_spec, vmem_spec, vmem_spec]
            + [q_spec(tile) for tile in queries]
            + [any_spec] * (2 + len(chunks) + len(after)),
            out_specs=vmem_spec,
            out_shape=jax.ShapeDtypeStruct((width, 2 * size * TILE), BF),
            scratch_shapes=[
                pltpu.VMEM((tiles,) + kt_shape, BF),
                pltpu.VMEM((tiles,) + v_shape, BF),
                pltpu.VMEM((2 * far_tiles + 1, heads, TILE, TILE), F32),
                pltpu.VMEM((heads, HEAD_DIM + 8, TILE), F32),
                pltpu.VMEM((heads, 8, TILE), F32),
                pltpu.VMEM((width, 2 * size * TILE), BF),
            ]
            + [pltpu.VMEM(chunk.shape, BF) for chunk in chunks]
            + [pltpu.SemaphoreType.DMA((len(chunks),)), pltpu.SemaphoreType.DMA((2,))],
            compiler_params=params(62),
            cost_estimate=cost((5 + 4 * size) * 1e9, 1e5),
            name="attend",
        )(key_bounds, labels, perm, *([q_tiles] * len(queries)), kt_own, v_own, *chunks, *after)

        gathers.append([attended])
        spread_pieces(stage, bits[:1], None)
        if stage >= 1:
            spread_pieces(stage - 1, bits[1:], attended)
    for stage in range(stages):
        if stage == 1:
            spread_pieces(stages - 1, bits[1:], layers[0])
        run_project(stage)

    tiles_out = [None] * own_tiles
    for stage in range(stages):
        for block in range(plan[stage]):
            for which in range(2):
                lane = (2 * block + which) * TILE
                tile = pair_tile(begins[stage] + block, which)
                tiles_out[tile] = layers[stage][:, lane : lane + TILE]
    layer_out = jnp.concatenate(tiles_out, axis=1)

    groups = tokens // 4
    share = groups // rows
    piece_groups = TILE // 4
    owner = dest_row // groups
    place = dest_row % groups
    index = jnp.arange(groups, dtype=jnp.int32)
    rank = jnp.sum(
        ((owner[:, None] == owner[None, :]) & (index[None, :] < index[:, None])).astype(jnp.int32),
        axis=1,
    )
    base = 32
    away = (owner - row_id) % rows
    info = jnp.stack([away * share + rank, place // base, place % base])
    info = info.reshape(3, own_tiles, piece_groups)
    halves = 2
    info = jnp.stack(
        [
            jnp.concatenate(
                [
                    info[:, pair_tile(block, which)]
                    for block in range(h * blocks // 2, (h + 1) * blocks // 2)
                    for which in range(2)
                ],
                axis=1,
            )
            for h in range(halves)
        ],
        axis=1,
    )
    slots = info[0][:, None, :]
    wide = round_up(width + 2, 128)
    places = jnp.concatenate(
        [
            jnp.stack([info[1], info[2]], axis=1).astype(BF),
            jnp.zeros((halves, wide - width - 2, 4 * piece_groups), BF),
        ],
        axis=1,
    )
    sent = pl.pallas_call(
        functools.partial(outgoing, rows),
        out_shape=[jax.ShapeDtypeStruct((share, wide), BF)] * rows,
        compiler_params=params(16),
        cost_estimate=cost(1e9, 1e5),
        name="outgoing",
    )(slots, places, parts[0], parts[-1])
    received = [sent[0]] + [
        lax.ppermute(sent[step], "row", [(i, (i + step) % rows) for i in range(rows)])
        for step in range(1, rows)
    ]
    image_rows = pl.pallas_call(
        functools.partial(incoming, width, base),
        out_shape=jax.ShapeDtypeStruct((width, groups), BF),
        compiler_params=params(16),
        cost_estimate=cost(1e9, 1e5),
        name="incoming",
    )(*received)
    return (layer_out, image_rows)


def solution(mesh):
    return jax.shard_map(
        body,
        mesh=mesh,
        in_specs=(P(None, "col", "row"), P("col", "row"), P(), P("col", None), P(), P(), P("row")),
        out_specs=(P("col", "row"), P("col", "row")),
        check_vma=False,
    )
```

```python
import functools
import math

import jax
import jax.numpy as jnp
from jax import lax
from jax.experimental import pallas as pl
from jax.experimental.pallas import tpu as pltpu
from jax.sharding import PartitionSpec as P

HEAD_DIM = 88
TILE = 256
FAR = -1e30
BF = jnp.bfloat16
F32 = jnp.float32


def params(mib):
    return pltpu.CompilerParams(vmem_limit_bytes=mib * 1024 * 1024)


def cost(flops, bytes_accessed):
    return pl.CostEstimate(flops=int(flops), bytes_accessed=int(bytes_accessed), transcendentals=0)


def round_up(value, unit):
    return -(-value // unit) * unit


def key_tile(keys, label, images, depth, kt_ref):
    heads = keys.shape[0] // HEAD_DIM
    tail = depth - HEAD_DIM
    at = lax.broadcasted_iota(jnp.int32, (tail, TILE), 0)
    mask = jnp.where((at == label) | (at >= images), 0.0, FAR)
    for head in range(heads):
        whole = jnp.concatenate([keys[head * HEAD_DIM : (head + 1) * HEAD_DIM], mask], axis=0)
        kt_ref[0, head] = jnp.transpose(whole).astype(BF)


def value_tile(values, v_ref):
    heads = values.shape[0] // HEAD_DIM
    ones = jnp.where(lax.broadcasted_iota(jnp.int32, (8, TILE), 0) == 0, 1.0, 0.0)
    for head in range(heads):
        v_ref[0, head] = jnp.concatenate(
            [values[head * HEAD_DIM : (head + 1) * HEAD_DIM], ones], axis=0
        ).astype(BF)


def prepare_own(images, depth, label_ref, qkv_ref, q_ref, kt_ref, v_ref):
    label = label_ref[0]
    queries = qkv_ref[0].astype(F32)
    heads = queries.shape[0] // HEAD_DIM
    at = lax.broadcasted_iota(jnp.int32, (depth - HEAD_DIM, TILE), 0)
    mark = jnp.where(at == label, 1.0, 0.0)
    for head in range(heads):
        q_ref[0, head] = jnp.concatenate(
            [queries[head * HEAD_DIM : (head + 1) * HEAD_DIM], mark], axis=0
        ).astype(BF)
    key_tile(qkv_ref[1].astype(F32), label, images, depth, kt_ref)
    value_tile(qkv_ref[2].astype(F32), v_ref)


def reorder_residual(perm_ref, low_ref, high_ref, out_ref):
    both = jnp.concatenate([low_ref[...], high_ref[...]], axis=1)
    out_ref[0] = jnp.dot(both, perm_ref[...], preferred_element_type=F32).astype(BF)


def attend(own, halos, images, base, rate, first_query, bounds, label_ref, perm_ref, *refs):
    count = len(halos)
    q_ref, kt_ref, v_ref, chunk_refs = refs[0], refs[1], refs[2], refs[3 : 3 + count]
    refs = refs[-(9 + count) :]
    out_ref, kt_s, v_s, scores_s, acc, top, att = refs[:7]
    raw_s, sems, own_sems = refs[7 : 7 + count], refs[-2], refs[-1]
    queries, heads = q_ref.shape[:2]
    depth = kt_s.shape[3]
    slots = pl.ds(own[0] - base, len(own))
    chunk_copies = [
        pltpu.make_async_copy(chunk_ref, raw, sems.at[at])
        for at, (chunk_ref, raw) in enumerate(zip(chunk_refs, raw_s))
    ]
    kt_copy = pltpu.make_async_copy(kt_ref, kt_s.at[slots], own_sems.at[0])
    v_copy = pltpu.make_async_copy(v_ref, v_s.at[slots], own_sems.at[1])
    for copy in chunk_copies + [kt_copy, v_copy]:
        copy.start()
    for tiles, copy, raw in zip(halos, chunk_copies, raw_s):
        copy.wait()
        for at, tile in enumerate(tiles):
            lanes = slice(at * TILE, (at + 1) * TILE)
            slot = pl.ds(tile - base, 1)
            key_tile(raw[0, :, lanes].astype(F32), label_ref[tile], images, depth, kt_s.at[slot])
            value_tile(raw[1, :, lanes].astype(F32), v_s.at[slot])
    kt_copy.wait()

    def attend_tile(side, carry):
        begin, end = bounds[0, first_query + side], bounds[1, first_query + side]
        acc[...] = jnp.zeros_like(acc)
        top[...] = jnp.full_like(top, FAR)

        def sweep(step):
            pairs = (end - begin) // 2

            def pair(index, carry):
                step(begin + 2 * index, 2)
                return carry

            def single(index, carry):
                step(end - 1, 1)
                return carry

            lax.fori_loop(0, pairs, pair, 0)
            lax.fori_loop(0, end - begin - 2 * pairs, single, 0)

        def score(tile, span):
            for head in range(heads):
                keys = kt_s[pl.ds(tile - base, span), head].reshape(span * TILE, -1)
                scores = jnp.dot(keys, q_ref[side, head], preferred_element_type=F32)
                scores_s[pl.ds(tile - begin, span), head] = scores.reshape(span, TILE, TILE)
                highest = jnp.max(scores.reshape(span * TILE // 8, 8, TILE), axis=0)
                top[head] = jnp.maximum(top[head], highest)

        sweep(score)

        @pl.when(side == 0)
        def _():
            v_copy.wait()

        tops = [jnp.max(top[head], axis=0, keepdims=True) for head in range(heads)]
        for head in range(heads):
            top[head, 0:1] = tops[head]

        def weigh(tile, span):
            for head in range(heads):
                scores = scores_s[pl.ds(tile - begin, span), head].reshape(span * TILE, TILE)
                weights = jnp.exp2((scores - top[head, 0:1]) * rate).astype(BF)
                values = [v_s[tile - base + at, head] for at in range(span)]
                values = values[0] if span == 1 else jnp.concatenate(values, axis=1)
                acc[head] += jnp.dot(values, weights, preferred_element_type=F32)

        sweep(weigh)
        whole = jnp.concatenate(
            [acc[head, :HEAD_DIM] / acc[head, HEAD_DIM : HEAD_DIM + 1] for head in range(heads)], axis=0
        )
        att[:, pl.ds(pl.multiple_of(side * TILE, TILE), TILE)] = whole.astype(BF)
        return carry

    lax.fori_loop(0, queries, attend_tile, 0)
    for at in range(queries // 2):
        lanes = slice(2 * at * TILE, 2 * (at + 1) * TILE)
        out_ref[:, lanes] = jnp.dot(
            att[:, lanes], perm_ref[...], preferred_element_type=F32
        ).astype(BF)


def project(order, last, col_ref, perm_ref, gain_ref, res_ref, wt_ref, mw_ref, *refs):
    count = len(order)
    att_refs, refs = refs[:count], refs[count:]
    if last:
        before_ref = refs[0]
    layer_ref, out_ref, gathered, layer_s, wt_s, mw_s, merged_s, att_sem, wt_sem, mw_sem = refs[-10:]
    width = att_refs[0].shape[0]
    full = wt_ref.shape[0]
    groups = layer_s.shape[1] // 4
    col = col_ref[0]

    def wt_copy(part):
        rows = pl.ds(pl.multiple_of(part * width, 16), width)
        return pltpu.make_async_copy(wt_ref.at[rows, :], wt_s.at[rows, :], wt_sem.at[part])

    att_copies = []
    for part, (bit, att_ref) in enumerate(zip(order, att_refs)):
        row = pl.multiple_of((col ^ bit) * width, 16)
        att_copies.append(
            pltpu.make_async_copy(att_ref, gathered.at[pl.ds(row, width), :], att_sem.at[part])
        )
    mw_copy = pltpu.make_async_copy(mw_ref, mw_s, mw_sem.at[0])
    for copy in att_copies + [wt_copy(part) for part in range(count)] + [mw_copy] * last:
        copy.start()
    for copy in att_copies:
        copy.wait()

    def project_part(part, carry):
        rows = pl.ds(pl.multiple_of(part * width, 16), width)
        wt_copy(part).wait()
        projected = jnp.dot(wt_s[rows, :], gathered[...], preferred_element_type=F32)
        layer_s[rows, :] = (res_ref[part, 0].astype(F32) + projected).astype(BF)
        return carry

    lax.fori_loop(0, count, project_part, 0)
    own = pl.ds(pl.multiple_of(col * width, 16), width)
    layer_ref[...] = lax.dot_general(
        layer_s[own, :], perm_ref[...], (((1,), (1,)), ((), ())), preferred_element_type=F32
    ).astype(BF)
    if last:
        mw_copy.wait()
        merged_s[...] = jnp.zeros_like(merged_s)

    def merge_part(j, carry):
        lanes = pl.ds(pl.multiple_of(j * groups, groups), groups)
        values = layer_s[:, lanes].astype(F32)
        values = values - jnp.sum(values, axis=0, keepdims=True) / full
        spread = jnp.sum(jnp.square(values), axis=0, keepdims=True) / full
        normed = (values * lax.rsqrt(spread + 1e-06) * gain_ref[...]).astype(BF)
        if last:
            both = jnp.concatenate([before_ref[:, lanes], normed], axis=1)
            weights = mw_s[:, pl.ds(pl.multiple_of(j * full, 128), full)]
            merged_s[...] += jnp.dot(weights, both, preferred_element_type=F32)
        else:
            out_ref[:, lanes] = normed
        return carry

    lax.fori_loop(0, 4, merge_part, 0)
    if last:
        out_ref[...] = merged_s[...].astype(BF)


def outgoing(pieces, slot_ref, place_ref, *refs):
    merged_refs, out_refs = refs[:-pieces], refs[-pieces:]
    total = None
    share, wide = out_refs[0].shape
    for part, merged_ref in enumerate(merged_refs):
        groups = merged_ref.shape[1]
        row = lax.broadcasted_iota(jnp.int32, (share * pieces, groups), 0)
        pick = jnp.where(row == slot_ref[part], 1.0, 0.0).astype(BF)
        rows = jnp.concatenate([merged_ref[...], place_ref[part]], axis=0)
        term = lax.dot_general(pick, rows, (((1,), (1,)), ((), ())), preferred_element_type=F32)
        total = term if total is None else total + term
    for piece, out_ref in enumerate(out_refs):
        out_ref[...] = total[piece * share : (piece + 1) * share].astype(BF)


def incoming(width, base, *refs):
    in_refs, out_ref = refs[:-1], refs[-1]
    rows = jnp.concatenate([in_ref[...] for in_ref in in_refs], axis=0)
    place = rows[:, width : width + 2].astype(F32)
    target = (place[:, 0:1] * base + place[:, 1:2]).astype(jnp.int32)
    slots = rows.shape[0]
    lane = lax.broadcasted_iota(jnp.int32, (slots, slots), 1)
    pick = jnp.where(lane == target, 1.0, 0.0).astype(BF)
    out_ref[...] = lax.dot_general(
        rows[:, :width], pick, (((0,), (0,)), ((), ())), preferred_element_type=F32
    ).astype(BF)


def body(qkv, residual_in, out_weight, merge_weight, merge_gain, image_groups, dest_row):
    width = qkv.shape[1]
    tokens = qkv.shape[2]
    heads = width // HEAD_DIM
    full = out_weight.shape[0]
    images = image_groups.shape[0]
    reach = tokens // 2
    own_tiles = tokens // TILE
    far_tiles = reach // TILE
    half = own_tiles // 2
    plan = [1] * half
    begins = [sum(plan[:s]) for s in range(len(plan))]
    stages = len(plan)
    depth = round_up(HEAD_DIM + images, 128)
    rate = math.log2(math.e) / math.sqrt(HEAD_DIM)
    rows, cols = lax.axis_size("row"), lax.axis_size("col")
    row_id, col_id = lax.axis_index("row"), lax.axis_index("col")
    forward = [(i, (i + 1) % rows) for i in range(rows)]
    backward = [((i + 1) % rows, i) for i in range(rows)]

    lefts, rights = [], []

    def send_chunk(stage, after):
        source = qkv
        if after is not None:
            source, _ = lax.optimization_barrier((qkv, after))
        near, far = begins[stage] * TILE, (begins[stage] + plan[stage]) * TILE
        tail = lax.slice(source, (1, 0, tokens - far), (3, width, tokens - near))
        head = lax.slice(source, (1, 0, near), (3, width, far))
        lefts.append(lax.ppermute(tail, "row", forward))
        rights.append(lax.ppermute(head, "row", backward))
        return tail, head

    first_chunk = send_chunk(0, None)

    image_ends = jnp.cumsum(image_groups) * 4
    window_tiles = own_tiles + 2 * far_tiles
    positions = row_id * tokens - reach + jnp.arange(window_tiles * TILE, dtype=jnp.int32)
    labels = jnp.sum((positions[:, None] >= image_ends[None, :]).astype(jnp.int32), axis=1)
    labels = jnp.where(positions >= 0, labels, -1).reshape(window_tiles, 1, TILE)
    starts = row_id * tokens + jnp.arange(own_tiles, dtype=jnp.int32) * TILE
    ends = starts + TILE - 1
    low = jnp.max(jnp.where(image_ends[None, :] <= starts[:, None], image_ends[None, :], 0), axis=1)
    high = jnp.min(
        jnp.where(image_ends[None, :] > ends[:, None], image_ends[None, :], rows * tokens), axis=1
    )
    window_start = row_id * tokens - reach
    low = (low - window_start) // TILE
    high = (high - window_start + TILE - 1) // TILE
    tile_at = jnp.arange(own_tiles, dtype=jnp.int32)
    low = jnp.maximum(low, tile_at)
    high = jnp.minimum(high, tile_at + 2 * far_tiles + 1)

    inner = plan[0]

    def pair_tile(block, which):
        near = half - inner + 2 * block + which
        mirrored = half + block if which else half - 1 - block
        if isinstance(block, int):
            return near if block < inner else mirrored
        return jnp.where(block < inner, near, mirrored)

    def stage_order(tile):
        return jnp.where(tile >= half, 2 * (tile - half) + 1, 2 * (half - 1 - tile))

    at = jnp.arange(2 * TILE, dtype=jnp.int32)
    perm = (((at % 4) * (TILE // 2) + at // 4)[:, None] == at[None, :]).astype(BF)

    qkv_after, _ = lax.optimization_barrier((qkv, first_chunk))
    kt_shape, v_shape = (heads, TILE, depth), (heads, HEAD_DIM + 8, TILE)
    q_tiles, kt_own, v_own = pl.pallas_call(
        functools.partial(prepare_own, images, depth),
        grid=(own_tiles,),
        in_specs=[
            pl.BlockSpec((1, 1, TILE), lambda i: (i + far_tiles, 0, 0)),
            pl.BlockSpec((3, width, TILE), lambda i: (0, 0, i)),
        ],
        out_specs=[
            pl.BlockSpec((1, heads, depth, TILE), lambda i: (stage_order(i), 0, 0, 0)),
            pl.BlockSpec((1,) + kt_shape, lambda i: (i, 0, 0, 0)),
            pl.BlockSpec((1,) + v_shape, lambda i: (i, 0, 0, 0)),
        ],
        out_shape=[
            jax.ShapeDtypeStruct((own_tiles, heads, depth, TILE), BF),
            jax.ShapeDtypeStruct((own_tiles,) + kt_shape, BF),
            jax.ShapeDtypeStruct((own_tiles,) + v_shape, BF),
        ],
        compiler_params=params(16),
        cost_estimate=cost(2e9, 1e5),
        name="prepare_own",
    )(labels, qkv_after)

    residual_in, _ = lax.optimization_barrier((residual_in, first_chunk))
    blocks = own_tiles // 2
    residual = pl.pallas_call(
        reorder_residual,
        grid=(blocks,),
        in_specs=[
            pl.BlockSpec((2 * TILE, 2 * TILE), lambda i: (0, 0)),
            pl.BlockSpec((width, TILE), lambda i: (0, pair_tile(i, 0))),
            pl.BlockSpec((width, TILE), lambda i: (0, pair_tile(i, 1))),
        ],
        out_specs=pl.BlockSpec((1, width, 2 * TILE), lambda i: (i, 0, 0)),
        out_shape=jax.ShapeDtypeStruct((blocks, width, 2 * TILE), BF),
        compiler_params=params(16),
        cost_estimate=cost(2e9, 1e5),
        name="reorder_residual",
    )(perm, residual_in, residual_in)
    residual = lax.all_gather(residual, "col", axis=0)
    tile_order = [pair_tile(block, which) for block in range(blocks) for which in range(2)]
    key_bounds = jnp.stack([low, high])
    key_bounds = jnp.stack([key_bounds[:, tile] for tile in tile_order], axis=1)
    gain = merge_gain[:, None]
    bits = []
    span = cols // 2
    while span:
        bits.append(span)
        span //= 2
    order = [0]
    for bit in bits:
        order = order + [bit ^ other for other in order]
    col_value = col_id.astype(jnp.int32).reshape(1)

    layers, parts, gathers = [], [], []
    any_spec = pl.BlockSpec(memory_space=pl.ANY)
    smem_spec = pl.BlockSpec(memory_space=pltpu.SMEM)
    vmem_spec = pl.BlockSpec(memory_space=pltpu.VMEM)
    def spread_pieces(stage, some_bits, after):
        pieces = gathers[stage]
        for bit in some_bits:
            pairs = [(i, i ^ bit) for i in range(cols)]
            sources = pieces
            if after is not None:
                sources, _ = lax.optimization_barrier((pieces, after))
            pieces = pieces + [lax.ppermute(piece, "col", pairs) for piece in sources]
        gathers[stage] = pieces

    def run_project(stage):
        size = plan[stage]
        last = stage % 2 == 1
        before = [parts[stage - 1]] if last else []
        columns = 2 * size * TILE
        after = [gathers[-1][0]] + layers[-1:]
        layer, part = pl.pallas_call(
            functools.partial(project, order, last),
            grid=(1,),
            in_specs=[
                smem_spec,
                vmem_spec,
                vmem_spec,
                pl.BlockSpec(
                    (cols, size, width, 2 * TILE),
                    functools.partial(lambda s, i: (0, s, 0, 0), begins[stage] // size),
                ),
                any_spec,
                any_spec,
            ]
            + [any_spec] * cols
            + [vmem_spec] * last
            + [any_spec] * len(after),
            out_specs=[vmem_spec, vmem_spec],
            out_shape=[
                jax.ShapeDtypeStruct((width, columns), BF),
                jax.ShapeDtypeStruct((width, TILE) if last else (full, columns), BF),
            ],
            scratch_shapes=[
                pltpu.VMEM((full, columns), BF),
                pltpu.VMEM((full, columns), BF),
                pltpu.VMEM((full, full), BF),
                pltpu.VMEM((width, 4 * full), BF),
                pltpu.VMEM((width, TILE), F32),
                pltpu.SemaphoreType.DMA((cols,)),
                pltpu.SemaphoreType.DMA((cols,)),
                pltpu.SemaphoreType.DMA((1,)),
            ],
            compiler_params=params(62),
            cost_estimate=cost((4 + 4 * size) * 1e9, 1e5),
            name="project",
        )(col_value, perm, gain, residual, out_weight_t, merge_weight, *gathers[stage], *before, *after)
        layers.append(layer)
        parts.append(part)

    for stage in range(stages):
        if stage + 1 < stages:
            send_chunk(stage + 1, (lefts[stage], rights[stage]))
        size, near = plan[stage], begins[stage]
        own = list(range(far_tiles, far_tiles + own_tiles))
        base_tile = far_tiles - near - size
        tiles = own_tiles + 2 * (near + size)
        halos, chunks = [], []
        for before in range(stage + 1):
            inner_edge, outer_edge = begins[before], begins[before] + plan[before]
            halos.append(list(range(far_tiles - outer_edge, far_tiles - inner_edge)))
            halos.append([far_tiles + own_tiles + at for at in range(inner_edge, outer_edge)])
            chunks += [lefts[before], rights[before]]
        after = [g[0] for g in gathers[-1:]] + layers[-1:]
        attended = pl.pallas_call(
            functools.partial(attend, own, halos, images, base_tile, rate, 2 * near),
            grid=(1,),
            in_specs=[
                smem_spec,
                vmem_spec,
                vmem_spec,
                pl.BlockSpec(
                    (2 * size, heads, depth, TILE),
                    functools.partial(lambda s, i: (s, 0, 0, 0), near // size),
                ),
            ]
            + [any_spec] * (2 + len(chunks) + len(after)),
            out_specs=vmem_spec,
            out_shape=jax.ShapeDtypeStruct((width, 2 * size * TILE), BF),
            scratch_shapes=[
                pltpu.VMEM((tiles,) + kt_shape, BF),
                pltpu.VMEM((tiles,) + v_shape, BF),
                pltpu.VMEM((2 * far_tiles + 1, heads, TILE, TILE), F32),
                pltpu.VMEM((heads, HEAD_DIM + 8, TILE), F32),
                pltpu.VMEM((heads, 8, TILE), F32),
                pltpu.VMEM((width, 2 * size * TILE), BF),
            ]
            + [pltpu.VMEM(chunk.shape, BF) for chunk in chunks]
            + [pltpu.SemaphoreType.DMA((len(chunks),)), pltpu.SemaphoreType.DMA((2,))],
            compiler_params=params(62),
            cost_estimate=cost((5 + 4 * size) * 1e9, 1e5),
            name="attend",
        )(key_bounds, labels, perm, q_tiles, kt_own, v_own, *chunks, *after)

        gathers.append([attended])
        spread_pieces(stage, bits[:1], None)
        if stage == 0:
            ready_weight, _ = lax.optimization_barrier((out_weight, attended))
            out_weight_t = jnp.transpose(ready_weight)
        if stage == 1:
            spread_pieces(0, bits[1:], attended)
        if stage >= 1:
            run_project(stage - 1)
            spread_pieces(stage, bits[1:], layers[stage - 1])
    run_project(stages - 1)

    tiles_out = [None] * own_tiles
    for stage in range(stages):
        for block in range(plan[stage]):
            for which in range(2):
                lane = (2 * block + which) * TILE
                tile = pair_tile(begins[stage] + block, which)
                tiles_out[tile] = layers[stage][:, lane : lane + TILE]
    layer_out = jnp.concatenate(tiles_out, axis=1)

    groups = tokens // 4
    share = groups // rows
    piece_groups = TILE // 4
    owner = dest_row // groups
    place = dest_row % groups
    index = jnp.arange(groups, dtype=jnp.int32)
    rank = jnp.sum(
        ((owner[:, None] == owner[None, :]) & (index[None, :] < index[:, None])).astype(jnp.int32),
        axis=1,
    )
    base = 32
    away = (owner - row_id) % rows
    info = jnp.stack([away * share + rank, place // base, place % base])
    info = info.reshape(3, own_tiles, piece_groups)
    halves = stages // 2
    info = jnp.stack(
        [
            jnp.concatenate(
                [
                    info[:, pair_tile(block, which)]
                    for block in (2 * h, 2 * h + 1)
                    for which in range(2)
                ],
                axis=1,
            )
            for h in range(halves)
        ],
        axis=1,
    )
    slots = info[0][:, None, :]
    wide = round_up(width + 2, 128)
    places = jnp.concatenate(
        [
            jnp.stack([info[1], info[2]], axis=1).astype(BF),
            jnp.zeros((halves, wide - width - 2, 4 * piece_groups), BF),
        ],
        axis=1,
    )
    sent = pl.pallas_call(
        functools.partial(outgoing, rows),
        out_shape=[jax.ShapeDtypeStruct((share, wide), BF)] * rows,
        compiler_params=params(16),
        cost_estimate=cost(1e9, 1e5),
        name="outgoing",
    )(slots, places, *parts[1::2])
    received = [sent[0]] + [
        lax.ppermute(sent[step], "row", [(i, (i + step) % rows) for i in range(rows)])
        for step in range(1, rows)
    ]
    image_rows = pl.pallas_call(
        functools.partial(incoming, width, base),
        out_shape=jax.ShapeDtypeStruct((width, groups), BF),
        compiler_params=params(16),
        cost_estimate=cost(1e9, 1e5),
        name="incoming",
    )(*received)
    return (layer_out, image_rows)


def solution(mesh):
    return jax.shard_map(
        body,
        mesh=mesh,
        in_specs=(P(None, "col", "row"), P("col", "row"), P(), P("col", None), P(), P(), P("row")),
        out_specs=(P("col", "row"), P("col", "row")),
        check_vma=False,
    )
```

```python
import functools
import math

import jax
import jax.numpy as jnp
from jax import lax
from jax.experimental import pallas as pl
from jax.experimental.pallas import tpu as pltpu
from jax.sharding import PartitionSpec as P

HEAD_DIM = 88
TILE = 256
FAR = -1e30
BF = jnp.bfloat16
F32 = jnp.float32


def params(mib):
    return pltpu.CompilerParams(vmem_limit_bytes=mib * 1024 * 1024)


def cost(flops, bytes_accessed):
    return pl.CostEstimate(flops=int(flops), bytes_accessed=int(bytes_accessed), transcendentals=0)


def round_up(value, unit):
    return -(-value // unit) * unit


def key_tile(keys, label, images, depth, kt_ref):
    heads = keys.shape[0] // HEAD_DIM
    tail = depth - HEAD_DIM
    at = lax.broadcasted_iota(jnp.int32, (tail, TILE), 0)
    mask = jnp.where((at == label) | (at >= images), 0.0, FAR)
    for head in range(heads):
        whole = jnp.concatenate([keys[head * HEAD_DIM : (head + 1) * HEAD_DIM], mask], axis=0)
        kt_ref[0, head] = jnp.transpose(whole).astype(BF)


def value_tile(values, v_ref):
    heads = values.shape[0] // HEAD_DIM
    ones = jnp.where(lax.broadcasted_iota(jnp.int32, (8, TILE), 0) == 0, 1.0, 0.0)
    for head in range(heads):
        v_ref[0, head] = jnp.concatenate(
            [values[head * HEAD_DIM : (head + 1) * HEAD_DIM], ones], axis=0
        ).astype(BF)


def prepare_own(images, depth, label_ref, qkv_ref, q_ref, kt_ref, v_ref):
    label = label_ref[0]
    queries = qkv_ref[0].astype(F32)
    heads = queries.shape[0] // HEAD_DIM
    at = lax.broadcasted_iota(jnp.int32, (depth - HEAD_DIM, TILE), 0)
    mark = jnp.where(at == label, 1.0, 0.0)
    for head in range(heads):
        q_ref[0, head] = jnp.concatenate(
            [queries[head * HEAD_DIM : (head + 1) * HEAD_DIM], mark], axis=0
        ).astype(BF)
    key_tile(qkv_ref[1].astype(F32), label, images, depth, kt_ref)
    value_tile(qkv_ref[2].astype(F32), v_ref)


def reorder_residual(perm_ref, low_ref, high_ref, out_ref):
    both = jnp.concatenate([low_ref[...], high_ref[...]], axis=1)
    out_ref[0] = jnp.dot(both, perm_ref[...], preferred_element_type=F32).astype(BF)


def attend(own, halos, images, base, rate, first_query, bounds, label_ref, *refs):
    count = len(halos)
    perm_hbm, q_hbm, kt_ref, v_ref, chunk_refs = *refs[:4], refs[4 : 4 + count]
    refs = refs[-(11 + count) :]
    out_ref, perm_ref, q_ref, kt_s, v_s, scores_s, acc, top, att = refs[:9]
    raw_s, sems, own_sems = refs[9 : 9 + count], refs[-2], refs[-1]
    queries, heads = q_ref.shape[0], q_ref.shape[1]
    depth = kt_s.shape[3]
    slots = pl.ds(own[0] - base, len(own))
    chunk_copies = [
        pltpu.make_async_copy(chunk_ref, raw, sems.at[at])
        for at, (chunk_ref, raw) in enumerate(zip(chunk_refs, raw_s))
    ]
    kt_copy = pltpu.make_async_copy(kt_ref, kt_s.at[slots], own_sems.at[0])
    v_copy = pltpu.make_async_copy(v_ref, v_s.at[slots], own_sems.at[1])
    q_copy = pltpu.make_async_copy(q_hbm.at[pl.ds(first_query, queries)], q_ref, own_sems.at[2])
    perm_copy = pltpu.make_async_copy(perm_hbm, perm_ref, own_sems.at[3])
    for copy in chunk_copies + [q_copy, kt_copy, v_copy, perm_copy]:
        copy.start()
    for tiles, copy, raw in zip(halos, chunk_copies, raw_s):
        copy.wait()
        for at, tile in enumerate(tiles):
            lanes = slice(at * TILE, (at + 1) * TILE)
            slot = pl.ds(tile - base, 1)
            key_tile(raw[0, :, lanes].astype(F32), label_ref[tile], images, depth, kt_s.at[slot])
            value_tile(raw[1, :, lanes].astype(F32), v_s.at[slot])
    q_copy.wait()
    kt_copy.wait()

    def attend_tile(side, carry):
        begin, end = bounds[0, first_query + side], bounds[1, first_query + side]
        acc[...] = jnp.zeros_like(acc)
        top[...] = jnp.full_like(top, FAR)

        def sweep(step):
            pairs = (end - begin) // 2

            def pair(index, carry):
                step(begin + 2 * index, 2)
                return carry

            def single(index, carry):
                step(end - 1, 1)
                return carry

            lax.fori_loop(0, pairs, pair, 0)
            lax.fori_loop(0, end - begin - 2 * pairs, single, 0)

        def score(tile, span):
            for head in range(heads):
                keys = kt_s[pl.ds(tile - base, span), head].reshape(span * TILE, -1)
                scores = jnp.dot(keys, q_ref[side, head], preferred_element_type=F32)
                scores_s[pl.ds(tile - begin, span), head] = scores.reshape(span, TILE, TILE)
                highest = jnp.max(scores.reshape(span * TILE // 8, 8, TILE), axis=0)
                top[head] = jnp.maximum(top[head], highest)

        sweep(score)

        @pl.when(side == 0)
        def _():
            v_copy.wait()

        tops = [jnp.max(top[head], axis=0, keepdims=True) for head in range(heads)]
        for head in range(heads):
            top[head, 0:1] = tops[head]

        def weigh(tile, span):
            for head in range(heads):
                scores = scores_s[pl.ds(tile - begin, span), head].reshape(span * TILE, TILE)
                weights = jnp.exp2((scores - top[head, 0:1]) * rate).astype(BF)
                values = [v_s[tile - base + at, head] for at in range(span)]
                values = values[0] if span == 1 else jnp.concatenate(values, axis=1)
                acc[head] += jnp.dot(values, weights, preferred_element_type=F32)

        sweep(weigh)
        whole = jnp.concatenate(
            [acc[head, :HEAD_DIM] / acc[head, HEAD_DIM : HEAD_DIM + 1] for head in range(heads)], axis=0
        )
        att[:, pl.ds(pl.multiple_of(side * TILE, TILE), TILE)] = whole.astype(BF)
        return carry

    lax.fori_loop(0, queries, attend_tile, 0)
    perm_copy.wait()
    for at in range(queries // 2):
        lanes = slice(2 * at * TILE, 2 * (at + 1) * TILE)
        out_ref[:, lanes] = jnp.dot(
            att[:, lanes], perm_ref[...], preferred_element_type=F32
        ).astype(BF)


def project(order, first, col_ref, gain_ref, perm_hbm, res_ref, wt_ref, mw_ref, *refs):
    count = len(order)
    att_refs = refs[:count]
    layer_ref, out_ref, gathered, layer_s, res_s, wt_s, mw_s, merged_s, perm_ref = refs[-13:-4]
    att_sem, wt_sem, res_sem, sems = refs[-4:]
    width = att_refs[0].shape[0]
    full = wt_ref.shape[0]
    block = 2 * TILE
    blocks = layer_s.shape[1] // block
    groups = block // 4
    col = col_ref[0]

    def part_copies(part):
        rows = pl.ds(pl.multiple_of(part * width, 16), width)
        return (
            pltpu.make_async_copy(wt_ref.at[rows, :], wt_s.at[rows, :], wt_sem.at[part]),
            pltpu.make_async_copy(
                res_ref.at[part, pl.ds(first, blocks)], res_s.at[part], res_sem.at[part]
            ),
        )

    att_copies = []
    for part, (bit, att_ref) in enumerate(zip(order, att_refs)):
        row = pl.multiple_of((col ^ bit) * width, 16)
        att_copies.append(
            pltpu.make_async_copy(att_ref, gathered.at[pl.ds(row, width), :], att_sem.at[part])
        )
    late = [
        pltpu.make_async_copy(perm_hbm, perm_ref, sems.at[0]),
        pltpu.make_async_copy(mw_ref, mw_s, sems.at[1]),
    ]
    for copy in att_copies:
        copy.start()
    for part in range(count):
        for copy in part_copies(part):
            copy.start()
    for copy in late:
        copy.start()
    for copy in att_copies:
        copy.wait()

    def project_part(part, carry):
        rows = pl.ds(pl.multiple_of(part * width, 16), width)
        for copy in part_copies(part):
            copy.wait()
        for at in range(blocks):
            lanes = slice(at * block, (at + 1) * block)
            projected = jnp.dot(wt_s[rows, :], gathered[:, lanes], preferred_element_type=F32)
            layer_s[rows, lanes] = (res_s[part, at].astype(F32) + projected).astype(BF)
        return carry

    lax.fori_loop(0, count, project_part, 0)
    for copy in late:
        copy.wait()
    own = pl.ds(pl.multiple_of(col * width, 16), width)
    for at in range(blocks):
        lanes = slice(at * block, (at + 1) * block)
        layer_ref[:, lanes] = lax.dot_general(
            layer_s[own, lanes], perm_ref[...], (((1,), (1,)), ((), ())), preferred_element_type=F32
        ).astype(BF)
    merged_s[...] = jnp.zeros_like(merged_s)

    def merge_part(j, carry):
        columns = []
        for at in range(blocks):
            lanes = pl.ds(pl.multiple_of(at * block + j * groups, groups), groups)
            values = layer_s[:, lanes].astype(F32)
            values = values - jnp.sum(values, axis=0, keepdims=True) / full
            spread = jnp.sum(jnp.square(values), axis=0, keepdims=True) / full
            normed = (values * lax.rsqrt(spread + 1e-06) * gain_ref[...]).astype(BF)
            columns.append(normed)
        weights = mw_s[:, pl.ds(pl.multiple_of(j * full, 128), full)]
        merged_s[...] += jnp.dot(
            weights, jnp.concatenate(columns, axis=1), preferred_element_type=F32
        )
        return carry

    lax.fori_loop(0, 4, merge_part, 0)
    out_ref[...] = merged_s[...].astype(BF)


def outgoing(pieces, slot_ref, place_ref, *refs):
    merged_refs, out_refs = refs[:-pieces], refs[-pieces:]
    total = None
    share, wide = out_refs[0].shape
    for part, merged_ref in enumerate(merged_refs):
        groups = merged_ref.shape[1]
        row = lax.broadcasted_iota(jnp.int32, (share * pieces, groups), 0)
        pick = jnp.where(row == slot_ref[part], 1.0, 0.0).astype(BF)
        rows = jnp.concatenate([merged_ref[...], place_ref[part]], axis=0)
        term = lax.dot_general(pick, rows, (((1,), (1,)), ((), ())), preferred_element_type=F32)
        total = term if total is None else total + term
    for piece, out_ref in enumerate(out_refs):
        out_ref[...] = total[piece * share : (piece + 1) * share].astype(BF)


def incoming(width, base, *refs):
    in_refs, out_ref = refs[:-1], refs[-1]
    rows = jnp.concatenate([in_ref[...] for in_ref in in_refs], axis=0)
    place = rows[:, width : width + 2].astype(F32)
    target = (place[:, 0:1] * base + place[:, 1:2]).astype(jnp.int32)
    slots = rows.shape[0]
    lane = lax.broadcasted_iota(jnp.int32, (slots, slots), 1)
    pick = jnp.where(lane == target, 1.0, 0.0).astype(BF)
    out_ref[...] = lax.dot_general(
        rows[:, :width], pick, (((0,), (0,)), ((), ())), preferred_element_type=F32
    ).astype(BF)


def body(qkv, residual_in, out_weight, merge_weight, merge_gain, image_groups, dest_row):
    width = qkv.shape[1]
    tokens = qkv.shape[2]
    heads = width // HEAD_DIM
    full = out_weight.shape[0]
    images = image_groups.shape[0]
    reach = tokens // 2
    own_tiles = tokens // TILE
    far_tiles = reach // TILE
    half = own_tiles // 2
    plan = [half // 2, half - half // 2]
    begins = [sum(plan[:s]) for s in range(len(plan))]
    stages = len(plan)
    depth = round_up(HEAD_DIM + images, 128)
    rate = math.log2(math.e) / math.sqrt(HEAD_DIM)
    rows, cols = lax.axis_size("row"), lax.axis_size("col")
    row_id, col_id = lax.axis_index("row"), lax.axis_index("col")
    forward = [(i, (i + 1) % rows) for i in range(rows)]
    backward = [((i + 1) % rows, i) for i in range(rows)]

    lefts, rights = [], []

    def send_chunk(stage, after):
        source = qkv
        if after is not None:
            source, _ = lax.optimization_barrier((qkv, after))
        near, far = begins[stage] * TILE, (begins[stage] + plan[stage]) * TILE
        tail = lax.slice(source, (1, 0, tokens - far), (3, width, tokens - near))
        head = lax.slice(source, (1, 0, near), (3, width, far))
        lefts.append(lax.ppermute(tail, "row", forward))
        rights.append(lax.ppermute(head, "row", backward))
        return tail, head

    first_chunk = send_chunk(0, None)

    image_ends = jnp.cumsum(image_groups) * 4
    window_tiles = own_tiles + 2 * far_tiles
    positions = row_id * tokens - reach + jnp.arange(window_tiles * TILE, dtype=jnp.int32)
    labels = jnp.sum((positions[:, None] >= image_ends[None, :]).astype(jnp.int32), axis=1)
    labels = jnp.where(positions >= 0, labels, -1).reshape(window_tiles, 1, TILE)
    starts = row_id * tokens + jnp.arange(own_tiles, dtype=jnp.int32) * TILE
    ends = starts + TILE - 1
    low = jnp.max(jnp.where(image_ends[None, :] <= starts[:, None], image_ends[None, :], 0), axis=1)
    high = jnp.min(
        jnp.where(image_ends[None, :] > ends[:, None], image_ends[None, :], rows * tokens), axis=1
    )
    window_start = row_id * tokens - reach
    low = (low - window_start) // TILE
    high = (high - window_start + TILE - 1) // TILE
    tile_at = jnp.arange(own_tiles, dtype=jnp.int32)
    low = jnp.maximum(low, tile_at)
    high = jnp.minimum(high, tile_at + 2 * far_tiles + 1)

    inner = plan[0]

    def pair_tile(block, which):
        near = half - inner + 2 * block + which
        mirrored = half + block if which else half - 1 - block
        if isinstance(block, int):
            return near if block < inner else mirrored
        return jnp.where(block < inner, near, mirrored)

    def stage_order(tile):
        mirrored = jnp.where(tile >= half, 2 * (tile - half) + 1, 2 * (half - 1 - tile))
        near = tile - (half - inner)
        return jnp.where((near >= 0) & (near < 2 * inner), near, mirrored)

    at = jnp.arange(2 * TILE, dtype=jnp.int32)
    perm = (((at % 4) * (TILE // 2) + at // 4)[:, None] == at[None, :]).astype(BF)

    qkv_after, _ = lax.optimization_barrier((qkv, first_chunk))
    kt_shape, v_shape = (heads, TILE, depth), (heads, HEAD_DIM + 8, TILE)
    q_tiles, kt_own, v_own = pl.pallas_call(
        functools.partial(prepare_own, images, depth),
        grid=(own_tiles,),
        in_specs=[
            pl.BlockSpec((1, 1, TILE), lambda i: (i + far_tiles, 0, 0)),
            pl.BlockSpec((3, width, TILE), lambda i: (0, 0, i)),
        ],
        out_specs=[
            pl.BlockSpec((1, heads, depth, TILE), lambda i: (stage_order(i), 0, 0, 0)),
            pl.BlockSpec((1,) + kt_shape, lambda i: (i, 0, 0, 0)),
            pl.BlockSpec((1,) + v_shape, lambda i: (i, 0, 0, 0)),
        ],
        out_shape=[
            jax.ShapeDtypeStruct((own_tiles, heads, depth, TILE), BF),
            jax.ShapeDtypeStruct((own_tiles,) + kt_shape, BF),
            jax.ShapeDtypeStruct((own_tiles,) + v_shape, BF),
        ],
        compiler_params=params(16),
        cost_estimate=cost(2e9, 1e5),
        name="prepare_own",
    )(labels, qkv_after)

    residual_in, _ = lax.optimization_barrier((residual_in, first_chunk))
    blocks = own_tiles // 2
    residual = pl.pallas_call(
        reorder_residual,
        grid=(blocks,),
        in_specs=[
            pl.BlockSpec((2 * TILE, 2 * TILE), lambda i: (0, 0)),
            pl.BlockSpec((width, TILE), lambda i: (0, pair_tile(i, 0))),
            pl.BlockSpec((width, TILE), lambda i: (0, pair_tile(i, 1))),
        ],
        out_specs=pl.BlockSpec((1, width, 2 * TILE), lambda i: (i, 0, 0)),
        out_shape=jax.ShapeDtypeStruct((blocks, width, 2 * TILE), BF),
        compiler_params=params(16),
        cost_estimate=cost(2e9, 1e5),
        name="reorder_residual",
    )(perm, residual_in, residual_in)
    residual = lax.all_gather(residual, "col", axis=0)
    tile_order = [pair_tile(block, which) for block in range(blocks) for which in range(2)]
    out_weight_t = jnp.transpose(out_weight)
    key_bounds = jnp.stack([low, high])
    key_bounds = jnp.stack([key_bounds[:, tile] for tile in tile_order], axis=1)
    gain = merge_gain[:, None]
    bits = []
    span = cols // 2
    while span:
        bits.append(span)
        span //= 2
    order = [0]
    for bit in bits:
        order = order + [bit ^ other for other in order]
    col_value = col_id.astype(jnp.int32).reshape(1)

    layers, parts, gathers = [], [], []
    any_spec = pl.BlockSpec(memory_space=pl.ANY)
    smem_spec = pl.BlockSpec(memory_space=pltpu.SMEM)
    vmem_spec = pl.BlockSpec(memory_space=pltpu.VMEM)
    def spread_pieces(stage, some_bits, after):
        pieces = gathers[stage]
        for bit in some_bits:
            pairs = [(i, i ^ bit) for i in range(cols)]
            sources = pieces
            if after is not None:
                sources, _ = lax.optimization_barrier((pieces, after))
            pieces = pieces + [lax.ppermute(piece, "col", pairs) for piece in sources]
        gathers[stage] = pieces

    def run_project(stage):
        size = plan[stage]
        columns, merged_columns = 2 * size * TILE, size * TILE // 2
        after = [gathers[-1][0]] + layers[-1:]
        layer, part = pl.pallas_call(
            functools.partial(project, order, begins[stage]),
            grid=(1,),
            in_specs=[smem_spec, vmem_spec] + [any_spec] * (4 + cols + len(after)),
            out_specs=[vmem_spec, vmem_spec],
            out_shape=[
                jax.ShapeDtypeStruct((width, columns), BF),
                jax.ShapeDtypeStruct((width, merged_columns), BF),
            ],
            scratch_shapes=[
                pltpu.VMEM((full, columns), BF),
                pltpu.VMEM((full, columns), BF),
                pltpu.VMEM((cols, size, width, 2 * TILE), BF),
                pltpu.VMEM((full, full), BF),
                pltpu.VMEM((width, 4 * full), BF),
                pltpu.VMEM((width, merged_columns), F32),
                pltpu.VMEM(perm.shape, BF),
                pltpu.SemaphoreType.DMA((cols,)),
                pltpu.SemaphoreType.DMA((cols,)),
                pltpu.SemaphoreType.DMA((cols,)),
                pltpu.SemaphoreType.DMA((2,)),
            ],
            compiler_params=params(62),
            cost_estimate=cost((4 + 4 * size) * 1e9, 1e5),
            name="project",
        )(col_value, gain, perm, residual, out_weight_t, merge_weight, *gathers[stage], *after)
        layers.append(layer)
        parts.append(part)

    for stage in range(stages):
        size, near = plan[stage], begins[stage]
        if stage + 1 < stages:
            send_chunk(stage + 1, (lefts[stage], rights[stage]))
        own = list(range(far_tiles, far_tiles + own_tiles))
        base_tile = far_tiles - near - size
        tiles = own_tiles + 2 * (near + size)
        halos, chunks = [], []
        for before in range(stage + 1):
            inner_edge, outer_edge = begins[before], begins[before] + plan[before]
            halos.append(list(range(far_tiles - outer_edge, far_tiles - inner_edge)))
            halos.append([far_tiles + own_tiles + at for at in range(inner_edge, outer_edge)])
            chunks += [lefts[before], rights[before]]
        after = [gathers[-1][0] if gathers else out_weight_t]
        attended = pl.pallas_call(
            functools.partial(attend, own, halos, images, base_tile, rate, 2 * near),
            grid=(1,),
            in_specs=[smem_spec, vmem_spec] + [any_spec] * (4 + len(chunks) + len(after)),
            out_specs=vmem_spec,
            out_shape=jax.ShapeDtypeStruct((width, 2 * size * TILE), BF),
            scratch_shapes=[
                pltpu.VMEM(perm.shape, BF),
                pltpu.VMEM((2 * size, heads, depth, TILE), BF),
                pltpu.VMEM((tiles,) + kt_shape, BF),
                pltpu.VMEM((tiles,) + v_shape, BF),
                pltpu.VMEM((2 * far_tiles + 1, heads, TILE, TILE), F32),
                pltpu.VMEM((heads, HEAD_DIM + 8, TILE), F32),
                pltpu.VMEM((heads, 8, TILE), F32),
                pltpu.VMEM((width, 2 * size * TILE), BF),
            ]
            + [pltpu.VMEM(chunk.shape, BF) for chunk in chunks]
            + [pltpu.SemaphoreType.DMA((len(chunks),)), pltpu.SemaphoreType.DMA((4,))],
            compiler_params=params(62),
            cost_estimate=cost((5 + 4 * size) * 1e9, 1e5),
            name="attend",
        )(key_bounds, labels, perm, q_tiles, kt_own, v_own, *chunks, *after)

        gathers.append([attended])
        spread_pieces(stage, bits[:1], None)
    spread_pieces(0, bits[1:], gathers[1][0])
    run_project(0)
    spread_pieces(1, bits[1:], layers[0])
    run_project(1)

    tiles_out = [None] * own_tiles
    for stage in range(stages):
        for block in range(plan[stage]):
            for which in range(2):
                lane = (2 * block + which) * TILE
                tile = pair_tile(begins[stage] + block, which)
                tiles_out[tile] = layers[stage][:, lane : lane + TILE]
    layer_out = jnp.concatenate(tiles_out, axis=1)

    groups = tokens // 4
    share = groups // rows
    piece_groups = TILE // 4
    owner = dest_row // groups
    place = dest_row % groups
    index = jnp.arange(groups, dtype=jnp.int32)
    rank = jnp.sum(
        ((owner[:, None] == owner[None, :]) & (index[None, :] < index[:, None])).astype(jnp.int32),
        axis=1,
    )
    base = 32
    away = (owner - row_id) % rows
    info = jnp.stack([away * share + rank, place // base, place % base])
    info = info.reshape(3, own_tiles, piece_groups)
    merges = [list(range(b, b + n)) for b, n in zip(begins, plan)]
    info = jnp.stack(
        [
            jnp.concatenate(
                [
                    info[:, pair_tile(block, which)]
                    for block in merge
                    for which in range(2)
                ],
                axis=1,
            )
            for merge in merges
        ],
        axis=1,
    )
    slots = info[0][:, None, :]
    wide = round_up(width + 2, 128)
    places = jnp.concatenate(
        [
            jnp.stack([info[1], info[2]], axis=1).astype(BF),
            jnp.zeros((len(merges), wide - width - 2, 4 * piece_groups), BF),
        ],
        axis=1,
    )
    sent = pl.pallas_call(
        functools.partial(outgoing, rows),
        out_shape=[jax.ShapeDtypeStruct((share, wide), BF)] * rows,
        compiler_params=params(16),
        cost_estimate=cost(1e9, 1e5),
        name="outgoing",
    )(slots, places, *parts)
    received = [sent[0]] + [
        lax.ppermute(sent[step], "row", [(i, (i + step) % rows) for i in range(rows)])
        for step in range(1, rows)
    ]
    image_rows = pl.pallas_call(
        functools.partial(incoming, width, base),
        out_shape=jax.ShapeDtypeStruct((width, groups), BF),
        compiler_params=params(16),
        cost_estimate=cost(1e9, 1e5),
        name="incoming",
    )(*received)
    return (layer_out, image_rows)


def solution(mesh):
    return jax.shard_map(
        body,
        mesh=mesh,
        in_specs=(P(None, "col", "row"), P("col", "row"), P(), P("col", None), P(), P(), P("row")),
        out_specs=(P("col", "row"), P("col", "row")),
        check_vma=False,
    )
```

```python
import functools
import math

import jax
import jax.numpy as jnp
from jax import lax
from jax.experimental import pallas as pl
from jax.experimental.pallas import tpu as pltpu
from jax.sharding import PartitionSpec as P

HEAD_DIM = 88
TILE = 256
FAR = -1e30
BF = jnp.bfloat16
F32 = jnp.float32


def params(mib):
    return pltpu.CompilerParams(vmem_limit_bytes=mib * 1024 * 1024)


def cost(flops, bytes_accessed):
    return pl.CostEstimate(flops=int(flops), bytes_accessed=int(bytes_accessed), transcendentals=0)


def round_up(value, unit):
    return -(-value // unit) * unit


def key_tile(keys, label, images, depth, kt_ref):
    heads = keys.shape[0] // HEAD_DIM
    tail = depth - HEAD_DIM
    at = lax.broadcasted_iota(jnp.int32, (tail, TILE), 0)
    mask = jnp.where((at == label) | (at >= images), 0.0, FAR)
    for head in range(heads):
        whole = jnp.concatenate([keys[head * HEAD_DIM : (head + 1) * HEAD_DIM], mask], axis=0)
        kt_ref[0, head] = jnp.transpose(whole).astype(BF)


def value_tile(values, v_ref):
    heads = values.shape[0] // HEAD_DIM
    ones = jnp.where(lax.broadcasted_iota(jnp.int32, (8, TILE), 0) == 0, 1.0, 0.0)
    for head in range(heads):
        v_ref[0, head] = jnp.concatenate(
            [values[head * HEAD_DIM : (head + 1) * HEAD_DIM], ones], axis=0
        ).astype(BF)


def prepare_own(images, depth, label_ref, qkv_ref, q_ref, kt_ref, v_ref):
    label = label_ref[0]
    queries = qkv_ref[0].astype(F32)
    heads = queries.shape[0] // HEAD_DIM
    at = lax.broadcasted_iota(jnp.int32, (depth - HEAD_DIM, TILE), 0)
    mark = jnp.where(at == label, 1.0, 0.0)
    for head in range(heads):
        q_ref[0, head] = jnp.concatenate(
            [queries[head * HEAD_DIM : (head + 1) * HEAD_DIM], mark], axis=0
        ).astype(BF)
    key_tile(qkv_ref[1].astype(F32), label, images, depth, kt_ref)
    value_tile(qkv_ref[2].astype(F32), v_ref)


def attend(own, halos, images, base, rate, first_query, bounds, label_ref, *refs):
    count = len(halos)
    q_hbm, kt_ref, v_ref, chunk_refs = *refs[:3], refs[3 : 3 + count]
    refs = refs[-(9 + count) :]
    out_ref, q_ref, kt_s, v_s, scores_s, acc, top = refs[:7]
    raw_s, sems, own_sems = refs[7 : 7 + count], refs[-2], refs[-1]
    queries, heads = q_ref.shape[0], q_ref.shape[1]
    depth = kt_s.shape[3]
    slots = pl.ds(own[0] - base, len(own))
    chunk_copies = [
        pltpu.make_async_copy(chunk_ref, raw, sems.at[at])
        for at, (chunk_ref, raw) in enumerate(zip(chunk_refs, raw_s))
    ]
    kt_copy = pltpu.make_async_copy(kt_ref, kt_s.at[slots], own_sems.at[0])
    v_copy = pltpu.make_async_copy(v_ref, v_s.at[slots], own_sems.at[1])
    q_copy = pltpu.make_async_copy(q_hbm.at[pl.ds(first_query, queries)], q_ref, own_sems.at[2])
    for copy in chunk_copies + [q_copy, kt_copy, v_copy]:
        copy.start()
    for tiles, copy, raw in zip(halos, chunk_copies, raw_s):
        copy.wait()
        for at, tile in enumerate(tiles):
            lanes = slice(at * TILE, (at + 1) * TILE)
            slot = pl.ds(tile - base, 1)
            key_tile(raw[0, :, lanes].astype(F32), label_ref[tile], images, depth, kt_s.at[slot])
            value_tile(raw[1, :, lanes].astype(F32), v_s.at[slot])
    q_copy.wait()
    kt_copy.wait()

    def attend_tile(side, carry):
        begin, end = bounds[0, first_query + side], bounds[1, first_query + side]
        acc[...] = jnp.zeros_like(acc)
        top[...] = jnp.full_like(top, FAR)

        def sweep(step):
            pairs = (end - begin) // 2

            def pair(index, carry):
                step(begin + 2 * index, 2)
                return carry

            def single(index, carry):
                step(end - 1, 1)
                return carry

            lax.fori_loop(0, pairs, pair, 0)
            lax.fori_loop(0, end - begin - 2 * pairs, single, 0)

        def score(tile, span):
            for head in range(heads):
                keys = kt_s[pl.ds(tile - base, span), head].reshape(span * TILE, -1)
                scores = jnp.dot(keys, q_ref[side, head], preferred_element_type=F32)
                scores_s[pl.ds(tile - begin, span), head] = scores.reshape(span, TILE, TILE)
                highest = jnp.max(scores.reshape(span * TILE // 8, 8, TILE), axis=0)
                top[head] = jnp.maximum(top[head], highest)

        sweep(score)

        @pl.when(side == 0)
        def _():
            v_copy.wait()

        tops = [jnp.max(top[head], axis=0, keepdims=True) for head in range(heads)]
        for head in range(heads):
            top[head, 0:1] = tops[head]

        def weigh(tile, span):
            for head in range(heads):
                scores = scores_s[pl.ds(tile - begin, span), head].reshape(span * TILE, TILE)
                weights = jnp.exp2((scores - top[head, 0:1]) * rate).astype(BF)
                values = [v_s[tile - base + at, head] for at in range(span)]
                values = values[0] if span == 1 else jnp.concatenate(values, axis=1)
                acc[head] += jnp.dot(values, weights, preferred_element_type=F32)

        sweep(weigh)
        whole = jnp.concatenate(
            [acc[head, :HEAD_DIM] / acc[head, HEAD_DIM : HEAD_DIM + 1] for head in range(heads)], axis=0
        )
        out_ref[:, pl.ds(pl.multiple_of(side * TILE, TILE), TILE)] = whole.astype(BF)
        return carry

    lax.fori_loop(0, queries, attend_tile, 0)


def project(order, spans, last, paired, col_ref, gain_ref, perm_hbm, res_ref, wt_ref, mw_ref, *refs):
    count = len(order)
    att_refs, before_hbm = refs[:count], refs[count]
    layer_ref, out_ref, gathered, layer_s, res_s, wt_s, mw_s, merged_s, before_ref, perm_ref = refs[-14:-4]
    att_sem, wt_sem, res_sem, sems = refs[-4:]
    width = att_refs[0].shape[0]
    full = wt_ref.shape[0]
    block = 2 * TILE
    blocks = layer_s.shape[1] // block
    groups = block // 4
    col = col_ref[0]

    def part_copies(part):
        rows = pl.ds(pl.multiple_of(part * width, 16), width)
        made = [pltpu.make_async_copy(wt_ref.at[rows, :], wt_s.at[rows, :], wt_sem.at[part])]
        for at, (column, token, size) in enumerate(spans):
            made.append(
                pltpu.make_async_copy(
                    res_ref.at[part, :, pl.ds(token, size)],
                    res_s.at[part, :, pl.ds(column, size)],
                    res_sem.at[part, at],
                )
            )
        return made

    att_copies = []
    for part, (bit, att_ref) in enumerate(zip(order, att_refs)):
        row = pl.multiple_of((col ^ bit) * width, 16)
        att_copies.append(
            pltpu.make_async_copy(att_ref, gathered.at[pl.ds(row, width), :], att_sem.at[part])
        )
    late = [pltpu.make_async_copy(perm_hbm, perm_ref, sems.at[0])]
    if last:
        late.append(pltpu.make_async_copy(mw_ref, mw_s, sems.at[1]))
    if paired:
        late.append(pltpu.make_async_copy(before_hbm, before_ref, sems.at[2]))
    for copy in att_copies:
        copy.start()
    for part in range(count):
        for copy in part_copies(part):
            copy.start()
    for copy in late:
        copy.start()
    for copy in att_copies:
        copy.wait()

    def project_part(part, carry):
        rows = pl.ds(pl.multiple_of(part * width, 16), width)
        for copy in part_copies(part):
            copy.wait()
        for at in range(blocks):
            lanes = slice(at * block, (at + 1) * block)
            projected = jnp.dot(wt_s[rows, :], gathered[:, lanes], preferred_element_type=F32)
            layer_s[rows, lanes] = (res_s[part, :, lanes].astype(F32) + projected).astype(BF)
        return carry

    lax.fori_loop(0, count, project_part, 0)
    layer_ref[...] = layer_s[pl.ds(pl.multiple_of(col * width, 16), width), :]

    def norm_part(at, carry):
        lanes = pl.ds(pl.multiple_of(at * groups, groups), groups)
        values = layer_s[:, lanes].astype(F32)
        values = values - jnp.sum(values, axis=0, keepdims=True) / full
        spread = jnp.sum(jnp.square(values), axis=0, keepdims=True) / full
        gathered[:, lanes] = (values * lax.rsqrt(spread + 1e-06) * gain_ref[...]).astype(BF)
        return carry

    lax.fori_loop(0, 4 * blocks, norm_part, 0)
    for copy in late:
        copy.wait()

    def group_part(part, carry):
        rows = pl.ds(pl.multiple_of(part * width, 16), width)
        for at in range(blocks):
            lanes = slice(at * block, (at + 1) * block)
            grouped = jnp.dot(gathered[rows, lanes], perm_ref[...], preferred_element_type=F32)
            layer_s[rows, lanes] = grouped.astype(BF)
        return carry

    lax.fori_loop(0, count, group_part, 0)
    if not last:
        out_ref[...] = layer_s[...]
        return
    merged_s[...] = jnp.zeros_like(merged_s)

    def merge_part(j, carry):
        columns = [before_ref[:, pl.ds(pl.multiple_of(j * groups, groups), groups)]] if paired else []
        for at in range(blocks):
            columns.append(layer_s[:, pl.ds(pl.multiple_of(at * block + j * groups, groups), groups)])
        weights = mw_s[:, pl.ds(pl.multiple_of(j * full, 128), full)]
        merged_s[...] += jnp.dot(
            weights, jnp.concatenate(columns, axis=1), preferred_element_type=F32
        )
        return carry

    lax.fori_loop(0, 4, merge_part, 0)
    out_ref[...] = merged_s[...].astype(BF)


def outgoing(pieces, slot_ref, place_ref, *refs):
    merged_refs, out_refs = refs[:-pieces], refs[-pieces:]
    total = None
    share, wide = out_refs[0].shape
    for part, merged_ref in enumerate(merged_refs):
        groups = merged_ref.shape[1]
        row = lax.broadcasted_iota(jnp.int32, (share * pieces, groups), 0)
        pick = jnp.where(row == slot_ref[part], 1.0, 0.0).astype(BF)
        rows = jnp.concatenate([merged_ref[...], place_ref[part]], axis=0)
        term = lax.dot_general(pick, rows, (((1,), (1,)), ((), ())), preferred_element_type=F32)
        total = term if total is None else total + term
    for piece, out_ref in enumerate(out_refs):
        out_ref[...] = total[piece * share : (piece + 1) * share].astype(BF)


def incoming(width, base, *refs):
    in_refs, out_ref = refs[:-1], refs[-1]
    rows = jnp.concatenate([in_ref[...] for in_ref in in_refs], axis=0)
    place = rows[:, width : width + 2].astype(F32)
    target = (place[:, 0:1] * base + place[:, 1:2]).astype(jnp.int32)
    slots = rows.shape[0]
    lane = lax.broadcasted_iota(jnp.int32, (slots, slots), 1)
    pick = jnp.where(lane == target, 1.0, 0.0).astype(BF)
    out_ref[...] = lax.dot_general(
        rows[:, :width], pick, (((0,), (0,)), ((), ())), preferred_element_type=F32
    ).astype(BF)


def body(qkv, residual_in, out_weight, merge_weight, merge_gain, image_groups, dest_row):
    width = qkv.shape[1]
    tokens = qkv.shape[2]
    heads = width // HEAD_DIM
    full = out_weight.shape[0]
    images = image_groups.shape[0]
    reach = tokens // 2
    own_tiles = tokens // TILE
    far_tiles = reach // TILE
    half = own_tiles // 2
    plan = [half // 2] + [1] * (half - half // 2)
    begins = [sum(plan[:s]) for s in range(len(plan))]
    stages = len(plan)
    depth = round_up(HEAD_DIM + images, 128)
    rate = math.log2(math.e) / math.sqrt(HEAD_DIM)
    rows, cols = lax.axis_size("row"), lax.axis_size("col")
    row_id, col_id = lax.axis_index("row"), lax.axis_index("col")
    forward = [(i, (i + 1) % rows) for i in range(rows)]
    backward = [((i + 1) % rows, i) for i in range(rows)]

    lefts, rights = [], []

    def send_chunk(stage, after):
        source = qkv
        if after is not None:
            source, _ = lax.optimization_barrier((qkv, after))
        near, far = begins[stage] * TILE, (begins[stage] + plan[stage]) * TILE
        tail = lax.slice(source, (1, 0, tokens - far), (3, width, tokens - near))
        head = lax.slice(source, (1, 0, near), (3, width, far))
        lefts.append(lax.ppermute(tail, "row", forward))
        rights.append(lax.ppermute(head, "row", backward))
        return tail, head

    first_chunk = send_chunk(0, None)
    residual = lax.all_gather(residual_in, "col", axis=0)
    blocks = own_tiles // 2

    image_ends = jnp.cumsum(image_groups) * 4
    window_tiles = own_tiles + 2 * far_tiles
    positions = row_id * tokens - reach + jnp.arange(window_tiles * TILE, dtype=jnp.int32)
    labels = jnp.sum((positions[:, None] >= image_ends[None, :]).astype(jnp.int32), axis=1)
    labels = jnp.where(positions >= 0, labels, -1).reshape(window_tiles, 1, TILE)
    starts = row_id * tokens + jnp.arange(own_tiles, dtype=jnp.int32) * TILE
    ends = starts + TILE - 1
    low = jnp.max(jnp.where(image_ends[None, :] <= starts[:, None], image_ends[None, :], 0), axis=1)
    high = jnp.min(
        jnp.where(image_ends[None, :] > ends[:, None], image_ends[None, :], rows * tokens), axis=1
    )
    window_start = row_id * tokens - reach
    low = (low - window_start) // TILE
    high = (high - window_start + TILE - 1) // TILE
    tile_at = jnp.arange(own_tiles, dtype=jnp.int32)
    low = jnp.maximum(low, tile_at)
    high = jnp.minimum(high, tile_at + 2 * far_tiles + 1)

    inner = plan[0]

    def pair_tile(block, which):
        near = half - inner + 2 * block + which
        mirrored = half + block if which else half - 1 - block
        if isinstance(block, int):
            return near if block < inner else mirrored
        return jnp.where(block < inner, near, mirrored)

    def stage_order(tile):
        mirrored = jnp.where(tile >= half, 2 * (tile - half) + 1, 2 * (half - 1 - tile))
        near = tile - (half - inner)
        return jnp.where((near >= 0) & (near < 2 * inner), near, mirrored)

    at = jnp.arange(2 * TILE, dtype=jnp.int32)
    perm = (((at % 4) * (TILE // 2) + at // 4)[:, None] == at[None, :]).astype(BF)

    qkv_after, _ = lax.optimization_barrier((qkv, first_chunk))
    kt_shape, v_shape = (heads, TILE, depth), (heads, HEAD_DIM + 8, TILE)
    q_tiles, kt_own, v_own = pl.pallas_call(
        functools.partial(prepare_own, images, depth),
        grid=(own_tiles,),
        in_specs=[
            pl.BlockSpec((1, 1, TILE), lambda i: (i + far_tiles, 0, 0)),
            pl.BlockSpec((3, width, TILE), lambda i: (0, 0, i)),
        ],
        out_specs=[
            pl.BlockSpec((1, heads, depth, TILE), lambda i: (stage_order(i), 0, 0, 0)),
            pl.BlockSpec((1,) + kt_shape, lambda i: (i, 0, 0, 0)),
            pl.BlockSpec((1,) + v_shape, lambda i: (i, 0, 0, 0)),
        ],
        out_shape=[
            jax.ShapeDtypeStruct((own_tiles, heads, depth, TILE), BF),
            jax.ShapeDtypeStruct((own_tiles,) + kt_shape, BF),
            jax.ShapeDtypeStruct((own_tiles,) + v_shape, BF),
        ],
        compiler_params=params(16),
        cost_estimate=cost(2e9, 1e5),
        name="prepare_own",
    )(labels, qkv_after)

    out_weight_t = jnp.transpose(out_weight)
    tile_order = [pair_tile(block, which) for block in range(blocks) for which in range(2)]
    key_bounds = jnp.stack([low, high])
    key_bounds = jnp.stack([key_bounds[:, tile] for tile in tile_order], axis=1)
    gain = merge_gain[:, None]
    bits = []
    span = cols // 2
    while span:
        bits.append(span)
        span //= 2
    order = [0]
    for bit in bits:
        order = order + [bit ^ other for other in order]
    col_value = col_id.astype(jnp.int32).reshape(1)

    layers, parts, gathers = [], [], []
    any_spec = pl.BlockSpec(memory_space=pl.ANY)
    smem_spec = pl.BlockSpec(memory_space=pltpu.SMEM)
    vmem_spec = pl.BlockSpec(memory_space=pltpu.VMEM)
    def spread_pieces(stage, some_bits, after):
        pieces = gathers[stage]
        for bit in some_bits:
            pairs = [(i, i ^ bit) for i in range(cols)]
            sources = pieces
            if after is not None:
                sources, _ = lax.optimization_barrier((pieces, after))
            pieces = pieces + [lax.ppermute(piece, "col", pairs) for piece in sources]
        gathers[stage] = pieces

    def run_project(stage):
        size = plan[stage]
        last, paired = stage != 1, stage == 2
        before = parts[1] if paired else perm
        columns = 2 * size * TILE
        merged_columns = (size + paired) * TILE // 2
        spans = []
        for at in range(size):
            tile, other = pair_tile(begins[stage] + at, 0), pair_tile(begins[stage] + at, 1)
            if other == tile + 1:
                spans.append((2 * at * TILE, tile * TILE, 2 * TILE))
            else:
                spans.append((2 * at * TILE, tile * TILE, TILE))
                spans.append(((2 * at + 1) * TILE, other * TILE, TILE))
        after = [gathers[-1][0]] + layers[-1:]
        layer, part = pl.pallas_call(
            functools.partial(project, order, spans, last, paired),
            grid=(1,),
            in_specs=[smem_spec, vmem_spec] + [any_spec] * (5 + cols + len(after)),
            out_specs=[vmem_spec, vmem_spec],
            out_shape=[
                jax.ShapeDtypeStruct((width, columns), BF),
                jax.ShapeDtypeStruct((width, merged_columns) if last else (full, columns), BF),
            ],
            scratch_shapes=[
                pltpu.VMEM((full, columns), BF),
                pltpu.VMEM((full, columns), BF),
                pltpu.VMEM((cols, width, columns), BF),
                pltpu.VMEM((full, full), BF),
                pltpu.VMEM((width, 4 * full), BF),
                pltpu.VMEM((width, merged_columns), F32),
                pltpu.VMEM((full, 2 * TILE), BF),
                pltpu.VMEM(perm.shape, BF),
                pltpu.SemaphoreType.DMA((cols,)),
                pltpu.SemaphoreType.DMA((cols,)),
                pltpu.SemaphoreType.DMA((cols, len(spans))),
                pltpu.SemaphoreType.DMA((3,)),
            ],
            compiler_params=params(62),
            cost_estimate=cost((4 + 4 * size) * 1e9, 1e5),
            name="project",
        )(col_value, gain, perm, residual, out_weight_t, merge_weight, *gathers[stage], before, *after)
        layers.append(layer)
        parts.append(part)

    for stage in range(stages):
        size, near = plan[stage], begins[stage]
        if stage + 1 < stages:
            send_chunk(stage + 1, (lefts[stage], rights[stage]))
        own = list(range(far_tiles, far_tiles + own_tiles))
        base_tile = far_tiles - near - size
        tiles = own_tiles + 2 * (near + size)
        halos, chunks = [], []
        for before in range(stage + 1):
            inner_edge, outer_edge = begins[before], begins[before] + plan[before]
            halos.append(list(range(far_tiles - outer_edge, far_tiles - inner_edge)))
            halos.append([far_tiles + own_tiles + at for at in range(inner_edge, outer_edge)])
            chunks += [lefts[before], rights[before]]
        after = [gathers[-1][0] if gathers else out_weight_t]
        attended = pl.pallas_call(
            functools.partial(attend, own, halos, images, base_tile, rate, 2 * near),
            grid=(1,),
            in_specs=[smem_spec, vmem_spec] + [any_spec] * (3 + len(chunks) + len(after)),
            out_specs=vmem_spec,
            out_shape=jax.ShapeDtypeStruct((width, 2 * size * TILE), BF),
            scratch_shapes=[
                pltpu.VMEM((2 * size, heads, depth, TILE), BF),
                pltpu.VMEM((tiles,) + kt_shape, BF),
                pltpu.VMEM((tiles,) + v_shape, BF),
                pltpu.VMEM((2 * far_tiles + 1, heads, TILE, TILE), F32),
                pltpu.VMEM((heads, HEAD_DIM + 8, TILE), F32),
                pltpu.VMEM((heads, 8, TILE), F32),
            ]
            + [pltpu.VMEM(chunk.shape, BF) for chunk in chunks]
            + [pltpu.SemaphoreType.DMA((len(chunks),)), pltpu.SemaphoreType.DMA((3,))],
            compiler_params=params(62),
            cost_estimate=cost((5 + 4 * size) * 1e9, 1e5),
            name="attend",
        )(key_bounds, labels, q_tiles, kt_own, v_own, *chunks, *after)

        gathers.append([attended])
        spread_pieces(stage, bits[:1], None)
        if stage >= 1:
            spread_pieces(stage - 1, bits[1:], attended)
    run_project(0)
    spread_pieces(2, bits[1:], layers[0])
    run_project(1)
    run_project(2)

    tiles_out = [None] * own_tiles
    for stage in range(stages):
        for block in range(plan[stage]):
            for which in range(2):
                lane = (2 * block + which) * TILE
                tile = pair_tile(begins[stage] + block, which)
                tiles_out[tile] = layers[stage][:, lane : lane + TILE]
    layer_out = jnp.concatenate(tiles_out, axis=1)

    groups = tokens // 4
    share = groups // rows
    piece_groups = TILE // 4
    owner = dest_row // groups
    place = dest_row % groups
    index = jnp.arange(groups, dtype=jnp.int32)
    rank = jnp.sum(
        ((owner[:, None] == owner[None, :]) & (index[None, :] < index[:, None])).astype(jnp.int32),
        axis=1,
    )
    base = 32
    away = (owner - row_id) % rows
    info = jnp.stack([away * share + rank, place // base, place % base])
    info = info.reshape(3, own_tiles, piece_groups)
    merges = [list(range(inner)), list(range(inner, half))]
    info = jnp.stack(
        [
            jnp.concatenate(
                [
                    info[:, pair_tile(block, which)]
                    for block in merge
                    for which in range(2)
                ],
                axis=1,
            )
            for merge in merges
        ],
        axis=1,
    )
    slots = info[0][:, None, :]
    wide = round_up(width + 2, 128)
    places = jnp.concatenate(
        [
            jnp.stack([info[1], info[2]], axis=1).astype(BF),
            jnp.zeros((len(merges), wide - width - 2, 4 * piece_groups), BF),
        ],
        axis=1,
    )
    sent = pl.pallas_call(
        functools.partial(outgoing, rows),
        out_shape=[jax.ShapeDtypeStruct((share, wide), BF)] * rows,
        compiler_params=params(16),
        cost_estimate=cost(1e9, 1e5),
        name="outgoing",
    )(slots, places, parts[0], parts[2])
    received = [sent[0]] + [
        lax.ppermute(sent[step], "row", [(i, (i + step) % rows) for i in range(rows)])
        for step in range(1, rows)
    ]
    image_rows = pl.pallas_call(
        functools.partial(incoming, width, base),
        out_shape=jax.ShapeDtypeStruct((width, groups), BF),
        compiler_params=params(16),
        cost_estimate=cost(1e9, 1e5),
        name="incoming",
    )(*received)
    return (layer_out, image_rows)


def solution(mesh):
    return jax.shard_map(
        body,
        mesh=mesh,
        in_specs=(P(None, "col", "row"), P("col", "row"), P(), P("col", None), P(), P(), P("row")),
        out_specs=(P("col", "row"), P("col", "row")),
        check_vma=False,
    )
```

```python
import functools
import math

import jax
import jax.numpy as jnp
from jax import lax
from jax.experimental import pallas as pl
from jax.experimental.pallas import tpu as pltpu
from jax.sharding import PartitionSpec as P

HEAD_DIM = 88
TILE = 256
FAR = -1e30
BF = jnp.bfloat16
F32 = jnp.float32


def params(mib):
    return pltpu.CompilerParams(vmem_limit_bytes=mib * 1024 * 1024)


def cost(flops, bytes_accessed):
    return pl.CostEstimate(flops=int(flops), bytes_accessed=int(bytes_accessed), transcendentals=0)


def round_up(value, unit):
    return -(-value // unit) * unit


def key_tile(keys, label, images, depth, kt_ref):
    heads = keys.shape[0] // HEAD_DIM
    tail = depth - HEAD_DIM
    at = lax.broadcasted_iota(jnp.int32, (tail, TILE), 0)
    mask = jnp.where((at == label) | (at >= images), 0.0, FAR)
    for head in range(heads):
        whole = jnp.concatenate([keys[head * HEAD_DIM : (head + 1) * HEAD_DIM], mask], axis=0)
        kt_ref[0, head] = jnp.transpose(whole).astype(BF)


def value_tile(values, v_ref):
    heads = values.shape[0] // HEAD_DIM
    ones = jnp.where(lax.broadcasted_iota(jnp.int32, (8, TILE), 0) == 0, 1.0, 0.0)
    for head in range(heads):
        v_ref[0, head] = jnp.concatenate(
            [values[head * HEAD_DIM : (head + 1) * HEAD_DIM], ones], axis=0
        ).astype(BF)


def prepare_own(images, depth, label_ref, qkv_ref, q_ref, kt_ref, v_ref):
    label = label_ref[0]
    queries = qkv_ref[0].astype(F32)
    heads = queries.shape[0] // HEAD_DIM
    at = lax.broadcasted_iota(jnp.int32, (depth - HEAD_DIM, TILE), 0)
    mark = jnp.where(at == label, 1.0, 0.0)
    for head in range(heads):
        q_ref[0, head] = jnp.concatenate(
            [queries[head * HEAD_DIM : (head + 1) * HEAD_DIM], mark], axis=0
        ).astype(BF)
    key_tile(qkv_ref[1].astype(F32), label, images, depth, kt_ref)
    value_tile(qkv_ref[2].astype(F32), v_ref)


def reorder_residual(perm_ref, low_ref, high_ref, out_ref):
    both = jnp.concatenate([low_ref[...], high_ref[...]], axis=1)
    out_ref[0] = jnp.dot(both, perm_ref[...], preferred_element_type=F32).astype(BF)


def attend(own, halos, images, base, rate, first_query, bounds, label_ref, *refs):
    count = len(halos)
    perm_hbm, q_hbm, kt_ref, v_ref, chunk_refs = *refs[:4], refs[4 : 4 + count]
    refs = refs[-(11 + count) :]
    out_ref, perm_ref, q_ref, kt_s, v_s, scores_s, acc, top, att = refs[:9]
    raw_s, sems, own_sems = refs[9 : 9 + count], refs[-2], refs[-1]
    queries, heads = q_ref.shape[0], q_ref.shape[1]
    depth = kt_s.shape[3]
    slots = pl.ds(own[0] - base, len(own))
    chunk_copies = [
        pltpu.make_async_copy(chunk_ref, raw, sems.at[at])
        for at, (chunk_ref, raw) in enumerate(zip(chunk_refs, raw_s))
    ]
    kt_copy = pltpu.make_async_copy(kt_ref, kt_s.at[slots], own_sems.at[0])
    v_copy = pltpu.make_async_copy(v_ref, v_s.at[slots], own_sems.at[1])
    q_copy = pltpu.make_async_copy(q_hbm.at[pl.ds(first_query, queries)], q_ref, own_sems.at[2])
    perm_copy = pltpu.make_async_copy(perm_hbm, perm_ref, own_sems.at[3])
    for copy in chunk_copies + [q_copy, kt_copy, v_copy, perm_copy]:
        copy.start()
    for tiles, copy, raw in zip(halos, chunk_copies, raw_s):
        copy.wait()
        for at, tile in enumerate(tiles):
            lanes = slice(at * TILE, (at + 1) * TILE)
            slot = pl.ds(tile - base, 1)
            key_tile(raw[0, :, lanes].astype(F32), label_ref[tile], images, depth, kt_s.at[slot])
            value_tile(raw[1, :, lanes].astype(F32), v_s.at[slot])
    q_copy.wait()
    kt_copy.wait()

    def attend_tile(side, carry):
        begin, end = bounds[0, first_query + side], bounds[1, first_query + side]
        acc[...] = jnp.zeros_like(acc)
        top[...] = jnp.full_like(top, FAR)

        def sweep(step):
            pairs = (end - begin) // 2

            def pair(index, carry):
                step(begin + 2 * index, 2)
                return carry

            def single(index, carry):
                step(end - 1, 1)
                return carry

            lax.fori_loop(0, pairs, pair, 0)
            lax.fori_loop(0, end - begin - 2 * pairs, single, 0)

        def score(tile, span):
            for head in range(heads):
                keys = kt_s[pl.ds(tile - base, span), head].reshape(span * TILE, -1)
                scores = jnp.dot(keys, q_ref[side, head], preferred_element_type=F32)
                scores_s[pl.ds(tile - begin, span), head] = scores.reshape(span, TILE, TILE)
                highest = jnp.max(scores.reshape(span * TILE // 8, 8, TILE), axis=0)
                top[head] = jnp.maximum(top[head], highest)

        sweep(score)

        @pl.when(side == 0)
        def _():
            v_copy.wait()

        tops = [jnp.max(top[head], axis=0, keepdims=True) for head in range(heads)]
        for head in range(heads):
            top[head, 0:1] = tops[head]

        def weigh(tile, span):
            for head in range(heads):
                scores = scores_s[pl.ds(tile - begin, span), head].reshape(span * TILE, TILE)
                weights = jnp.exp2((scores - top[head, 0:1]) * rate).astype(BF)
                values = [v_s[tile - base + at, head] for at in range(span)]
                values = values[0] if span == 1 else jnp.concatenate(values, axis=1)
                acc[head] += jnp.dot(values, weights, preferred_element_type=F32)

        sweep(weigh)
        whole = jnp.concatenate(
            [acc[head, :HEAD_DIM] / acc[head, HEAD_DIM : HEAD_DIM + 1] for head in range(heads)], axis=0
        )
        att[:, pl.ds(pl.multiple_of(side * TILE, TILE), TILE)] = whole.astype(BF)
        return carry

    lax.fori_loop(0, queries, attend_tile, 0)
    perm_copy.wait()
    for at in range(queries // 2):
        lanes = slice(2 * at * TILE, 2 * (at + 1) * TILE)
        out_ref[:, lanes] = jnp.dot(
            att[:, lanes], perm_ref[...], preferred_element_type=F32
        ).astype(BF)


def project(order, first, parts, col_ref, gain_ref, perm_hbm, res_ref, wt_ref, mw_ref, *refs):
    count = len(order)
    att_refs = refs[: count * parts]
    layer_ref, out_ref, gathered, layer_s, res_s, wt_s, mw_s, merged_s, perm_ref = refs[-13:-4]
    att_sem, wt_sem, res_sem, sems = refs[-4:]
    width = att_refs[0].shape[0]
    full = wt_ref.shape[0]
    block = 2 * TILE
    blocks = layer_s.shape[1] // block
    groups = block // 4
    col = col_ref[0]

    def part_copies(part):
        rows = pl.ds(pl.multiple_of(part * width, 16), width)
        return (
            pltpu.make_async_copy(wt_ref.at[rows, :], wt_s.at[rows, :], wt_sem.at[part]),
            pltpu.make_async_copy(
                res_ref.at[part, pl.ds(first, blocks)], res_s.at[part], res_sem.at[part]
            ),
        )

    att_copies = []
    for at, att_ref in enumerate(att_refs):
        row = pl.multiple_of((col ^ order[at % count]) * width, 16)
        span = att_ref.shape[1]
        lanes = pl.ds(at // count * span, span)
        att_copies.append(
            pltpu.make_async_copy(att_ref, gathered.at[pl.ds(row, width), lanes], att_sem.at[at])
        )
    late = [
        pltpu.make_async_copy(perm_hbm, perm_ref, sems.at[0]),
        pltpu.make_async_copy(mw_ref, mw_s, sems.at[1]),
    ]
    for copy in att_copies:
        copy.start()
    for part in range(count):
        for copy in part_copies(part):
            copy.start()
    for copy in late:
        copy.start()
    for copy in att_copies:
        copy.wait()

    def project_part(part, carry):
        rows = pl.ds(pl.multiple_of(part * width, 16), width)
        for copy in part_copies(part):
            copy.wait()
        for at in range(blocks):
            lanes = slice(at * block, (at + 1) * block)
            projected = jnp.dot(wt_s[rows, :], gathered[:, lanes], preferred_element_type=F32)
            layer_s[rows, lanes] = (res_s[part, at].astype(F32) + projected).astype(BF)
        return carry

    lax.fori_loop(0, count, project_part, 0)
    for copy in late:
        copy.wait()
    own = pl.ds(pl.multiple_of(col * width, 16), width)
    for at in range(blocks):
        lanes = slice(at * block, (at + 1) * block)
        layer_ref[:, lanes] = lax.dot_general(
            layer_s[own, lanes], perm_ref[...], (((1,), (1,)), ((), ())), preferred_element_type=F32
        ).astype(BF)
    merged_s[...] = jnp.zeros_like(merged_s)

    def merge_part(j, carry):
        columns = []
        for at in range(blocks):
            lanes = pl.ds(pl.multiple_of(at * block + j * groups, groups), groups)
            values = layer_s[:, lanes].astype(F32)
            values = values - jnp.sum(values, axis=0, keepdims=True) / full
            spread = jnp.sum(jnp.square(values), axis=0, keepdims=True) / full
            normed = (values * lax.rsqrt(spread + 1e-06) * gain_ref[...]).astype(BF)
            columns.append(normed)
        weights = mw_s[:, pl.ds(pl.multiple_of(j * full, 128), full)]
        merged_s[...] += jnp.dot(
            weights, jnp.concatenate(columns, axis=1), preferred_element_type=F32
        )
        return carry

    lax.fori_loop(0, 4, merge_part, 0)
    out_ref[...] = merged_s[...].astype(BF)


def outgoing(pieces, slot_ref, place_ref, *refs):
    merged_refs, out_refs = refs[:-pieces], refs[-pieces:]
    total = None
    share, wide = out_refs[0].shape
    for part, merged_ref in enumerate(merged_refs):
        groups = merged_ref.shape[1]
        row = lax.broadcasted_iota(jnp.int32, (share * pieces, groups), 0)
        pick = jnp.where(row == slot_ref[part], 1.0, 0.0).astype(BF)
        rows = jnp.concatenate([merged_ref[...], place_ref[part]], axis=0)
        term = lax.dot_general(pick, rows, (((1,), (1,)), ((), ())), preferred_element_type=F32)
        total = term if total is None else total + term
    for piece, out_ref in enumerate(out_refs):
        out_ref[...] = total[piece * share : (piece + 1) * share].astype(BF)


def incoming(width, base, *refs):
    in_refs, out_ref = refs[:-1], refs[-1]
    rows = jnp.concatenate([in_ref[...] for in_ref in in_refs], axis=0)
    place = rows[:, width : width + 2].astype(F32)
    target = (place[:, 0:1] * base + place[:, 1:2]).astype(jnp.int32)
    slots = rows.shape[0]
    lane = lax.broadcasted_iota(jnp.int32, (slots, slots), 1)
    pick = jnp.where(lane == target, 1.0, 0.0).astype(BF)
    out_ref[...] = lax.dot_general(
        rows[:, :width], pick, (((0,), (0,)), ((), ())), preferred_element_type=F32
    ).astype(BF)


def body(qkv, residual_in, out_weight, merge_weight, merge_gain, image_groups, dest_row):
    width = qkv.shape[1]
    tokens = qkv.shape[2]
    heads = width // HEAD_DIM
    full = out_weight.shape[0]
    images = image_groups.shape[0]
    reach = tokens // 2
    own_tiles = tokens // TILE
    far_tiles = reach // TILE
    half = own_tiles // 2
    plan = [half // 2] + [1] * (half - half // 2)
    begins = [sum(plan[:s]) for s in range(len(plan))]
    stages = len(plan)
    depth = round_up(HEAD_DIM + images, 128)
    rate = math.log2(math.e) / math.sqrt(HEAD_DIM)
    rows, cols = lax.axis_size("row"), lax.axis_size("col")
    row_id, col_id = lax.axis_index("row"), lax.axis_index("col")
    forward = [(i, (i + 1) % rows) for i in range(rows)]
    backward = [((i + 1) % rows, i) for i in range(rows)]

    lefts, rights = [], []

    def send_chunk(stage, after):
        source = qkv
        if after is not None:
            source, _ = lax.optimization_barrier((qkv, after))
        near, far = begins[stage] * TILE, (begins[stage] + plan[stage]) * TILE
        tail = lax.slice(source, (1, 0, tokens - far), (3, width, tokens - near))
        head = lax.slice(source, (1, 0, near), (3, width, far))
        lefts.append(lax.ppermute(tail, "row", forward))
        rights.append(lax.ppermute(head, "row", backward))
        return tail, head

    first_chunk = send_chunk(0, None)

    image_ends = jnp.cumsum(image_groups) * 4
    window_tiles = own_tiles + 2 * far_tiles
    positions = row_id * tokens - reach + jnp.arange(window_tiles * TILE, dtype=jnp.int32)
    labels = jnp.sum((positions[:, None] >= image_ends[None, :]).astype(jnp.int32), axis=1)
    labels = jnp.where(positions >= 0, labels, -1).reshape(window_tiles, 1, TILE)
    starts = row_id * tokens + jnp.arange(own_tiles, dtype=jnp.int32) * TILE
    ends = starts + TILE - 1
    low = jnp.max(jnp.where(image_ends[None, :] <= starts[:, None], image_ends[None, :], 0), axis=1)
    high = jnp.min(
        jnp.where(image_ends[None, :] > ends[:, None], image_ends[None, :], rows * tokens), axis=1
    )
    window_start = row_id * tokens - reach
    low = (low - window_start) // TILE
    high = (high - window_start + TILE - 1) // TILE
    tile_at = jnp.arange(own_tiles, dtype=jnp.int32)
    low = jnp.maximum(low, tile_at)
    high = jnp.minimum(high, tile_at + 2 * far_tiles + 1)

    inner = plan[0]

    def pair_tile(block, which):
        near = half - inner + 2 * block + which
        mirrored = half + block if which else half - 1 - block
        if isinstance(block, int):
            return near if block < inner else mirrored
        return jnp.where(block < inner, near, mirrored)

    def stage_order(tile):
        mirrored = jnp.where(tile >= half, 2 * (tile - half) + 1, 2 * (half - 1 - tile))
        near = tile - (half - inner)
        return jnp.where((near >= 0) & (near < 2 * inner), near, mirrored)

    at = jnp.arange(2 * TILE, dtype=jnp.int32)
    perm = (((at % 4) * (TILE // 2) + at // 4)[:, None] == at[None, :]).astype(BF)

    qkv_after, _ = lax.optimization_barrier((qkv, first_chunk))
    kt_shape, v_shape = (heads, TILE, depth), (heads, HEAD_DIM + 8, TILE)
    q_tiles, kt_own, v_own = pl.pallas_call(
        functools.partial(prepare_own, images, depth),
        grid=(own_tiles,),
        in_specs=[
            pl.BlockSpec((1, 1, TILE), lambda i: (i + far_tiles, 0, 0)),
            pl.BlockSpec((3, width, TILE), lambda i: (0, 0, i)),
        ],
        out_specs=[
            pl.BlockSpec((1, heads, depth, TILE), lambda i: (stage_order(i), 0, 0, 0)),
            pl.BlockSpec((1,) + kt_shape, lambda i: (i, 0, 0, 0)),
            pl.BlockSpec((1,) + v_shape, lambda i: (i, 0, 0, 0)),
        ],
        out_shape=[
            jax.ShapeDtypeStruct((own_tiles, heads, depth, TILE), BF),
            jax.ShapeDtypeStruct((own_tiles,) + kt_shape, BF),
            jax.ShapeDtypeStruct((own_tiles,) + v_shape, BF),
        ],
        compiler_params=params(16),
        cost_estimate=cost(2e9, 1e5),
        name="prepare_own",
    )(labels, qkv_after)

    residual_in, _ = lax.optimization_barrier((residual_in, first_chunk))
    blocks = own_tiles // 2
    residual = pl.pallas_call(
        reorder_residual,
        grid=(blocks,),
        in_specs=[
            pl.BlockSpec((2 * TILE, 2 * TILE), lambda i: (0, 0)),
            pl.BlockSpec((width, TILE), lambda i: (0, pair_tile(i, 0))),
            pl.BlockSpec((width, TILE), lambda i: (0, pair_tile(i, 1))),
        ],
        out_specs=pl.BlockSpec((1, width, 2 * TILE), lambda i: (i, 0, 0)),
        out_shape=jax.ShapeDtypeStruct((blocks, width, 2 * TILE), BF),
        compiler_params=params(16),
        cost_estimate=cost(2e9, 1e5),
        name="reorder_residual",
    )(perm, residual_in, residual_in)
    residual = lax.all_gather(residual, "col", axis=0)
    tile_order = [pair_tile(block, which) for block in range(blocks) for which in range(2)]
    out_weight_t = jnp.transpose(out_weight)
    key_bounds = jnp.stack([low, high])
    key_bounds = jnp.stack([key_bounds[:, tile] for tile in tile_order], axis=1)
    gain = merge_gain[:, None]
    bits = []
    span = cols // 2
    while span:
        bits.append(span)
        span //= 2
    order = [0]
    for bit in bits:
        order = order + [bit ^ other for other in order]
    col_value = col_id.astype(jnp.int32).reshape(1)

    layers, parts, gathers = [], [], []
    any_spec = pl.BlockSpec(memory_space=pl.ANY)
    smem_spec = pl.BlockSpec(memory_space=pltpu.SMEM)
    vmem_spec = pl.BlockSpec(memory_space=pltpu.VMEM)
    def spread_pieces(stage, some_bits, after):
        pieces = gathers[stage]
        for bit in some_bits:
            pairs = [(i, i ^ bit) for i in range(cols)]
            sources = pieces
            if after is not None:
                sources, _ = lax.optimization_barrier((pieces, after))
            pieces = pieces + [lax.ppermute(piece, "col", pairs) for piece in sources]
        gathers[stage] = pieces

    def run_project(first, members):
        size = sum(plan[stage] for stage in members)
        pieces = [piece for stage in members for piece in gathers[stage]]
        columns, merged_columns = 2 * size * TILE, size * TILE // 2
        after = [gathers[-1][0]] + layers[-1:]
        layer, part = pl.pallas_call(
            functools.partial(project, order, first, len(members)),
            grid=(1,),
            in_specs=[smem_spec, vmem_spec] + [any_spec] * (4 + len(pieces) + len(after)),
            out_specs=[vmem_spec, vmem_spec],
            out_shape=[
                jax.ShapeDtypeStruct((width, columns), BF),
                jax.ShapeDtypeStruct((width, merged_columns), BF),
            ],
            scratch_shapes=[
                pltpu.VMEM((full, columns), BF),
                pltpu.VMEM((full, columns), BF),
                pltpu.VMEM((cols, size, width, 2 * TILE), BF),
                pltpu.VMEM((full, full), BF),
                pltpu.VMEM((width, 4 * full), BF),
                pltpu.VMEM((width, merged_columns), F32),
                pltpu.VMEM(perm.shape, BF),
                pltpu.SemaphoreType.DMA((len(pieces),)),
                pltpu.SemaphoreType.DMA((cols,)),
                pltpu.SemaphoreType.DMA((cols,)),
                pltpu.SemaphoreType.DMA((2,)),
            ],
            compiler_params=params(62),
            cost_estimate=cost((4 + 4 * size) * 1e9, 1e5),
            name="project",
        )(col_value, gain, perm, residual, out_weight_t, merge_weight, *pieces, *after)
        layers.append(layer)
        parts.append(part)

    for stage in range(stages):
        size, near = plan[stage], begins[stage]
        if stage + 1 < stages:
            send_chunk(stage + 1, (lefts[stage], rights[stage]))
        own = list(range(far_tiles, far_tiles + own_tiles))
        base_tile = far_tiles - near - size
        tiles = own_tiles + 2 * (near + size)
        halos, chunks = [], []
        for before in range(stage + 1):
            inner_edge, outer_edge = begins[before], begins[before] + plan[before]
            halos.append(list(range(far_tiles - outer_edge, far_tiles - inner_edge)))
            halos.append([far_tiles + own_tiles + at for at in range(inner_edge, outer_edge)])
            chunks += [lefts[before], rights[before]]
        after = [gathers[-1][0] if gathers else out_weight_t]
        attended = pl.pallas_call(
            functools.partial(attend, own, halos, images, base_tile, rate, 2 * near),
            grid=(1,),
            in_specs=[smem_spec, vmem_spec] + [any_spec] * (4 + len(chunks) + len(after)),
            out_specs=vmem_spec,
            out_shape=jax.ShapeDtypeStruct((width, 2 * size * TILE), BF),
            scratch_shapes=[
                pltpu.VMEM(perm.shape, BF),
                pltpu.VMEM((2 * size, heads, depth, TILE), BF),
                pltpu.VMEM((tiles,) + kt_shape, BF),
                pltpu.VMEM((tiles,) + v_shape, BF),
                pltpu.VMEM((2 * far_tiles + 1, heads, TILE, TILE), F32),
                pltpu.VMEM((heads, HEAD_DIM + 8, TILE), F32),
                pltpu.VMEM((heads, 8, TILE), F32),
                pltpu.VMEM((width, 2 * size * TILE), BF),
            ]
            + [pltpu.VMEM(chunk.shape, BF) for chunk in chunks]
            + [pltpu.SemaphoreType.DMA((len(chunks),)), pltpu.SemaphoreType.DMA((4,))],
            compiler_params=params(62),
            cost_estimate=cost((5 + 4 * size) * 1e9, 1e5),
            name="attend",
        )(key_bounds, labels, perm, q_tiles, kt_own, v_own, *chunks, *after)

        gathers.append([attended])
        spread_pieces(stage, bits[:1], None)
        if stage >= 1:
            spread_pieces(stage - 1, bits[1:], attended)
    run_project(0, [0])
    spread_pieces(stages - 1, bits[1:], layers[0])
    run_project(inner, list(range(1, stages)))

    tiles_out = [None] * own_tiles
    for layer, first in zip(layers, (0, inner)):
        for block in range(layer.shape[1] // (2 * TILE)):
            for which in range(2):
                lane = (2 * block + which) * TILE
                tiles_out[pair_tile(first + block, which)] = layer[:, lane : lane + TILE]
    layer_out = jnp.concatenate(tiles_out, axis=1)

    groups = tokens // 4
    share = groups // rows
    piece_groups = TILE // 4
    owner = dest_row // groups
    place = dest_row % groups
    index = jnp.arange(groups, dtype=jnp.int32)
    rank = jnp.sum(
        ((owner[:, None] == owner[None, :]) & (index[None, :] < index[:, None])).astype(jnp.int32),
        axis=1,
    )
    base = 32
    away = (owner - row_id) % rows
    info = jnp.stack([away * share + rank, place // base, place % base])
    info = info.reshape(3, own_tiles, piece_groups)
    merges = [list(range(inner)), list(range(inner, half))]
    info = jnp.stack(
        [
            jnp.concatenate(
                [
                    info[:, pair_tile(block, which)]
                    for block in merge
                    for which in range(2)
                ],
                axis=1,
            )
            for merge in merges
        ],
        axis=1,
    )
    slots = info[0][:, None, :]
    wide = round_up(width + 2, 128)
    places = jnp.concatenate(
        [
            jnp.stack([info[1], info[2]], axis=1).astype(BF),
            jnp.zeros((len(merges), wide - width - 2, 4 * piece_groups), BF),
        ],
        axis=1,
    )
    sent = pl.pallas_call(
        functools.partial(outgoing, rows),
        out_shape=[jax.ShapeDtypeStruct((share, wide), BF)] * rows,
        compiler_params=params(16),
        cost_estimate=cost(1e9, 1e5),
        name="outgoing",
    )(slots, places, *parts)
    received = [sent[0]] + [
        lax.ppermute(sent[step], "row", [(i, (i + step) % rows) for i in range(rows)])
        for step in range(1, rows)
    ]
    image_rows = pl.pallas_call(
        functools.partial(incoming, width, base),
        out_shape=jax.ShapeDtypeStruct((width, groups), BF),
        compiler_params=params(16),
        cost_estimate=cost(1e9, 1e5),
        name="incoming",
    )(*received)
    return (layer_out, image_rows)


def solution(mesh):
    return jax.shard_map(
        body,
        mesh=mesh,
        in_specs=(P(None, "col", "row"), P("col", "row"), P(), P("col", None), P(), P(), P("row")),
        out_specs=(P("col", "row"), P("col", "row")),
        check_vma=False,
    )
```

```python
import functools
import math

import jax
import jax.numpy as jnp
from jax import lax
from jax.experimental import pallas as pl
from jax.experimental.pallas import tpu as pltpu
from jax.sharding import PartitionSpec as P

HEAD_DIM = 88
TILE = 256
FAR = -1e30
BF = jnp.bfloat16
F32 = jnp.float32


def params(mib):
    return pltpu.CompilerParams(vmem_limit_bytes=mib * 1024 * 1024)


def cost(flops, bytes_accessed):
    return pl.CostEstimate(flops=int(flops), bytes_accessed=int(bytes_accessed), transcendentals=0)


def round_up(value, unit):
    return -(-value // unit) * unit


def key_tile(keys, label, images, depth, kt_ref):
    heads = keys.shape[0] // HEAD_DIM
    tail = depth - HEAD_DIM
    at = lax.broadcasted_iota(jnp.int32, (tail, TILE), 0)
    mask = jnp.where((at == label) | (at >= images), 0.0, FAR)
    for head in range(heads):
        whole = jnp.concatenate([keys[head * HEAD_DIM : (head + 1) * HEAD_DIM], mask], axis=0)
        kt_ref[0, head] = jnp.transpose(whole).astype(BF)


def value_tile(values, v_ref):
    heads = values.shape[0] // HEAD_DIM
    ones = jnp.where(lax.broadcasted_iota(jnp.int32, (8, TILE), 0) == 0, 1.0, 0.0)
    for head in range(heads):
        v_ref[0, head] = jnp.concatenate(
            [values[head * HEAD_DIM : (head + 1) * HEAD_DIM], ones], axis=0
        ).astype(BF)


def prepare_own(images, depth, label_ref, qkv_ref, q_ref, kt_ref, v_ref):
    label = label_ref[0]
    queries = qkv_ref[0].astype(F32)
    heads = queries.shape[0] // HEAD_DIM
    at = lax.broadcasted_iota(jnp.int32, (depth - HEAD_DIM, TILE), 0)
    mark = jnp.where(at == label, 1.0, 0.0)
    for head in range(heads):
        q_ref[0, head] = jnp.concatenate(
            [queries[head * HEAD_DIM : (head + 1) * HEAD_DIM], mark], axis=0
        ).astype(BF)
    key_tile(qkv_ref[1].astype(F32), label, images, depth, kt_ref)
    value_tile(qkv_ref[2].astype(F32), v_ref)


def reorder_residual(perm_ref, low_ref, high_ref, out_ref):
    both = jnp.concatenate([low_ref[...], high_ref[...]], axis=1)
    out_ref[0] = jnp.dot(both, perm_ref[...], preferred_element_type=F32).astype(BF)


def attend(own, halos, images, base, rate, first_query, bounds, label_ref, *refs):
    count = len(halos)
    perm_hbm, q_hbm, kt_ref, v_ref, chunk_refs = *refs[:4], refs[4 : 4 + count]
    refs = refs[-(11 + count) :]
    out_ref, perm_ref, q_ref, kt_s, v_s, scores_s, acc, top, att = refs[:9]
    raw_s, sems, own_sems = refs[9 : 9 + count], refs[-2], refs[-1]
    queries, heads = q_ref.shape[0], q_ref.shape[1]
    depth = kt_s.shape[3]
    slots = pl.ds(own[0] - base, len(own))
    chunk_copies = [
        pltpu.make_async_copy(chunk_ref, raw, sems.at[at])
        for at, (chunk_ref, raw) in enumerate(zip(chunk_refs, raw_s))
    ]
    kt_copy = pltpu.make_async_copy(kt_ref, kt_s.at[slots], own_sems.at[0])
    v_copy = pltpu.make_async_copy(v_ref, v_s.at[slots], own_sems.at[1])
    q_copy = pltpu.make_async_copy(q_hbm.at[pl.ds(first_query, queries)], q_ref, own_sems.at[2])
    perm_copy = pltpu.make_async_copy(perm_hbm, perm_ref, own_sems.at[3])
    for copy in chunk_copies + [q_copy, kt_copy, v_copy, perm_copy]:
        copy.start()
    for tiles, copy, raw in zip(halos, chunk_copies, raw_s):
        copy.wait()
        for at, tile in enumerate(tiles):
            lanes = slice(at * TILE, (at + 1) * TILE)
            slot = pl.ds(tile - base, 1)
            key_tile(raw[0, :, lanes].astype(F32), label_ref[tile], images, depth, kt_s.at[slot])
            value_tile(raw[1, :, lanes].astype(F32), v_s.at[slot])
    q_copy.wait()
    kt_copy.wait()

    def attend_tile(side, carry):
        begin, end = bounds[0, first_query + side], bounds[1, first_query + side]
        acc[...] = jnp.zeros_like(acc)
        top[...] = jnp.full_like(top, FAR)

        def sweep(step):
            pairs = (end - begin) // 2

            def pair(index, carry):
                step(begin + 2 * index, 2)
                return carry

            def single(index, carry):
                step(end - 1, 1)
                return carry

            lax.fori_loop(0, pairs, pair, 0)
            lax.fori_loop(0, end - begin - 2 * pairs, single, 0)

        def score(tile, span):
            for head in range(heads):
                keys = kt_s[pl.ds(tile - base, span), head].reshape(span * TILE, -1)
                scores = jnp.dot(keys, q_ref[side, head], preferred_element_type=F32)
                scores_s[pl.ds(tile - begin, span), head] = scores.reshape(span, TILE, TILE)
                highest = jnp.max(scores.reshape(span * TILE // 8, 8, TILE), axis=0)
                top[head] = jnp.maximum(top[head], highest)

        sweep(score)

        @pl.when(side == 0)
        def _():
            v_copy.wait()

        tops = [jnp.max(top[head], axis=0, keepdims=True) for head in range(heads)]
        for head in range(heads):
            top[head, 0:1] = tops[head]

        def weigh(tile, span):
            for head in range(heads):
                scores = scores_s[pl.ds(tile - begin, span), head].reshape(span * TILE, TILE)
                weights = jnp.exp2((scores - top[head, 0:1]) * rate).astype(BF)
                values = [v_s[tile - base + at, head] for at in range(span)]
                values = values[0] if span == 1 else jnp.concatenate(values, axis=1)
                acc[head] += jnp.dot(values, weights, preferred_element_type=F32)

        sweep(weigh)
        whole = jnp.concatenate(
            [acc[head, :HEAD_DIM] / acc[head, HEAD_DIM : HEAD_DIM + 1] for head in range(heads)], axis=0
        )
        att[:, pl.ds(pl.multiple_of(side * TILE, TILE), TILE)] = whole.astype(BF)
        return carry

    lax.fori_loop(0, queries, attend_tile, 0)
    perm_copy.wait()
    for at in range(queries // 2):
        lanes = slice(2 * at * TILE, 2 * (at + 1) * TILE)
        out_ref[:, lanes] = jnp.dot(
            att[:, lanes], perm_ref[...], preferred_element_type=F32
        ).astype(BF)


def project(order, first, parts, col_ref, gain_ref, perm_hbm, res_ref, wt_ref, mw_ref, *refs):
    count = len(order)
    att_refs = refs[: count * parts]
    layer_ref, out_ref, gathered, layer_s, res_s, wt_s, mw_s, merged_s, perm_ref = refs[-13:-4]
    att_sem, wt_sem, res_sem, sems = refs[-4:]
    width = att_refs[0].shape[0]
    full = wt_ref.shape[0]
    block = 2 * TILE
    blocks = layer_s.shape[1] // block
    groups = block // 4
    col = col_ref[0]

    def part_copies(part):
        rows = pl.ds(pl.multiple_of(part * width, 16), width)
        return (
            pltpu.make_async_copy(wt_ref.at[rows, :], wt_s.at[rows, :], wt_sem.at[part]),
            pltpu.make_async_copy(
                res_ref.at[part, pl.ds(first, blocks)], res_s.at[part], res_sem.at[part]
            ),
        )

    att_copies = []
    for at, att_ref in enumerate(att_refs):
        row = pl.multiple_of((col ^ order[at % count]) * width, 16)
        span = att_ref.shape[1]
        lanes = pl.ds(at // count * span, span)
        att_copies.append(
            pltpu.make_async_copy(att_ref, gathered.at[pl.ds(row, width), lanes], att_sem.at[at])
        )
    late = [
        pltpu.make_async_copy(perm_hbm, perm_ref, sems.at[0]),
        pltpu.make_async_copy(mw_ref, mw_s, sems.at[1]),
    ]
    for copy in att_copies:
        copy.start()
    for part in range(count):
        for copy in part_copies(part):
            copy.start()
    for copy in late:
        copy.start()
    for copy in att_copies:
        copy.wait()

    def project_part(part, carry):
        rows = pl.ds(pl.multiple_of(part * width, 16), width)
        for copy in part_copies(part):
            copy.wait()
        for at in range(blocks):
            lanes = slice(at * block, (at + 1) * block)
            projected = jnp.dot(wt_s[rows, :], gathered[:, lanes], preferred_element_type=F32)
            layer_s[rows, lanes] = (res_s[part, at].astype(F32) + projected).astype(BF)
        return carry

    lax.fori_loop(0, count, project_part, 0, unroll=True)
    for copy in late:
        copy.wait()
    own = pl.ds(pl.multiple_of(col * width, 16), width)
    for at in range(blocks):
        lanes = slice(at * block, (at + 1) * block)
        layer_ref[:, lanes] = lax.dot_general(
            layer_s[own, lanes], perm_ref[...], (((1,), (1,)), ((), ())), preferred_element_type=F32
        ).astype(BF)
    merged_s[...] = jnp.zeros_like(merged_s)

    def merge_part(j, carry):
        columns = []
        for at in range(blocks):
            lanes = pl.ds(pl.multiple_of(at * block + j * groups, groups), groups)
            values = layer_s[:, lanes].astype(F32)
            values = values - jnp.sum(values, axis=0, keepdims=True) / full
            spread = jnp.sum(jnp.square(values), axis=0, keepdims=True) / full
            normed = (values * lax.rsqrt(spread + 1e-06) * gain_ref[...]).astype(BF)
            columns.append(normed)
        weights = mw_s[:, pl.ds(pl.multiple_of(j * full, 128), full)]
        merged_s[...] += jnp.dot(
            weights, jnp.concatenate(columns, axis=1), preferred_element_type=F32
        )
        return carry

    lax.fori_loop(0, 4, merge_part, 0, unroll=True)
    out_ref[...] = merged_s[...].astype(BF)


def outgoing(pieces, slot_ref, place_ref, *refs):
    merged_refs, out_refs = refs[:-pieces], refs[-pieces:]
    total = None
    share, wide = out_refs[0].shape
    for part, merged_ref in enumerate(merged_refs):
        groups = merged_ref.shape[1]
        row = lax.broadcasted_iota(jnp.int32, (share * pieces, groups), 0)
        pick = jnp.where(row == slot_ref[part], 1.0, 0.0).astype(BF)
        rows = jnp.concatenate([merged_ref[...], place_ref[part]], axis=0)
        term = lax.dot_general(pick, rows, (((1,), (1,)), ((), ())), preferred_element_type=F32)
        total = term if total is None else total + term
    for piece, out_ref in enumerate(out_refs):
        out_ref[...] = total[piece * share : (piece + 1) * share].astype(BF)


def incoming(width, base, *refs):
    in_refs, out_ref = refs[:-1], refs[-1]
    rows = jnp.concatenate([in_ref[...] for in_ref in in_refs], axis=0)
    place = rows[:, width : width + 2].astype(F32)
    target = (place[:, 0:1] * base + place[:, 1:2]).astype(jnp.int32)
    slots = rows.shape[0]
    lane = lax.broadcasted_iota(jnp.int32, (slots, slots), 1)
    pick = jnp.where(lane == target, 1.0, 0.0).astype(BF)
    out_ref[...] = lax.dot_general(
        rows[:, :width], pick, (((0,), (0,)), ((), ())), preferred_element_type=F32
    ).astype(BF)


def body(qkv, residual_in, out_weight, merge_weight, merge_gain, image_groups, dest_row):
    width = qkv.shape[1]
    tokens = qkv.shape[2]
    heads = width // HEAD_DIM
    full = out_weight.shape[0]
    images = image_groups.shape[0]
    reach = tokens // 2
    own_tiles = tokens // TILE
    far_tiles = reach // TILE
    half = own_tiles // 2
    plan = [half // 2] + [1] * (half - half // 2)
    begins = [sum(plan[:s]) for s in range(len(plan))]
    stages = len(plan)
    depth = round_up(HEAD_DIM + images, 128)
    rate = math.log2(math.e) / math.sqrt(HEAD_DIM)
    rows, cols = lax.axis_size("row"), lax.axis_size("col")
    row_id, col_id = lax.axis_index("row"), lax.axis_index("col")
    forward = [(i, (i + 1) % rows) for i in range(rows)]
    backward = [((i + 1) % rows, i) for i in range(rows)]

    lefts, rights = [], []

    def send_chunk(stage, after):
        source = qkv
        if after is not None:
            source, _ = lax.optimization_barrier((qkv, after))
        near, far = begins[stage] * TILE, (begins[stage] + plan[stage]) * TILE
        tail = lax.slice(source, (1, 0, tokens - far), (3, width, tokens - near))
        head = lax.slice(source, (1, 0, near), (3, width, far))
        lefts.append(lax.ppermute(tail, "row", forward))
        rights.append(lax.ppermute(head, "row", backward))
        return tail, head

    first_chunk = send_chunk(0, None)

    image_ends = jnp.cumsum(image_groups) * 4
    window_tiles = own_tiles + 2 * far_tiles
    positions = row_id * tokens - reach + jnp.arange(window_tiles * TILE, dtype=jnp.int32)
    labels = jnp.sum((positions[:, None] >= image_ends[None, :]).astype(jnp.int32), axis=1)
    labels = jnp.where(positions >= 0, labels, -1).reshape(window_tiles, 1, TILE)
    starts = row_id * tokens + jnp.arange(own_tiles, dtype=jnp.int32) * TILE
    ends = starts + TILE - 1
    low = jnp.max(jnp.where(image_ends[None, :] <= starts[:, None], image_ends[None, :], 0), axis=1)
    high = jnp.min(
        jnp.where(image_ends[None, :] > ends[:, None], image_ends[None, :], rows * tokens), axis=1
    )
    window_start = row_id * tokens - reach
    low = (low - window_start) // TILE
    high = (high - window_start + TILE - 1) // TILE
    tile_at = jnp.arange(own_tiles, dtype=jnp.int32)
    low = jnp.maximum(low, tile_at)
    high = jnp.minimum(high, tile_at + 2 * far_tiles + 1)

    inner = plan[0]

    def pair_tile(block, which):
        near = half - inner + 2 * block + which
        mirrored = half + block if which else half - 1 - block
        if isinstance(block, int):
            return near if block < inner else mirrored
        return jnp.where(block < inner, near, mirrored)

    def stage_order(tile):
        mirrored = jnp.where(tile >= half, 2 * (tile - half) + 1, 2 * (half - 1 - tile))
        near = tile - (half - inner)
        return jnp.where((near >= 0) & (near < 2 * inner), near, mirrored)

    at = jnp.arange(2 * TILE, dtype=jnp.int32)
    perm = (((at % 4) * (TILE // 2) + at // 4)[:, None] == at[None, :]).astype(BF)

    qkv_after, _ = lax.optimization_barrier((qkv, first_chunk))
    kt_shape, v_shape = (heads, TILE, depth), (heads, HEAD_DIM + 8, TILE)
    q_tiles, kt_own, v_own = pl.pallas_call(
        functools.partial(prepare_own, images, depth),
        grid=(own_tiles,),
        in_specs=[
            pl.BlockSpec((1, 1, TILE), lambda i: (i + far_tiles, 0, 0)),
            pl.BlockSpec((3, width, TILE), lambda i: (0, 0, i)),
        ],
        out_specs=[
            pl.BlockSpec((1, heads, depth, TILE), lambda i: (stage_order(i), 0, 0, 0)),
            pl.BlockSpec((1,) + kt_shape, lambda i: (i, 0, 0, 0)),
            pl.BlockSpec((1,) + v_shape, lambda i: (i, 0, 0, 0)),
        ],
        out_shape=[
            jax.ShapeDtypeStruct((own_tiles, heads, depth, TILE), BF),
            jax.ShapeDtypeStruct((own_tiles,) + kt_shape, BF),
            jax.ShapeDtypeStruct((own_tiles,) + v_shape, BF),
        ],
        compiler_params=params(16),
        cost_estimate=cost(2e9, 1e5),
        name="prepare_own",
    )(labels, qkv_after)

    residual_in, _ = lax.optimization_barrier((residual_in, first_chunk))
    blocks = own_tiles // 2
    residual = pl.pallas_call(
        reorder_residual,
        grid=(blocks,),
        in_specs=[
            pl.BlockSpec((2 * TILE, 2 * TILE), lambda i: (0, 0)),
            pl.BlockSpec((width, TILE), lambda i: (0, pair_tile(i, 0))),
            pl.BlockSpec((width, TILE), lambda i: (0, pair_tile(i, 1))),
        ],
        out_specs=pl.BlockSpec((1, width, 2 * TILE), lambda i: (i, 0, 0)),
        out_shape=jax.ShapeDtypeStruct((blocks, width, 2 * TILE), BF),
        compiler_params=params(16),
        cost_estimate=cost(2e9, 1e5),
        name="reorder_residual",
    )(perm, residual_in, residual_in)
    residual = lax.all_gather(residual, "col", axis=0)
    tile_order = [pair_tile(block, which) for block in range(blocks) for which in range(2)]
    out_weight_t = jnp.transpose(out_weight)
    key_bounds = jnp.stack([low, high])
    key_bounds = jnp.stack([key_bounds[:, tile] for tile in tile_order], axis=1)
    gain = merge_gain[:, None]
    bits = []
    span = cols // 2
    while span:
        bits.append(span)
        span //= 2
    order = [0]
    for bit in bits:
        order = order + [bit ^ other for other in order]
    col_value = col_id.astype(jnp.int32).reshape(1)

    layers, parts, gathers = [], [], []
    any_spec = pl.BlockSpec(memory_space=pl.ANY)
    smem_spec = pl.BlockSpec(memory_space=pltpu.SMEM)
    vmem_spec = pl.BlockSpec(memory_space=pltpu.VMEM)
    def spread_pieces(stage, some_bits, after):
        pieces = gathers[stage]
        for bit in some_bits:
            pairs = [(i, i ^ bit) for i in range(cols)]
            sources = pieces
            if after is not None:
                sources, _ = lax.optimization_barrier((pieces, after))
            pieces = pieces + [lax.ppermute(piece, "col", pairs) for piece in sources]
        gathers[stage] = pieces

    def run_project(first, members):
        size = sum(plan[stage] for stage in members)
        pieces = [piece for stage in members for piece in gathers[stage]]
        columns, merged_columns = 2 * size * TILE, size * TILE // 2
        after = [gathers[-1][0]] + layers[-1:]
        layer, part = pl.pallas_call(
            functools.partial(project, order, first, len(members)),
            grid=(1,),
            in_specs=[smem_spec, vmem_spec] + [any_spec] * (4 + len(pieces) + len(after)),
            out_specs=[vmem_spec, vmem_spec],
            out_shape=[
                jax.ShapeDtypeStruct((width, columns), BF),
                jax.ShapeDtypeStruct((width, merged_columns), BF),
            ],
            scratch_shapes=[
                pltpu.VMEM((full, columns), BF),
                pltpu.VMEM((full, columns), BF),
                pltpu.VMEM((cols, size, width, 2 * TILE), BF),
                pltpu.VMEM((full, full), BF),
                pltpu.VMEM((width, 4 * full), BF),
                pltpu.VMEM((width, merged_columns), F32),
                pltpu.VMEM(perm.shape, BF),
                pltpu.SemaphoreType.DMA((len(pieces),)),
                pltpu.SemaphoreType.DMA((cols,)),
                pltpu.SemaphoreType.DMA((cols,)),
                pltpu.SemaphoreType.DMA((2,)),
            ],
            compiler_params=params(62),
            cost_estimate=cost((4 + 4 * size) * 1e9, 1e5),
            name="project",
        )(col_value, gain, perm, residual, out_weight_t, merge_weight, *pieces, *after)
        layers.append(layer)
        parts.append(part)

    for stage in range(stages):
        size, near = plan[stage], begins[stage]
        if stage + 1 < stages:
            send_chunk(stage + 1, (lefts[stage], rights[stage]))
        own = list(range(far_tiles, far_tiles + own_tiles))
        base_tile = far_tiles - near - size
        tiles = own_tiles + 2 * (near + size)
        halos, chunks = [], []
        for before in range(stage + 1):
            inner_edge, outer_edge = begins[before], begins[before] + plan[before]
            halos.append(list(range(far_tiles - outer_edge, far_tiles - inner_edge)))
            halos.append([far_tiles + own_tiles + at for at in range(inner_edge, outer_edge)])
            chunks += [lefts[before], rights[before]]
        after = [gathers[-1][0] if gathers else out_weight_t]
        attended = pl.pallas_call(
            functools.partial(attend, own, halos, images, base_tile, rate, 2 * near),
            grid=(1,),
            in_specs=[smem_spec, vmem_spec] + [any_spec] * (4 + len(chunks) + len(after)),
            out_specs=vmem_spec,
            out_shape=jax.ShapeDtypeStruct((width, 2 * size * TILE), BF),
            scratch_shapes=[
                pltpu.VMEM(perm.shape, BF),
                pltpu.VMEM((2 * size, heads, depth, TILE), BF),
                pltpu.VMEM((tiles,) + kt_shape, BF),
                pltpu.VMEM((tiles,) + v_shape, BF),
                pltpu.VMEM((2 * far_tiles + 1, heads, TILE, TILE), F32),
                pltpu.VMEM((heads, HEAD_DIM + 8, TILE), F32),
                pltpu.VMEM((heads, 8, TILE), F32),
                pltpu.VMEM((width, 2 * size * TILE), BF),
            ]
            + [pltpu.VMEM(chunk.shape, BF) for chunk in chunks]
            + [pltpu.SemaphoreType.DMA((len(chunks),)), pltpu.SemaphoreType.DMA((4,))],
            compiler_params=params(62),
            cost_estimate=cost((5 + 4 * size) * 1e9, 1e5),
            name="attend",
        )(key_bounds, labels, perm, q_tiles, kt_own, v_own, *chunks, *after)

        gathers.append([attended])
        spread_pieces(stage, bits[:1], None)
        if stage >= 1:
            spread_pieces(stage - 1, bits[1:], attended)
    run_project(0, [0])
    spread_pieces(stages - 1, bits[1:], layers[0])
    run_project(inner, list(range(1, stages)))

    tiles_out = [None] * own_tiles
    for layer, first in zip(layers, (0, inner)):
        for block in range(layer.shape[1] // (2 * TILE)):
            for which in range(2):
                lane = (2 * block + which) * TILE
                tiles_out[pair_tile(first + block, which)] = layer[:, lane : lane + TILE]
    layer_out = jnp.concatenate(tiles_out, axis=1)

    groups = tokens // 4
    share = groups // rows
    piece_groups = TILE // 4
    owner = dest_row // groups
    place = dest_row % groups
    index = jnp.arange(groups, dtype=jnp.int32)
    rank = jnp.sum(
        ((owner[:, None] == owner[None, :]) & (index[None, :] < index[:, None])).astype(jnp.int32),
        axis=1,
    )
    base = 32
    away = (owner - row_id) % rows
    info = jnp.stack([away * share + rank, place // base, place % base])
    info = info.reshape(3, own_tiles, piece_groups)
    merges = [list(range(inner)), list(range(inner, half))]
    info = jnp.stack(
        [
            jnp.concatenate(
                [
                    info[:, pair_tile(block, which)]
                    for block in merge
                    for which in range(2)
                ],
                axis=1,
            )
            for merge in merges
        ],
        axis=1,
    )
    slots = info[0][:, None, :]
    wide = round_up(width + 2, 128)
    places = jnp.concatenate(
        [
            jnp.stack([info[1], info[2]], axis=1).astype(BF),
            jnp.zeros((len(merges), wide - width - 2, 4 * piece_groups), BF),
        ],
        axis=1,
    )
    sent = pl.pallas_call(
        functools.partial(outgoing, rows),
        out_shape=[jax.ShapeDtypeStruct((share, wide), BF)] * rows,
        compiler_params=params(16),
        cost_estimate=cost(1e9, 1e5),
        name="outgoing",
    )(slots, places, *parts)
    received = [sent[0]] + [
        lax.ppermute(sent[step], "row", [(i, (i + step) % rows) for i in range(rows)])
        for step in range(1, rows)
    ]
    image_rows = pl.pallas_call(
        functools.partial(incoming, width, base),
        out_shape=jax.ShapeDtypeStruct((width, groups), BF),
        compiler_params=params(16),
        cost_estimate=cost(1e9, 1e5),
        name="incoming",
    )(*received)
    return (layer_out, image_rows)


def solution(mesh):
    return jax.shard_map(
        body,
        mesh=mesh,
        in_specs=(P(None, "col", "row"), P("col", "row"), P(), P("col", None), P(), P(), P("row")),
        out_specs=(P("col", "row"), P("col", "row")),
        check_vma=False,
    )
```
